32 devices in a mesh: chaos: 4 (over z), space: 8 (over y, x, core).
Axes of the slice: x: 2, y: 2, z: 4, core: 2. Of those that a mesh axis runs over, the one named last changes fastest.
Arguments:
- panels: bfloat16 [212, 24, 2304], P('chaos', 'space'), may hold values from -6 to 6
- mean_field: float32 [24, 2304], P('space'), may hold values from 0.5 to 2
- fluctuations: float32 [6, 24, 2304], P(None, 'space'), may hold values from -1.5 to 1.5
- products: float32 [1218], replicated, may hold values from -4 to 4
- triples: int32 [1218, 3], replicated, may hold values from 0 to 209, as said below
- owner_slot: int32 [210], replicated, may hold values from 0 to 211, as said below
Outputs:
- first_apply: bfloat16 [212, 24, 2304], P('chaos', 'space')
- second_apply: bfloat16 [212, 24, 2304], P('chaos', 'space')
The draws below stay inside these ranges and needn't reach their ends.
Inputs may be any that keep to these rules, and one draw needn't show every extreme that they name: `triples`: each row (i, j, k) names a nonzero of G_k; i and j are below 210, k below 7; repeated rows add; every chaos coefficient is some row's i and some row's j. `owner_slot`: distinct slots; slot s belongs to the group s // 53 along chaos.
All inputs are finite; a program needn't handle non-finite values.
Results may differ from the reference program's by a relative error of at most 0.007.
Values may be sent and summed in bfloat16 or wider, within the bound.
No kernel may reach another device: no remote copies, remote signals or barrier semaphores. Data moves between devices by JAX's collectives and lax.ppermute only.
A program may use at most 128 MiB of HBM per device.

```python
import math
import jax
import jax.numpy as jnp
from jax import lax

P_SIZE = 210
NPAR = 6
KF = 7
NNZ = 1218
NXY = 48
SLOTS = 212
NZ = 24
XY = 2304


def draw_triples(key, part):
    keys_all = jax.random.split(key, 5)
    row_index = jnp.concatenate([jax.random.permutation(keys_all[0], P_SIZE).astype(jnp.int32), jax.random.randint(keys_all[1], (NNZ - P_SIZE,), 0, P_SIZE).astype(jnp.int32)])
    column_index = jnp.concatenate([jax.random.permutation(keys_all[2], P_SIZE).astype(jnp.int32), jax.random.randint(keys_all[3], (NNZ - P_SIZE,), 0, P_SIZE).astype(jnp.int32)])
    fields = jax.random.randint(keys_all[4], (NNZ,), 0, KF).astype(jnp.int32)
    return jnp.stack([row_index, column_index, fields], axis=1).astype(jnp.int32)


def draw_owner_slot(key, part):
    keys_all = jax.random.split(key, 2)
    middle_slots = (jax.random.permutation(keys_all[0], SLOTS - 2) + 1).astype(jnp.int32)
    chosen = jnp.concatenate([jnp.array([0, SLOTS - 1], jnp.int32), middle_slots[SLOTS - P_SIZE:]])
    return jax.random.permutation(keys_all[1], chosen).astype(jnp.int32)


def block_levels(rng, dims, cuts, least, largest):
    gain, own = 1.0, jax.random.fold_in(rng, 6)
    for dim, parts in cuts:
        heights = jnp.exp(jax.random.uniform(jax.random.fold_in(own, dim), (parts,), jnp.float32, least / len(cuts), largest / len(cuts)))
        gain = gain * jnp.repeat(heights, dims[dim] // parts).reshape([-1 if axis == dim else 1 for axis in range(len(dims))])
    return gain


def gaussian(rng, shape, scale, most, shards=(), held_as=jnp.bfloat16):
    values = jax.random.normal(rng, shape, jnp.float32) * scale
    if len(shards) > 0:
        values = block_levels(rng, shape, shards, -0.22, 0.18) * values
    return jnp.clip(values, min=-most, max=most).astype(held_as)


def setup_inputs(seed: int = 0) -> dict:
    key_list = jax.random.split(jax.random.key(seed), 7)
    panels = gaussian(key_list[0], (SLOTS, NZ, XY), 1.0, 6.0, ((0, 4), (1, 8)))
    mean_field = jnp.clip(jnp.exp(math.log(2.0) - 1.3862944 * jax.random.uniform(key_list[1], (NZ, XY), jnp.float32) ** block_levels(key_list[1], (NZ, XY), ((0, 8),), -0.2, 0.2)), 0.5, 2.0)
    fluctuations = gaussian(key_list[2], (NPAR, NZ, XY), 0.3, 1.5, ((1, 8),), jnp.float32)
    products = gaussian(key_list[3], (NNZ,), 1.0, 4.0, (), jnp.float32)
    triples = draw_triples(jax.random.fold_in(key_list[6], 71), 0)
    owner_slot = draw_owner_slot(jax.random.fold_in(key_list[6], 71), 0)
    return dict(panels=panels, mean_field=mean_field, fluctuations=fluctuations, products=products, triples=triples, owner_slot=owner_slot)


scale_factor = 0.15


def shifted(source, offset, inside):
    length_last = source.shape[-1]
    padding = [(0, 0)] * (source.ndim - 1)
    if offset > 0:
        moved_values = jnp.pad(source[..., offset:], padding + [(0, offset)])
    else:
        moved_values = jnp.pad(source[..., :length_last + offset], padding + [(-offset, 0)])
    return jnp.where(inside, moved_values, jnp.zeros_like(moved_values))


def diffusion(extended, conductance_ext, side_cells):
    center = extended[..., 1:-1, :]
    conduct = conductance_ext[1:-1]
    flux_sum = 0.5 * (conduct + conductance_ext[2:]) * (center - extended[..., 2:, :])
    flux_sum = flux_sum + 0.5 * (conduct + conductance_ext[:-2]) * (center - extended[..., :-2, :])
    column = lax.iota(jnp.int32, center.shape[-1]) % side_cells
    everywhere = column >= 0
    for offset, inside in ((1, column < side_cells - 1), (-1, column > 0), (side_cells, everywhere), (-side_cells, everywhere)):
        flux_sum = flux_sum + 0.5 * (conduct + shifted(conduct, offset, inside)) * (center - shifted(center, offset, inside))
    return flux_sum


def first_rows(triples):
    entry_keys = (triples[:, 2] * P_SIZE + triples[:, 0]) * P_SIZE + triples[:, 1]
    matching = entry_keys[:, None] == entry_keys[None, :]
    earlier = lax.iota(jnp.int32, NNZ)[None, :] < lax.iota(jnp.int32, NNZ)[:, None]
    return jnp.logical_not(jnp.any(matching & earlier, axis=1))


def galerkin_apply(chaos_panels, padded_coef, tables, triples, leading):
    flat_panels = chaos_panels.reshape(P_SIZE, NZ * XY)
    result = jnp.zeros((P_SIZE, NZ, XY), jnp.float32)
    entry_values = tables[triples[:, 2], triples[:, 0], triples[:, 1]].astype(jnp.float32)
    for field_index in range(KF):
        weights = jnp.where(leading & (triples[:, 2] == field_index), entry_values, jnp.zeros_like(entry_values))

        def add_entry(running, entry):
            weight, row_index, column_index = entry
            return running.at[row_index].add(weight * flat_panels[column_index].astype(jnp.float32)), None

        running, _ = lax.scan(add_entry, jnp.zeros((P_SIZE, NZ * XY), jnp.float32), (weights, triples[:, 0], triples[:, 1]))
        combined = lax.optimization_barrier(running.astype(jnp.bfloat16))
        combined = combined.astype(jnp.float32).reshape(P_SIZE, NZ, XY)
        extended = jnp.pad(combined, ((0, 0), (1, 1), (0, 0)))
        result = result + diffusion(extended, padded_coef[field_index], NXY)
    return (scale_factor * result).astype(jnp.bfloat16)


def reference(panels, mean_field, fluctuations, products, triples, owner_slot):
    coefficients = jnp.concatenate([mean_field[None], fluctuations], axis=0)
    padded_coef = jnp.pad(coefficients, ((0, 0), (1, 1), (0, 0)))
    tables = jnp.zeros((KF, P_SIZE, P_SIZE), jnp.float32).at[triples[:, 2], triples[:, 0], triples[:, 1]].add(products)
    tables = tables.astype(jnp.bfloat16)
    leading = first_rows(triples)
    chaos_panels = panels[owner_slot]
    first_values = galerkin_apply(chaos_panels, padded_coef, tables, triples, leading)
    second_values = galerkin_apply(first_values, padded_coef, tables, triples, leading)
    empty_slots = jnp.zeros((SLOTS, NZ, XY), jnp.bfloat16)
    return empty_slots.at[owner_slot].set(first_values), empty_slots.at[owner_slot].set(second_values)
```

```python
import functools

import jax
import jax.numpy as jnp
from jax import lax
from jax.experimental import pallas as pl
from jax.experimental.pallas import tpu as pltpu
from jax.sharding import PartitionSpec as P

NXY = 48
SCALE = 0.15
LANES = 128
REACH = 2
BLOCK = 32
VMEM = pltpu.VMEM
F32, BF16 = jnp.float32, jnp.bfloat16


def up(value, step):
    return -(-value // step) * step


def params(megabytes):
    return pltpu.CompilerParams(vmem_limit_bytes=megabytes << 20)


def whole(count):
    return [pl.BlockSpec(memory_space=VMEM)] * count


def cut_kernel(count, chunk, me_ref, x_ref, *refs):
    *out_refs, held = refs
    planes, own, cells = x_ref.shape
    padded, width = out_refs[0].shape[1:]
    halo = REACH * NXY
    me = me_ref[0]
    held[...] = jnp.zeros_like(held)
    lane = lax.broadcasted_iota(jnp.int32, (padded, LANES), 1)
    for plane in range(planes):
        held[0:own, :] = x_ref[plane].astype(F32)
        values = held[...]
        for target in range(count):
            turned = values if target == 0 else pltpu.roll(values, cells - target * chunk, 1)
            body = turned[:, : up(chunk + halo, LANES)]
            column = lax.broadcasted_iota(jnp.int32, body.shape, 1)
            end = chunk if target == count - 1 else chunk + halo
            body = jnp.where(column < end, body, 0.0)
            if body.shape[1] < width:
                body = jnp.concatenate([body, jnp.zeros((padded, width - body.shape[1]), F32)], axis=1)
            before = turned[:, cells - LANES :]
            if target == 0:
                before = jnp.zeros_like(before)
            last = jnp.where(lane < LANES - halo, body[:, width - LANES :], before)
            window = jnp.concatenate([body[:, : width - LANES], last], axis=1).astype(BF16)
            for step in range(count):

                @pl.when(lax.bitwise_xor(me, target) == step)
                def _():
                    out_refs[step][plane] = window


def tables_kernel(fields, entries_ref, products_ref, slots_ref, out_ref, by_column):
    rows = by_column.shape[1]
    total = entries_ref.shape[1]
    names = slots_ref.shape[1]
    slots = slots_ref[...].astype(BF16)

    def placed(which):
        name = lax.broadcasted_iota(jnp.int32, (names, total), 0)
        chosen = jnp.where(name == entries_ref[which : which + 1, :], 1.0, 0.0).astype(BF16)
        return jnp.dot(slots, chosen, preferred_element_type=F32)[0:1].astype(jnp.int32)

    row, column = placed(0), placed(1)
    field = entries_ref[2:3, :]
    place = (row // BLOCK) * (fields * BLOCK) + field * BLOCK + row % BLOCK
    rest = products_ref[0:1, :]
    here = lax.broadcasted_iota(jnp.int32, (rows, total), 0) == column
    for part in range(3):
        piece = rest.astype(BF16).astype(F32)
        rest = rest - piece
        by_column[part] = jnp.where(here, piece, 0.0).astype(BF16)
    size = fields * BLOCK

    @pl.loop(0, rows // BLOCK)
    def _(block):
        index = lax.broadcasted_iota(jnp.int32, (size, total), 0) + block * size
        chosen = jnp.where(index == place, 1.0, 0.0).astype(BF16)
        acc = jnp.zeros((size, rows), F32)
        for part in range(3):
            acc += lax.dot_general(
                chosen, by_column[part], (((1,), (1,)), ((), ())), preferred_element_type=F32
            )
        out_ref[pl.ds(pl.multiple_of(block * size, size), size), :] = acc.astype(BF16)


def load_planes(piece_refs, before_ref, after_ref, store):
    planes = piece_refs[0].shape[0]

    def joined(parts):
        return jnp.concatenate([p.astype(F32) for p in parts], axis=0).astype(BF16)

    store[0] = joined([before_ref[i] for i in range(len(piece_refs))])
    for plane in range(planes):
        store[plane + 1] = joined([piece[plane] for piece in piece_refs])
    store[planes + 1] = joined([after_ref[i] for i in range(len(piece_refs))])


def apply_kernel(count, final, *refs):
    piece_refs = refs[:count]
    before_ref, after_ref, tables_ref, weights_ref, masks_ref = refs[count : count + 5]
    if final:
        out_refs = refs[count + 5 : 2 * count + 5]
        held, mixed, weights, result = refs[2 * count + 5 :]
    else:
        out_refs = refs[count + 5 : 2 * count + 5]
        own_refs = refs[2 * count + 5 : 3 * count + 5]
        edge_refs = refs[3 * count + 5 : 3 * count + 7]
        held, mixed, weights, result = refs[3 * count + 7 :]
    planes, padded, width = piece_refs[0].shape
    rows = count * padded
    fields = weights_ref.shape[1]
    load_planes(piece_refs, before_ref, after_ref, held)
    for plane in range(weights_ref.shape[0]):
        for field in range(fields):
            for way in range(6):
                weights[plane, field, way] = jnp.broadcast_to(
                    weights_ref[plane, field, way : way + 1, :], (8, width)
                )
    result[...] = jnp.zeros_like(result)
    size = fields * BLOCK

    def spread(value):
        return jnp.broadcast_to(value[None], (BLOCK // 8, 8, width)).reshape(BLOCK, width)

    for plane in range(planes + 2):
        mixed[...] = jnp.dot(tables_ref[...], held[plane], preferred_element_type=F32).astype(BF16)

        @pl.loop(0, rows // BLOCK)
        def _(block):
            start = pl.multiple_of(block * BLOCK, BLOCK)
            base = pl.multiple_of(block * size, size)

            def sums(ways):
                totals = [jnp.zeros((BLOCK, width), F32) for _ in ways]
                for field in range(fields):
                    values = mixed[pl.ds(base + field * BLOCK, BLOCK), :].astype(F32)
                    for i, way in enumerate(ways):
                        totals[i] += spread(weights[plane, field, way]) * values
                return totals

            here = pl.ds(start, BLOCK)
            if 0 < plane < planes + 1:
                ahead, behind = sums((0, 1))
                flux = ahead + behind - pltpu.roll(behind, width - NXY, 1) - pltpu.roll(ahead, NXY, 1)
                ahead, behind = sums((2, 3))
                flux += ahead + behind
                flux -= spread(masks_ref[0]) * pltpu.roll(behind, width - 1, 1)
                flux -= spread(masks_ref[1]) * pltpu.roll(ahead, 1, 1)
                ahead, behind = sums((4, 5))
                result[plane - 1, here, :] += flux + ahead + behind
                if plane < planes:
                    result[plane, here, :] -= ahead
                if plane > 1:
                    result[plane - 2, here, :] -= behind
            elif plane == 0:
                (ahead,) = sums((4,))
                result[0, here, :] -= ahead
            else:
                (behind,) = sums((5,))
                result[planes - 1, here, :] -= behind

    chunk = out_refs[0].shape[2]
    for plane in range(planes):
        values = SCALE * result[plane]
        if not final:
            values = values * jnp.broadcast_to(masks_ref[2][None], (rows // 8, 8, width)).reshape(rows, width)
        for step in range(count):
            part = values[step * padded : (step + 1) * padded]
            out_refs[step][plane] = part[:, :chunk].astype(BF16)
            if not final:
                own_refs[step][plane] = part.astype(BF16)
                if plane == 0:
                    edge_refs[0][step] = part.astype(BF16)
                if plane == planes - 1:
                    edge_refs[1][step] = part.astype(BF16)


def join_kernel(count, me_ref, *refs):
    piece_refs, (out_ref, held) = refs[:count], refs[count:]
    planes, own, cells = out_ref.shape
    chunk = piece_refs[0].shape[2]
    me = me_ref[0]
    for step in range(count):
        held[lax.bitwise_xor(me, step)] = piece_refs[step][...].astype(F32)
    for plane in range(planes):
        line = jnp.concatenate([held[source, plane][:, :chunk] for source in range(count)], axis=1)
        out_ref[plane] = line[:own].astype(BF16)


def shards(panels, mean_field, fluctuations, products, triples, owner_slot):
    count, slabs = lax.axis_size("chaos"), lax.axis_size("space")
    me = lax.axis_index("chaos")
    own, planes, cells = panels.shape
    chunk, halo = cells // count, REACH * NXY
    width = up(chunk + 2 * halo, LANES)
    padded = up(own, 8)
    rows = count * padded
    fields = 1 + fluctuations.shape[0]
    me_array = me.astype(jnp.int32).reshape(1)
    smem = pl.BlockSpec(memory_space=pltpu.SMEM)

    def exchange(block, step):
        return lax.ppermute(block, "chaos", [(i, i ^ step) for i in range(count)])

    def neighbours(first_plane, last_plane):
        upward = [(i, i + 1) for i in range(slabs - 1)]
        downward = [(target, source) for source, target in upward]
        return lax.ppermute(last_plane, "space", upward), lax.ppermute(first_plane, "space", downward)

    piece = jax.ShapeDtypeStruct((planes, padded, width), BF16)
    cut = pl.pallas_call(
        functools.partial(cut_kernel, count, chunk),
        out_shape=[piece] * count,
        in_specs=[smem] + whole(1),
        out_specs=whole(count),
        scratch_shapes=[VMEM((padded, cells), F32)],
        compiler_params=params(32),
        name="cut",
    )(me_array, jnp.transpose(panels, (1, 0, 2)))
    pieces = [cut[0]] + [exchange(cut[step], step) for step in range(1, count)]

    coefficients = jnp.concatenate([mean_field[None], fluctuations], axis=0)
    before, after = neighbours(coefficients[:, 0], coefficients[:, -1])
    coefficients = jnp.concatenate([before[:, None], coefficients, after[:, None]], axis=1)

    def window(array):
        array = jnp.pad(array, ((0, 0),) * (array.ndim - 1) + ((halo, halo),))
        array = lax.dynamic_slice_in_dim(array, me * chunk, chunk + 2 * halo, array.ndim - 1)
        gap = jnp.zeros(array.shape[:-1] + (width - chunk - 2 * halo,), array.dtype)
        return jnp.concatenate([array[..., halo:], gap, array[..., :halo]], axis=-1)

    conduct = window(coefficients)
    lane_grid = window(jnp.where(jnp.arange(cells) >= 0, jnp.arange(cells) % NXY, 0) + 1)
    not_last = jnp.where(lane_grid == NXY, 0.0, 1.0)
    not_first = jnp.where(lane_grid == 1, 0.0, 1.0)
    inside = jnp.where(lane_grid > 0, 1.0, 0.0)
    masks = jnp.broadcast_to(jnp.stack([not_last, not_first, inside])[:, None], (3, 8, width))
    middle = conduct[:, 1:-1]
    ways = [
        jnp.roll(middle, -NXY, -1),
        jnp.roll(middle, NXY, -1),
        jnp.roll(middle, -1, -1) * not_last,
        jnp.roll(middle, 1, -1) * not_first,
    ]
    zeros = jnp.zeros_like(middle[:, :1])
    faces = [jnp.pad(0.5 * (middle + way), ((0, 0), (1, 1), (0, 0))) for way in ways]
    rising = 0.5 * (conduct[:, :-1] + conduct[:, 1:])
    faces += [jnp.concatenate([rising, zeros], axis=1), jnp.concatenate([zeros, rising], axis=1)]
    weights = jnp.stack(faces, axis=0).transpose(2, 1, 0, 3)

    total = up(products.shape[0], 2 * LANES)
    names = up(owner_slot.shape[0], LANES)
    entries = jnp.pad(triples.T, ((0, 5), (0, total - products.shape[0])), constant_values=-1)
    values = jnp.pad(products, (0, total - products.shape[0]))[None]
    group = owner_slot // own
    slots = lax.bitwise_xor(group, me) * padded + owner_slot - group * own
    slots = jnp.broadcast_to(jnp.pad(slots, (0, names - slots.shape[0])).astype(F32)[None], (16, names))
    tables = pl.pallas_call(
        functools.partial(tables_kernel, fields),
        out_shape=jax.ShapeDtypeStruct((fields * rows, rows), BF16),
        in_specs=whole(3),
        out_specs=whole(1)[0],
        scratch_shapes=[VMEM((3, rows, total), BF16)],
        compiler_params=params(32),
        name="tables",
    )(entries, values, slots)

    def apply(parts, first_halo, last_halo, final):
        short = jax.ShapeDtypeStruct((planes, padded, chunk), BF16)
        out_shape = [short] * count
        if not final:
            edge = jax.ShapeDtypeStruct((count, padded, width), BF16)
            out_shape += [piece] * count + [edge, edge]
        return pl.pallas_call(
            functools.partial(apply_kernel, count, final),
            out_shape=out_shape,
            in_specs=whole(count + 5),
            out_specs=whole(len(out_shape)),
            scratch_shapes=[
                VMEM((planes + 2, rows, width), BF16),
                VMEM((fields * rows, width), BF16),
                VMEM((planes + 2, fields, 6, 8, width), F32),
                VMEM((planes, rows, width), F32),
            ],
            compiler_params=params(48),
            name="second" if final else "first",
        )(*parts, first_halo, last_halo, tables, weights, masks)

    def join(parts):
        joined = pl.pallas_call(
            functools.partial(join_kernel, count),
            out_shape=jax.ShapeDtypeStruct((planes, own, cells), BF16),
            in_specs=[smem] + whole(count),
            out_specs=whole(1)[0],
            scratch_shapes=[VMEM((count, planes, padded, chunk), F32)],
            compiler_params=params(32),
            name="join",
        )(me_array, *parts)
        return jnp.transpose(joined, (1, 0, 2))

    def back(parts):
        return [parts[0]] + [exchange(parts[step], step) for step in range(1, count)]

    low, high = neighbours(jnp.stack([p[0] for p in pieces]), jnp.stack([p[-1] for p in pieces]))
    first = apply(pieces, low, high, False)
    low, high = neighbours(first[-2], first[-1])
    second = apply(first[count : 2 * count], low, high, True)
    return join(back(first[:count])), join(back(second))


def solution(mesh):
    in_specs = (P("chaos", "space", None), P("space", None), P(None, "space", None), P(), P(), P())
    out_specs = (P("chaos", "space", None), P("chaos", "space", None))
    return jax.shard_map(shards, mesh=mesh, in_specs=in_specs, out_specs=out_specs, check_vma=False)
```

```python
import functools

import jax
import jax.numpy as jnp
from jax import lax
from jax.experimental import pallas as pl
from jax.experimental.pallas import tpu as pltpu
from jax.sharding import PartitionSpec as P

NXY = 48
SCALE = 0.15
LANES = 128
REACH = 2
BLOCK = 32
VMEM = pltpu.VMEM
F32, BF16 = jnp.float32, jnp.bfloat16
NEXT_X, LAST_X, NEXT_Y, LAST_Y, NEXT_Z, LAST_Z, ALL = range(7)


def up(value, step):
    return -(-value // step) * step


def call(kernel, name, out_shape, args, scratch=(), scalars=0, unread=0):
    in_specs = [pl.BlockSpec(memory_space=pltpu.SMEM)] * scalars
    in_specs += [pl.BlockSpec(memory_space=VMEM)] * (len(args) - scalars - unread)
    in_specs += [pl.BlockSpec(memory_space=pl.ANY)] * unread
    return pl.pallas_call(
        kernel,
        out_shape=out_shape,
        in_specs=in_specs,
        out_specs=[pl.BlockSpec(memory_space=VMEM)] * len(out_shape),
        scratch_shapes=scratch,
        compiler_params=pltpu.CompilerParams(vmem_limit_bytes=40 << 20),
        name=name,
    )(*args)


def cut_kernel(count, chunk, me_ref, x_ref, mean_ref, other_ref, *refs):
    edge_refs, middle_refs = refs[:count], refs[count : 2 * count]
    low_ref, high_ref, held = refs[2 * count :]
    planes, own, cells = x_ref.shape
    _, padded, width = edge_refs[0].shape
    halo = REACH * NXY
    me = me_ref[0]
    for out_ref, plane in ((low_ref, 0), (high_ref, planes - 1)):
        out_ref[0:1, :] = mean_ref[plane : plane + 1, :]
        for field in range(other_ref.shape[0]):
            out_ref[field + 1 : field + 2, :] = other_ref[field, plane : plane + 1, :]
    held[...] = jnp.zeros_like(held)
    lane = lax.broadcasted_iota(jnp.int32, (padded, LANES), 1)
    for plane in range(planes):
        held[0:own, :] = x_ref[plane].astype(F32)
        values = held[...]
        for target in range(count):
            turned = values if target == 0 else pltpu.roll(values, cells - target * chunk, 1)
            body = turned[:, : up(chunk + halo, LANES)]
            column = lax.broadcasted_iota(jnp.int32, body.shape, 1)
            end = chunk if target == count - 1 else chunk + halo
            body = jnp.where(column < end, body, 0.0)
            if body.shape[1] < width:
                body = jnp.concatenate([body, jnp.zeros((padded, width - body.shape[1]), F32)], axis=1)
            before = turned[:, cells - LANES :]
            if target == 0:
                before = jnp.zeros_like(before)
            last = jnp.where(lane < LANES - halo, body[:, width - LANES :], before)
            window = jnp.concatenate([body[:, : width - LANES], last], axis=1).astype(BF16)
            for step in range(count):

                @pl.when(lax.bitwise_xor(me, target) == step)
                def _():
                    if plane == 0:
                        edge_refs[step][0] = window
                    elif plane == planes - 1:
                        edge_refs[step][1] = window
                    else:
                        middle_refs[step][...] = window


def tables_kernel(fields, entries_ref, products_ref, slots_ref, out_ref, by_column):
    rows = by_column.shape[1]
    total = entries_ref.shape[1]
    names = slots_ref.shape[1]
    slots = slots_ref[...].astype(BF16)

    def placed(which):
        name = lax.broadcasted_iota(jnp.int32, (names, total), 0)
        chosen = jnp.where(name == entries_ref[which : which + 1, :], 1.0, 0.0).astype(BF16)
        return jnp.dot(slots, chosen, preferred_element_type=F32)[0:1].astype(jnp.int32)

    row, column = placed(0), placed(1)
    field = entries_ref[2:3, :]
    place = (row // BLOCK) * (fields * BLOCK) + field * BLOCK + row % BLOCK
    rest = products_ref[0:1, :]
    here = lax.broadcasted_iota(jnp.int32, (rows, total), 0) == column
    for part in range(3):
        piece = rest.astype(BF16).astype(F32)
        rest = rest - piece
        by_column[part] = jnp.where(here, piece, 0.0).astype(BF16)
    size = fields * BLOCK

    @pl.loop(0, rows // BLOCK)
    def _(block):
        index = lax.broadcasted_iota(jnp.int32, (size, total), 0) + block * size
        chosen = jnp.where(index == place, 1.0, 0.0).astype(BF16)
        acc = jnp.zeros((size, rows), F32)
        for part in range(3):
            acc += lax.dot_general(
                chosen, by_column[part], (((1,), (1,)), ((), ())), preferred_element_type=F32
            )
        out_ref[pl.ds(pl.multiple_of(block * size, size), size), :] = acc.astype(BF16)


def weights_kernel(conduct_ref, masks_ref, out_ref):
    planes, fields, _, tiles = out_ref.shape[:4]
    width = tiles * LANES

    def mask(which):
        return jnp.concatenate([masks_ref[which, tile, 0:1, :] for tile in range(tiles)], axis=1)

    for plane in range(planes):
        own = conduct_ref[plane + 1]
        others = (
            pltpu.roll(own, width - NXY, 1),
            pltpu.roll(own, NXY, 1),
            pltpu.roll(own, width - 1, 1) * mask(0),
            pltpu.roll(own, 1, 1) * mask(1),
            conduct_ref[plane + 2],
            conduct_ref[plane],
        )
        for way, other in enumerate(others):
            face = 0.5 * (own + other)
            for field in range(fields):
                for tile in range(tiles):
                    out_ref[plane, field, way, tile] = jnp.broadcast_to(
                        face[field : field + 1, tile * LANES : (tile + 1) * LANES], (8, LANES)
                    )


def joined(parts):
    return jnp.concatenate([part.astype(F32) for part in parts], axis=0).astype(BF16)


def edges_kernel(count, *refs):
    parts, (low_ref, high_ref) = refs[:count], refs[-2:]
    low_ref[...] = joined([part[0] for part in parts])
    high_ref[...] = joined([part[1] for part in parts])


def spread(value):
    return jnp.broadcast_to(value[None], (BLOCK // 8, 8, LANES)).reshape(BLOCK, LANES)


def mix(tables_ref, values, mixed):
    result = jnp.dot(tables_ref[...], values, preferred_element_type=F32).astype(BF16)
    for tile in range(values.shape[1] // LANES):
        mixed[tile] = result[:, tile * LANES : (tile + 1) * LANES]


def weigh(mixed, weights_ref, plane, ways, sums):
    _, tiles, rows, _ = sums.shape
    fields = weights_ref.shape[1]

    @pl.loop(0, rows // BLOCK * tiles)
    def _(index):
        block, tile = index // tiles, index % tiles
        here = pl.ds(pl.multiple_of(block * BLOCK, BLOCK), BLOCK)
        base = pl.multiple_of(block * (fields * BLOCK), fields * BLOCK)
        totals = [jnp.zeros((BLOCK, LANES), F32) for _ in ways]
        for field in range(fields):
            values = mixed[tile, pl.ds(base + field * BLOCK, BLOCK), :].astype(F32)
            for i, way in enumerate(ways):
                totals[i] += spread(weights_ref[plane, field, way, tile]) * values
        for i, way in enumerate(ways):
            sums[way, tile, here, :] = totals[i]
        if len(ways) == 6:
            sums[ALL, tile, here, :] = functools.reduce(jnp.add, totals)


def settle(sums, masks_ref, write):
    _, tiles, rows, _ = sums.shape
    lane = lax.broadcasted_iota(jnp.int32, (BLOCK, LANES), 1)
    for block in range(rows // BLOCK):
        here = slice(block * BLOCK, (block + 1) * BLOCK)

        def ahead(way, shift):
            turned = [pltpu.roll(sums[way, tile, here, :], LANES - shift, 1) for tile in range(tiles)]
            return [jnp.where(lane < LANES - shift, turned[t], turned[(t + 1) % tiles]) for t in range(tiles)]

        def behind(way, shift):
            turned = [pltpu.roll(sums[way, tile, here, :], shift, 1) for tile in range(tiles)]
            return [jnp.where(lane >= shift, turned[t], turned[(t - 1) % tiles]) for t in range(tiles)]

        shares = zip(ahead(LAST_X, NXY), behind(NEXT_X, NXY), ahead(LAST_Y, 1), behind(NEXT_Y, 1))
        for tile, (a, b, c, d) in enumerate(shares):
            value = sums[ALL, tile, here, :] - a - b
            value = value - spread(masks_ref[0, tile]) * c - spread(masks_ref[1, tile]) * d
            write(tile, here, value)


def outer(low, high, tables_ref, weights_ref, masks_ref, low_out, high_out, middle_out, mixed, sums):
    last = weights_ref.shape[0] - 1
    for plane, values, out_ref, way in ((0, low, low_out, NEXT_Z), (last, high, high_out, LAST_Z)):
        mix(tables_ref, values, mixed)
        weigh(mixed, weights_ref, plane, range(6), sums)

        def write(tile, here, value):
            out_ref[tile, here, :] = value
            given = sums[way, tile, here, :]
            middle_out[tile, here, :] = -given if plane == 0 else middle_out[tile, here, :] - given

        settle(sums, masks_ref, write)


def inner(values, low_in, high_in, middle_in, tables_ref, weights_ref, masks_ref, low_out, high_out, out, mixed, sums):
    mix(tables_ref, values, mixed)
    weigh(mixed, weights_ref, 1, range(6), sums)

    def write(tile, here, value):
        out[tile, here, :] = SCALE * (value + middle_in[tile, here, :])
        low_out[tile, here, :] = low_in[tile, here, :] - sums[LAST_Z, tile, here, :]
        high_out[tile, here, :] = high_in[tile, here, :] - sums[NEXT_Z, tile, here, :]

    settle(sums, masks_ref, write)


def emit(result, masks_ref, whole_ref, piece_refs, plane):
    tiles, rows, _ = result.shape
    if whole_ref is not None:
        for tile in range(tiles):
            inside = jnp.broadcast_to(masks_ref[2, tile][None], (rows // 8, 8, LANES)).reshape(rows, LANES)
            whole_ref[:, tile * LANES : (tile + 1) * LANES] = (result[tile] * inside).astype(BF16)
    padded, chunk = piece_refs[0].shape[-2:]
    for step, piece_ref in enumerate(piece_refs):
        for tile in range(up(chunk, LANES) // LANES):
            lanes = min(LANES, chunk - tile * LANES)
            part = result[tile, step * padded : (step + 1) * padded, :][:, :lanes].astype(BF16)
            if plane is None:
                piece_ref[:, tile * LANES : tile * LANES + lanes] = part
            else:
                piece_ref[plane, :, tile * LANES : tile * LANES + lanes] = part


def outer_kernel(low_ref, high_ref, tables_ref, weights_ref, masks_ref, low_out, high_out, middle_out, mixed, sums):
    outer(
        low_ref[...], high_ref[...], tables_ref, weights_ref, masks_ref, low_out, high_out, middle_out, mixed, sums
    )


def inner_kernel(count, *refs):
    parts = refs[:count]
    low_in, high_in, middle_in, tables_ref, weights_ref, masks_ref = refs[count : count + 6]
    low_out, high_out, whole_ref, *pieces = refs[count + 6 : 2 * count + 9]
    mixed, sums, result = refs[2 * count + 9 :]
    values = joined([part[...] for part in parts])
    inner(
        values, low_in, high_in, middle_in, tables_ref, weights_ref, masks_ref, low_out, high_out, result, mixed, sums
    )
    emit(result, masks_ref, whole_ref, pieces, None)


def own_kernel(low_ref, values_ref, high_ref, tables_ref, weights_ref, masks_ref, low_out, high_out, *refs):
    *pieces, mixed, sums, result, middle, low, high = refs
    outer(low_ref[...], high_ref[...], tables_ref, weights_ref, masks_ref, low, high, middle, mixed, sums)
    inner(
        values_ref[...], low, high, middle, tables_ref, weights_ref, masks_ref, low_out, high_out, result, mixed, sums
    )
    emit(result, masks_ref, None, pieces, None)


def fix_kernel(count, first, before_ref, after_ref, low_in, high_in, tables_ref, weights_ref, masks_ref, *refs):
    if first:
        wholes, nears, refs = refs[:2], refs[2:4], refs[4:]
    pieces, (mixed, sums, result) = refs[:count], refs[count:]
    last = weights_ref.shape[0] - 1
    sides = ((before_ref, low_in, 0, LAST_Z), (after_ref, high_in, last, NEXT_Z))
    for side, (halo_ref, share_ref, plane, way) in enumerate(sides):
        mix(tables_ref, halo_ref[...], mixed)
        weigh(mixed, weights_ref, plane, (way,), sums)
        for tile in range(sums.shape[1]):
            result[tile] = SCALE * (share_ref[tile] - sums[way, tile])
        emit(result, masks_ref, wholes[side] if first else None, pieces, side)
        if first:
            nears[side][...] = wholes[side][:, : nears[side].shape[1]]


def join_kernel(count, me_ref, *refs):
    edge_refs, middle_refs, (out_ref, held) = refs[:count], refs[count : 2 * count], refs[2 * count :]
    planes, own, cells = out_ref.shape
    me = me_ref[0]
    for step in range(count):
        source = lax.bitwise_xor(me, step)
        held[source, 0] = edge_refs[step][0].astype(F32)
        held[source, 1] = middle_refs[step][...].astype(F32)
        held[source, 2] = edge_refs[step][1].astype(F32)
    for plane in range(planes):
        line = jnp.concatenate([held[source, plane] for source in range(count)], axis=1)
        out_ref[plane] = line[:own].astype(BF16)


def shards(panels, mean_field, fluctuations, products, triples, owner_slot):
    count, slabs = lax.axis_size("chaos"), lax.axis_size("space")
    me = lax.axis_index("chaos")
    own, planes, cells = panels.shape
    assert planes == 3
    chunk, halo = cells // count, REACH * NXY
    width = up(chunk + 2 * halo, LANES)
    near = up(chunk, LANES)
    padded = up(own, 8)
    rows = count * padded
    fields = 1 + fluctuations.shape[0]
    me_array = me.astype(jnp.int32).reshape(1)
    tiles = width // LANES

    def exchange(block, step):
        return lax.ppermute(block, "chaos", [(i, i ^ step) for i in range(count)])

    def exchanged(blocks):
        return [blocks[0]] + [exchange(blocks[step], step) for step in range(1, count)]

    def neighbours(first_plane, last_plane):
        upward = [(i, i + 1) for i in range(slabs - 1)]
        downward = [(target, source) for source, target in upward]
        return lax.ppermute(last_plane, "space", upward), lax.ppermute(first_plane, "space", downward)

    def shape(*dims, dtype=BF16):
        return jax.ShapeDtypeStruct(dims, dtype)

    cut = call(
        functools.partial(cut_kernel, count, chunk),
        "cut",
        [shape(2, padded, width)] * count + [shape(padded, width)] * count + [shape(fields, cells, dtype=F32)] * 2,
        (me_array, jnp.transpose(panels, (1, 0, 2)), mean_field, fluctuations),
        [VMEM((padded, cells), F32)],
        scalars=1,
    )
    edges, middles = exchanged(cut[:count]), exchanged(cut[count : 2 * count])

    total = up(products.shape[0], 2 * LANES)
    names = up(owner_slot.shape[0], LANES)
    entries = jnp.pad(triples.T, ((0, 5), (0, total - products.shape[0])), constant_values=-1)
    values = jnp.pad(products, (0, total - products.shape[0]))[None]
    group = owner_slot // own
    slots = lax.bitwise_xor(group, me) * padded + owner_slot - group * own
    slots = jnp.broadcast_to(jnp.pad(slots, (0, names - slots.shape[0])).astype(F32)[None], (16, names))
    (tables,) = call(
        functools.partial(tables_kernel, fields),
        "tables",
        [shape(fields * rows, rows)],
        (entries, values, slots),
        [VMEM((3, rows, total), BF16)],
    )

    before, after = neighbours(*cut[2 * count :])
    conduct = jnp.concatenate([mean_field[:, None], fluctuations.transpose(1, 0, 2)], axis=1)
    conduct = jnp.concatenate([before[None], conduct, after[None]], axis=0)
    conduct = jnp.pad(conduct, ((0, 0), (0, 0), (halo, halo)))
    conduct = lax.dynamic_slice_in_dim(conduct, me * chunk, chunk + 2 * halo, 2)
    gap = jnp.zeros(conduct.shape[:-1] + (width - chunk - 2 * halo,), F32)
    conduct = jnp.concatenate([conduct[..., halo:], gap, conduct[..., :halo]], axis=-1)

    lane = jnp.arange(width)
    place = jnp.where(lane < width - halo, lane, lane - width) + halo
    row = place // NXY - REACH + me * (chunk // NXY)
    inside = (row >= 0) & (row < NXY) & ((lane < chunk + halo) | (lane >= width - halo))
    masks = jnp.stack([place % NXY < NXY - 1, place % NXY > 0, inside]).astype(F32)
    masks = jnp.broadcast_to(masks.reshape(3, tiles, 1, LANES), (3, tiles, 8, LANES))
    (weights,) = call(
        weights_kernel, "weights", [shape(planes, fields, 6, tiles, 8, LANES, dtype=F32)], (conduct, masks)
    )

    common = (tables, weights, masks)
    plane_whole = shape(rows, width)
    share = shape(tiles, rows, LANES, dtype=F32)
    piece, pair = shape(padded, chunk), shape(2, padded, chunk)
    mixed = VMEM((tiles, fields * rows, LANES), BF16)
    sums = VMEM((7, tiles, rows, LANES), F32)
    result = VMEM((tiles, rows, LANES), F32)

    low, high = call(
        functools.partial(edges_kernel, count), "edges", [plane_whole] * 2, (*edges, tables, weights), unread=2
    )
    before, after = neighbours(low, high)
    low, high, middle = call(outer_kernel, "outer", [share] * 3, (low, high, *common), [mixed, sums])
    low, high, middle, *first_middles = call(
        functools.partial(inner_kernel, count),
        "inner",
        [share] * 2 + [plane_whole] + [piece] * count,
        (*middles, low, high, middle, *common),
        [mixed, sums, result],
    )
    first_middles = exchanged(first_middles)
    low, high, low_near, high_near, *first_edges = call(
        functools.partial(fix_kernel, count, True),
        "fix",
        [plane_whole] * 2 + [shape(rows, near)] * 2 + [pair] * count,
        (before, after, low, high, *common),
        [mixed, sums, result],
    )
    before, after = neighbours(low_near, high_near)
    first_edges = exchanged(first_edges)
    low, high, *second_middles = call(
        own_kernel,
        "own",
        [share] * 2 + [piece] * count,
        (low, middle, high, *common),
        [mixed, sums] + [result] * 4,
    )
    second_middles = exchanged(second_middles)
    near_tiles = near // LANES
    second_edges = exchanged(
        call(
            functools.partial(fix_kernel, count, False),
            "last",
            [pair] * count,
            (before, after, low, high, *common),
            [
                VMEM((near_tiles, fields * rows, LANES), BF16),
                VMEM((7, near_tiles, rows, LANES), F32),
                VMEM((near_tiles, rows, LANES), F32),
            ],
        )
    )

    def join(edge_parts, middle_parts):
        (result,) = call(
            functools.partial(join_kernel, count),
            "join",
            [shape(planes, own, cells)],
            (me_array, *edge_parts, *middle_parts),
            [VMEM((count, planes, padded, chunk), F32)],
            scalars=1,
        )
        return jnp.transpose(result, (1, 0, 2))

    return join(first_edges, first_middles), join(second_edges, second_middles)


def solution(mesh):
    in_specs = (P("chaos", "space", None), P("space", None), P(None, "space", None), P(), P(), P())
    out_specs = (P("chaos", "space", None), P("chaos", "space", None))
    return jax.shard_map(shards, mesh=mesh, in_specs=in_specs, out_specs=out_specs, check_vma=False)
```

```python
import functools

import jax
import jax.numpy as jnp
from jax import lax
from jax.experimental import pallas as pl
from jax.experimental.pallas import tpu as pltpu
from jax.sharding import PartitionSpec as P

NXY = 48
SCALE = 0.15
LANES = 128
REACH = 2
BLOCK = 32
VMEM = pltpu.VMEM
F32, BF16 = jnp.float32, jnp.bfloat16
NEXT_X, LAST_X, NEXT_Y, LAST_Y, NEXT_Z, LAST_Z, ALL = range(7)


def up(value, step):
    return -(-value // step) * step


def call(kernel, name, micros, out_shape, args, scratch=(), scalars=0, unread=0):
    in_specs = [pl.BlockSpec(memory_space=pltpu.SMEM)] * scalars
    in_specs += [pl.BlockSpec(memory_space=VMEM)] * (len(args) - scalars - unread)
    in_specs += [pl.BlockSpec(memory_space=pl.ANY)] * unread
    return pl.pallas_call(
        kernel,
        out_shape=out_shape,
        in_specs=in_specs,
        out_specs=[pl.BlockSpec(memory_space=VMEM)] * len(out_shape),
        scratch_shapes=scratch,
        compiler_params=pltpu.CompilerParams(vmem_limit_bytes=40 << 20),
        cost_estimate=pl.CostEstimate(flops=0, bytes_accessed=int(micros * 3.6e6), transcendentals=0),
        name=name,
    )(*args)


def cut_kernel(count, chunk, me_ref, x_ref, *refs):
    edge_refs, middle_refs = refs[:count], refs[count : 2 * count]
    held = refs[2 * count]
    planes, own, cells = x_ref.shape
    _, padded, width = edge_refs[0].shape
    halo = REACH * NXY
    me = me_ref[0]
    held[...] = jnp.zeros_like(held)
    lane = lax.broadcasted_iota(jnp.int32, (padded, LANES), 1)
    for plane in range(planes):
        held[0:own, :] = x_ref[plane].astype(F32)
        values = held[...]
        for target in range(count):
            turned = values if target == 0 else pltpu.roll(values, cells - target * chunk, 1)
            body = turned[:, : up(chunk + halo, LANES)]
            column = lax.broadcasted_iota(jnp.int32, body.shape, 1)
            end = chunk if target == count - 1 else chunk + halo
            body = jnp.where(column < end, body, 0.0)
            if body.shape[1] < width:
                body = jnp.concatenate([body, jnp.zeros((padded, width - body.shape[1]), F32)], axis=1)
            before = turned[:, cells - LANES :]
            if target == 0:
                before = jnp.zeros_like(before)
            last = jnp.where(lane < LANES - halo, body[:, width - LANES :], before)
            window = jnp.concatenate([body[:, : width - LANES], last], axis=1).astype(BF16)
            for step in range(count):

                @pl.when(lax.bitwise_xor(me, target) == step)
                def _():
                    if plane == 0:
                        edge_refs[step][0] = window
                    elif plane == planes - 1:
                        edge_refs[step][1] = window
                    else:
                        middle_refs[step][...] = window


def sides_kernel(mean_ref, other_ref, _, low_ref, high_ref):
    for out_ref, plane in ((low_ref, 0), (high_ref, mean_ref.shape[0] - 1)):
        out_ref[0:1, :] = mean_ref[plane : plane + 1, :]
        for field in range(other_ref.shape[0]):
            out_ref[field + 1 : field + 2, :] = other_ref[field, plane : plane + 1, :]


def tables_kernel(fields, entries_ref, products_ref, slots_ref, _, out_ref, by_column):
    rows = by_column.shape[1]
    total = entries_ref.shape[1]
    names = slots_ref.shape[1]
    slots = slots_ref[...].astype(BF16)

    def placed(which):
        name = lax.broadcasted_iota(jnp.int32, (names, total), 0)
        chosen = jnp.where(name == entries_ref[which : which + 1, :], 1.0, 0.0).astype(BF16)
        return jnp.dot(slots, chosen, preferred_element_type=F32)[0:1].astype(jnp.int32)

    row, column = placed(0), placed(1)
    field = entries_ref[2:3, :]
    place = (row // BLOCK) * (fields * BLOCK) + field * BLOCK + row % BLOCK
    rest = products_ref[0:1, :]
    here = lax.broadcasted_iota(jnp.int32, (rows, total), 0) == column
    for part in range(3):
        piece = rest.astype(BF16).astype(F32)
        rest = rest - piece
        by_column[part] = jnp.where(here, piece, 0.0).astype(BF16)
    size = fields * BLOCK

    @pl.loop(0, rows // BLOCK)
    def _(block):
        index = lax.broadcasted_iota(jnp.int32, (size, total), 0) + block * size
        chosen = jnp.where(index == place, 1.0, 0.0).astype(BF16)
        acc = jnp.zeros((size, rows), F32)
        for part in range(3):
            acc += lax.dot_general(
                chosen, by_column[part], (((1,), (1,)), ((), ())), preferred_element_type=F32
            )
        out_ref[pl.ds(pl.multiple_of(block * size, size), size), :] = acc.astype(BF16)


def weights_kernel(conduct_ref, masks_ref, out_ref):
    planes, fields, _, tiles = out_ref.shape[:4]
    width = tiles * LANES

    def mask(which):
        return jnp.concatenate([masks_ref[which, tile, 0:1, :] for tile in range(tiles)], axis=1)

    for plane in range(planes):
        own = conduct_ref[plane + 1]
        others = (
            pltpu.roll(own, width - NXY, 1),
            pltpu.roll(own, NXY, 1),
            pltpu.roll(own, width - 1, 1) * mask(0),
            pltpu.roll(own, 1, 1) * mask(1),
            conduct_ref[plane + 2],
            conduct_ref[plane],
        )
        for way, other in enumerate(others):
            face = 0.5 * (own + other)
            for field in range(fields):
                for tile in range(tiles):
                    out_ref[plane, field, way, tile] = jnp.broadcast_to(
                        face[field : field + 1, tile * LANES : (tile + 1) * LANES], (8, LANES)
                    )


def joined(parts):
    return jnp.concatenate([part.astype(F32) for part in parts], axis=0).astype(BF16)


def edges_kernel(count, *refs):
    parts, (low_ref, high_ref) = refs[:count], refs[-2:]
    low_ref[...] = joined([part[0] for part in parts])
    high_ref[...] = joined([part[1] for part in parts])


def spread(value):
    return jnp.broadcast_to(value[None], (BLOCK // 8, 8, LANES)).reshape(BLOCK, LANES)


def mix(tables_ref, values, mixed):
    result = jnp.dot(tables_ref[...], values, preferred_element_type=F32).astype(BF16)
    for tile in range(values.shape[1] // LANES):
        mixed[tile] = result[:, tile * LANES : (tile + 1) * LANES]


def weigh(mixed, weights_ref, plane, ways, sums):
    _, tiles, rows, _ = sums.shape
    fields = weights_ref.shape[1]
    for tile in range(tiles):
        for block in range(rows // BLOCK):
            totals = [None] * len(ways)
            for field in range(fields):
                start = (block * fields + field) * BLOCK
                values = mixed[tile, start : start + BLOCK, :].astype(F32)
                for i, way in enumerate(ways):
                    term = spread(weights_ref[plane, field, way, tile]) * values
                    totals[i] = term if field == 0 else totals[i] + term
            here = slice(block * BLOCK, (block + 1) * BLOCK)
            for i, way in enumerate(ways):
                sums[way, tile, here, :] = totals[i]
            if len(ways) == 6:
                sums[ALL, tile, here, :] = functools.reduce(jnp.add, totals)


def settle(sums, masks_ref, write):
    _, tiles, rows, _ = sums.shape
    lane = lax.broadcasted_iota(jnp.int32, (BLOCK, LANES), 1)
    for block in range(rows // BLOCK):
        here = slice(block * BLOCK, (block + 1) * BLOCK)

        def ahead(way, shift):
            turned = [pltpu.roll(sums[way, tile, here, :], LANES - shift, 1) for tile in range(tiles)]
            return [jnp.where(lane < LANES - shift, turned[t], turned[(t + 1) % tiles]) for t in range(tiles)]

        def behind(way, shift):
            turned = [pltpu.roll(sums[way, tile, here, :], shift, 1) for tile in range(tiles)]
            return [jnp.where(lane >= shift, turned[t], turned[(t - 1) % tiles]) for t in range(tiles)]

        shares = zip(ahead(LAST_X, NXY), behind(NEXT_X, NXY), ahead(LAST_Y, 1), behind(NEXT_Y, 1))
        for tile, (a, b, c, d) in enumerate(shares):
            value = sums[ALL, tile, here, :] - a - b
            value = value - spread(masks_ref[0, tile]) * c - spread(masks_ref[1, tile]) * d
            write(tile, here, value)


def outer(low, high, tables_ref, weights_ref, masks_ref, low_out, high_out, middle_out, mixed, sums):
    last = weights_ref.shape[0] - 1
    for plane, values, out_ref, way in ((0, low, low_out, NEXT_Z), (last, high, high_out, LAST_Z)):
        mix(tables_ref, values, mixed)
        weigh(mixed, weights_ref, plane, range(6), sums)

        def write(tile, here, value):
            out_ref[tile, here, :] = value
            given = sums[way, tile, here, :]
            middle_out[tile, here, :] = -given if plane == 0 else middle_out[tile, here, :] - given

        settle(sums, masks_ref, write)


def inner(values, low_in, high_in, middle_in, tables_ref, weights_ref, masks_ref, low_out, high_out, out, mixed, sums):
    mix(tables_ref, values, mixed)
    weigh(mixed, weights_ref, 1, range(6), sums)

    def write(tile, here, value):
        out[tile, here, :] = SCALE * (value + middle_in[tile, here, :])
        low_out[tile, here, :] = low_in[tile, here, :] - sums[LAST_Z, tile, here, :]
        high_out[tile, here, :] = high_in[tile, here, :] - sums[NEXT_Z, tile, here, :]

    settle(sums, masks_ref, write)


def fill(result, masks_ref, out_ref):
    tiles, rows, _ = result.shape
    for tile in range(tiles):
        inside = jnp.broadcast_to(masks_ref[2, tile][None], (rows // 8, 8, LANES)).reshape(rows, LANES)
        out_ref[:, tile * LANES : (tile + 1) * LANES] = (result[tile] * inside).astype(BF16)


def packing(planes, chunk):
    full, odd = divmod(chunk, LANES)
    beside = LANES // odd if odd else 0
    return full, odd, beside, planes * full + (-(-planes // beside) if odd else 0)


def emit(results, chunk, piece_refs):
    full, odd, beside, _ = packing(len(results), chunk)
    padded = piece_refs[0].shape[1]
    lane = lax.broadcasted_iota(jnp.int32, (padded, LANES), 1)
    for step, piece_ref in enumerate(piece_refs):
        here = slice(step * padded, (step + 1) * padded)
        for plane, result in enumerate(results):
            for tile in range(full):
                piece_ref[plane * full + tile] = result[tile, here, :].astype(BF16)
        for first in range(0, len(results) if odd else 0, beside or 1):
            packed = results[first][full, here, :]
            for place in range(1, min(beside, len(results) - first)):
                turned = pltpu.roll(results[first + place][full, here, :], place * odd, 1)
                packed = jnp.where(lane < place * odd, packed, turned)
            piece_ref[len(results) * full + first // beside] = packed.astype(BF16)


def outer_kernel(low_ref, high_ref, tables_ref, weights_ref, masks_ref, *refs):
    low_out, high_out, middle_out, mixed, sums = refs[-5:]
    outer(
        low_ref[...], high_ref[...], tables_ref, weights_ref, masks_ref, low_out, high_out, middle_out, mixed, sums
    )


def inner_kernel(count, *refs):
    parts = refs[:count]
    low_in, high_in, middle_in, tables_ref, weights_ref, masks_ref = refs[count : count + 6]
    low_out, high_out, middle_out, whole_ref, mixed, sums = refs[count + 6 :]
    values = joined([part[...] for part in parts])
    inner(
        values, low_in, high_in, middle_in, tables_ref, weights_ref, masks_ref, low_out, high_out, middle_out, mixed, sums
    )
    fill(middle_out, masks_ref, whole_ref)


def own_kernel(
    low_ref, values_ref, high_ref, tables_ref, weights_ref, masks_ref, low_out, high_out, middle_out, mixed, sums, *held
):
    low, high, middle = held
    outer(low_ref[...], high_ref[...], tables_ref, weights_ref, masks_ref, low, high, middle, mixed, sums)
    inner(
        values_ref[...], low, high, middle, tables_ref, weights_ref, masks_ref, low_out, high_out, middle_out, mixed, sums
    )


def fix_kernel(count, chunk, first, before_ref, after_ref, low_in, high_in, middle_in, *refs):
    tables_ref, weights_ref, masks_ref, *refs = refs
    if first:
        wholes, nears, refs = refs[:2], refs[2:4], refs[4:]
    pieces, (mixed, sums, low, high) = refs[:count], refs[count:]
    last = weights_ref.shape[0] - 1
    sides = ((before_ref, low_in, low, 0, LAST_Z), (after_ref, high_in, high, last, NEXT_Z))
    for side, (halo_ref, share_ref, result, plane, way) in enumerate(sides):
        mix(tables_ref, halo_ref[...], mixed)
        weigh(mixed, weights_ref, plane, (way,), sums)
        for tile in range(sums.shape[1]):
            result[tile] = SCALE * (share_ref[tile] - sums[way, tile])
        if first:
            fill(result, masks_ref, wholes[side])
            nears[side][...] = wholes[side][:, : nears[side].shape[1]]
    emit((low, middle_in, high), chunk, pieces)


def join_kernel(count, chunk, me_ref, *refs):
    piece_refs, (out_ref, held) = refs[:count], refs[count:]
    planes, own, _ = out_ref.shape
    full, odd, beside, _ = packing(planes, chunk)
    me = me_ref[0]
    for step in range(count):
        held[lax.bitwise_xor(me, step)] = piece_refs[step][...].astype(F32)
    for plane in range(planes):
        parts = []
        for source in range(count):
            parts += [held[source, plane * full + tile] for tile in range(full)]
            if odd:
                tile, place = planes * full + plane // beside, plane % beside
                parts.append(held[source, tile][:, place * odd : (place + 1) * odd])
        out_ref[plane] = jnp.concatenate(parts, axis=1)[:own].astype(BF16)


def shards(panels, mean_field, fluctuations, products, triples, owner_slot):
    count, slabs = lax.axis_size("chaos"), lax.axis_size("space")
    me = lax.axis_index("chaos")
    own, planes, cells = panels.shape
    assert planes == 3
    chunk, halo = cells // count, REACH * NXY
    width = up(chunk + 2 * halo, LANES)
    near = up(chunk, LANES)
    padded = up(own, 8)
    rows = count * padded
    fields = 1 + fluctuations.shape[0]
    me_array = me.astype(jnp.int32).reshape(1)
    tiles = width // LANES

    def exchange(block, step):
        return lax.ppermute(block, "chaos", [(i, i ^ step) for i in range(count)])

    def exchanged(blocks):
        return [blocks[0]] + [exchange(blocks[step], step) for step in range(1, count)]

    def neighbours(first_plane, last_plane):
        upward = [(i, i + 1) for i in range(slabs - 1)]
        downward = [(target, source) for source, target in upward]
        return lax.ppermute(last_plane, "space", upward), lax.ppermute(first_plane, "space", downward)

    def shape(*dims, dtype=BF16):
        return jax.ShapeDtypeStruct(dims, dtype)

    cut = call(
        functools.partial(cut_kernel, count, chunk),
        "cut",
        1,
        [shape(2, padded, width)] * count + [shape(padded, width)] * count,
        (me_array, jnp.transpose(panels, (1, 0, 2))),
        [VMEM((padded, cells), F32)],
        scalars=1,
    )
    edges, middles = exchanged(cut[:count]), exchanged(cut[count : 2 * count])

    total = up(products.shape[0], 2 * LANES)
    names = up(owner_slot.shape[0], LANES)
    entries = jnp.pad(triples.T, ((0, 5), (0, total - products.shape[0])), constant_values=-1)
    values = jnp.pad(products, (0, total - products.shape[0]))[None]
    group = owner_slot // own
    slots = lax.bitwise_xor(group, me) * padded + owner_slot - group * own
    slots = jnp.broadcast_to(jnp.pad(slots, (0, names - slots.shape[0])).astype(F32)[None], (16, names))
    (tables,) = call(
        functools.partial(tables_kernel, fields),
        "tables",
        5,
        [shape(fields * rows, rows)],
        (entries, values, slots, cut[0]),
        [VMEM((3, rows, total), BF16)],
        unread=1,
    )

    sides = call(
        sides_kernel,
        "sides",
        0.2,
        [shape(fields, cells, dtype=F32)] * 2,
        (mean_field, fluctuations, tables),
        unread=1,
    )
    before, after = neighbours(*sides)
    conduct = jnp.concatenate([mean_field[:, None], fluctuations.transpose(1, 0, 2)], axis=1)
    conduct = jnp.concatenate([before[None], conduct, after[None]], axis=0)
    conduct = jnp.pad(conduct, ((0, 0), (0, 0), (halo, halo)))
    conduct = lax.dynamic_slice_in_dim(conduct, me * chunk, chunk + 2 * halo, 2)
    gap = jnp.zeros(conduct.shape[:-1] + (width - chunk - 2 * halo,), F32)
    conduct = jnp.concatenate([conduct[..., halo:], gap, conduct[..., :halo]], axis=-1)

    lane = jnp.arange(width)
    place = jnp.where(lane < width - halo, lane, lane - width) + halo
    row = place // NXY - REACH + me * (chunk // NXY)
    inside = (row >= 0) & (row < NXY) & ((lane < chunk + halo) | (lane >= width - halo))
    masks = jnp.stack([place % NXY < NXY - 1, place % NXY > 0, inside]).astype(F32)
    masks = jnp.broadcast_to(masks.reshape(3, tiles, 1, LANES), (3, tiles, 8, LANES))
    (weights,) = call(
        weights_kernel, "weights", 0.3, [shape(planes, fields, 6, tiles, 8, LANES, dtype=F32)], (conduct, masks)
    )

    common = (tables, weights, masks)
    plane_whole = shape(rows, width)
    share = shape(tiles, rows, LANES, dtype=F32)
    pieces = [shape(packing(planes, chunk)[-1], padded, LANES)] * count
    near_tiles = near // LANES

    def scratch(tiles, held):
        held = [VMEM((tiles, rows, LANES), F32)] * held
        return [VMEM((tiles, fields * rows, LANES), BF16), VMEM((7, tiles, rows, LANES), F32)] + held

    low, high = call(
        functools.partial(edges_kernel, count), "edges", 0.5, [plane_whole] * 2, (*edges, tables, weights), unread=2
    )
    before, after = neighbours(low, high)
    low, high, middle = call(
        outer_kernel,
        "outer",
        6,
        [share] * 3,
        (low, high, *common, *middles[1:]),
        scratch(tiles, 0),
        unread=count - 1,
    )
    low, high, middle, middle_whole = call(
        functools.partial(inner_kernel, count),
        "inner",
        3,
        [share] * 3 + [plane_whole],
        (*middles, low, high, middle, *common),
        scratch(tiles, 0),
    )
    low, high, low_near, high_near, *first = call(
        functools.partial(fix_kernel, count, chunk, True),
        "fix",
        3,
        [plane_whole] * 2 + [shape(rows, near)] * 2 + pieces,
        (before, after, low, high, middle, *common),
        scratch(tiles, 2),
    )
    before, after = neighbours(low_near, high_near)
    first = exchanged(first)
    low, high, middle = call(
        own_kernel, "own", 9, [share] * 3, (low, middle_whole, high, *common), scratch(tiles, 3)
    )
    second = call(
        functools.partial(fix_kernel, count, chunk, False),
        "last",
        3,
        pieces,
        (before, after, low, high, middle, *common),
        scratch(near_tiles, 2),
    )
    second = exchanged(second)

    def join(parts):
        (result,) = call(
            functools.partial(join_kernel, count, chunk),
            "join",
            1,
            [shape(planes, own, cells)],
            (me_array, *parts),
            [VMEM((count,) + pieces[0].shape, F32)],
            scalars=1,
        )
        return jnp.transpose(result, (1, 0, 2))

    return join(first), join(second)


def solution(mesh):
    in_specs = (P("chaos", "space", None), P("space", None), P(None, "space", None), P(), P(), P())
    out_specs = (P("chaos", "space", None), P("chaos", "space", None))
    return jax.shard_map(shards, mesh=mesh, in_specs=in_specs, out_specs=out_specs, check_vma=False)
```

```python
import functools

import jax
import jax.numpy as jnp
from jax import lax
from jax.experimental import pallas as pl
from jax.experimental.pallas import tpu as pltpu
from jax.sharding import PartitionSpec as P

NXY = 48
SCALE = 0.15
LANES = 128
REACH = 2
BLOCK = 32
VMEM = pltpu.VMEM
F32, BF16 = jnp.float32, jnp.bfloat16
NEXT_X, LAST_X, NEXT_Y, LAST_Y, NEXT_Z, LAST_Z, ALL = range(7)


def up(value, step):
    return -(-value // step) * step


def call(kernel, name, micros, out_shape, args, scratch=(), scalars=0, unread=0):
    in_specs = [pl.BlockSpec(memory_space=pltpu.SMEM)] * scalars
    in_specs += [pl.BlockSpec(memory_space=VMEM)] * (len(args) - scalars - unread)
    in_specs += [pl.BlockSpec(memory_space=pl.ANY)] * unread
    return pl.pallas_call(
        kernel,
        out_shape=out_shape,
        in_specs=in_specs,
        out_specs=[pl.BlockSpec(memory_space=VMEM)] * len(out_shape),
        scratch_shapes=scratch,
        compiler_params=pltpu.CompilerParams(vmem_limit_bytes=40 << 20),
        cost_estimate=pl.CostEstimate(flops=0, bytes_accessed=int(micros * 3.6e6), transcendentals=0),
        name=name,
    )(*args)


def cut_kernel(count, chunk, place_ref, x_ref, *refs):
    *out_refs, held = refs
    planes, own, cells = x_ref.shape
    _, padded, width = out_refs[0].shape
    halo = REACH * NXY
    me, turn = place_ref[0], place_ref[1]
    held[...] = jnp.zeros_like(held)
    lane = lax.broadcasted_iota(jnp.int32, (padded, LANES), 1)
    for plane in range(planes):
        held[0:own, :] = x_ref[plane].astype(F32)
        values = held[...]
        for target in range(count):
            turned = values if target == 0 else pltpu.roll(values, cells - target * chunk, 1)
            body = turned[:, : up(chunk + halo, LANES)]
            column = lax.broadcasted_iota(jnp.int32, body.shape, 1)
            end = chunk if target == count - 1 else chunk + halo
            body = jnp.where(column < end, body, 0.0)
            if body.shape[1] < width:
                body = jnp.concatenate([body, jnp.zeros((padded, width - body.shape[1]), F32)], axis=1)
            before = turned[:, cells - LANES :]
            if target == 0:
                before = jnp.zeros_like(before)
            last = jnp.where(lane < LANES - halo, body[:, width - LANES :], before)
            window = jnp.concatenate([body[:, : width - LANES], last], axis=1).astype(BF16)
            for step in range(count):

                @pl.when(lax.bitwise_xor(me, target) == step)
                def _():
                    out_refs[step][plane + turn * (planes - 1 - 2 * plane)] = window


def sides_kernel(place_ref, mean_ref, other_ref, _, low_ref, high_ref):
    turn = place_ref[1]
    last = mean_ref.shape[0] - 1
    for plane, turned, out_ref in ((0, last, low_ref), (last, 0, high_ref)):

        def facing(ref):
            return jnp.where(turn > 0, ref[turned : turned + 1, :], ref[plane : plane + 1, :])

        out_ref[0:1, :] = facing(mean_ref)
        for field in range(other_ref.shape[0]):
            out_ref[field + 1 : field + 2, :] = facing(other_ref.at[field])


def tables_kernel(fields, own, place_ref, triples_ref, products_ref, owners_ref, _, out_ref, held, by_column):
    rows, total = by_column.shape[1:]
    entries, factors = triples_ref.shape[1], products_ref.shape[1]
    named = owners_ref.shape[1]
    names = up(named, LANES)
    padded = up(own, 8)
    held[...] = jnp.zeros_like(held)
    held[0:3, :entries] = triples_ref[...].astype(F32)
    held[3:4, :factors] = products_ref[...]
    held[4:5, :named] = owners_ref[...].astype(F32)
    owners = held[4:5, :names].astype(jnp.int32)
    group = owners // own
    slots = lax.bitwise_xor(group, place_ref[0]) * padded + owners - group * own
    slots = jnp.broadcast_to(slots.astype(F32), (16, names)).astype(BF16)

    def placed(which):
        name = lax.broadcasted_iota(jnp.int32, (names, total), 0)
        chosen = jnp.where(name == held[which : which + 1, :].astype(jnp.int32), 1.0, 0.0).astype(BF16)
        return jnp.dot(slots, chosen, preferred_element_type=F32)[0:1].astype(jnp.int32)

    row, column = placed(0), placed(1)
    field = held[2:3, :].astype(jnp.int32)
    place = (row // BLOCK) * (fields * BLOCK) + field * BLOCK + row % BLOCK
    rest = held[3:4, :]
    here = lax.broadcasted_iota(jnp.int32, (rows, total), 0) == column
    for part in range(3):
        piece = rest.astype(BF16).astype(F32)
        rest = rest - piece
        by_column[part] = jnp.where(here, piece, 0.0).astype(BF16)
    size = fields * BLOCK

    @pl.loop(0, rows // BLOCK)
    def _(block):
        index = lax.broadcasted_iota(jnp.int32, (size, total), 0) + block * size
        chosen = jnp.where(index == place, 1.0, 0.0).astype(BF16)
        acc = jnp.zeros((size, rows), F32)
        for part in range(3):
            acc += lax.dot_general(
                chosen, by_column[part], (((1,), (1,)), ((), ())), preferred_element_type=F32
            )
        out_ref[pl.ds(pl.multiple_of(block * size, size), size), :] = acc.astype(BF16)


def weights_kernel(conduct_ref, masks_ref, out_ref):
    planes, fields, _, tiles = out_ref.shape[:4]
    width = tiles * LANES

    def mask(which):
        return jnp.concatenate([masks_ref[which, tile, 0:1, :] for tile in range(tiles)], axis=1)

    for plane in range(planes):
        own = conduct_ref[plane + 1]
        others = (
            pltpu.roll(own, width - NXY, 1),
            pltpu.roll(own, NXY, 1),
            pltpu.roll(own, width - 1, 1) * mask(0),
            pltpu.roll(own, 1, 1) * mask(1),
            conduct_ref[plane + 2],
            conduct_ref[plane],
        )
        for way, other in enumerate(others):
            face = 0.5 * (own + other)
            for field in range(fields):
                for tile in range(tiles):
                    out_ref[plane, field, way, tile] = jnp.broadcast_to(
                        face[field : field + 1, tile * LANES : (tile + 1) * LANES], (8, LANES)
                    )


def joined(parts):
    return jnp.concatenate([part.astype(F32) for part in parts], axis=0).astype(BF16)


def gather_kernel(count, *refs):
    parts, out_refs = refs[:count], refs[-refs[0].shape[0] :]
    for plane, out_ref in enumerate(out_refs):
        out_ref[...] = joined([part[plane] for part in parts])


def spread(value):
    return jnp.broadcast_to(value[None], (BLOCK // 8, 8, LANES)).reshape(BLOCK, LANES)


def mix(tables_ref, values, mixed):
    result = jnp.dot(tables_ref[...], values, preferred_element_type=F32).astype(BF16)
    for tile in range(values.shape[1] // LANES):
        mixed[tile] = result[:, tile * LANES : (tile + 1) * LANES]


def weigh(mixed, weights_ref, plane, ways, sums, tiles):
    rows = sums.shape[2]
    fields = weights_ref.shape[1]
    for tile in tiles:
        for block in range(rows // BLOCK):
            totals = [None] * len(ways)
            for field in range(fields):
                start = (block * fields + field) * BLOCK
                values = mixed[tile, start : start + BLOCK, :].astype(F32)
                for i, way in enumerate(ways):
                    term = spread(weights_ref[plane, field, way, tile]) * values
                    totals[i] = term if field == 0 else totals[i] + term
            here = slice(block * BLOCK, (block + 1) * BLOCK)
            for i, way in enumerate(ways):
                sums[way, tile, here, :] = totals[i]
            if len(ways) == 6:
                sums[ALL, tile, here, :] = functools.reduce(jnp.add, totals)


def settle(sums, masks_ref, tiles, write):
    every, rows = sums.shape[1], sums.shape[2]
    lane = lax.broadcasted_iota(jnp.int32, (BLOCK, LANES), 1)
    for block in range(rows // BLOCK):
        here = slice(block * BLOCK, (block + 1) * BLOCK)

        def ahead(way, shift):
            turned = [pltpu.roll(sums[way, tile, here, :], LANES - shift, 1) for tile in range(tiles)]
            following = turned[1:] + turned[: 1 if tiles == every else 0]
            following += turned[-1:] * (tiles - len(following))
            return [jnp.where(lane < LANES - shift, turned[t], following[t]) for t in range(tiles)]

        def behind(way, shift, ring):
            turned = [pltpu.roll(sums[way, tile, here, :], shift, 1) for tile in range(tiles)]
            before = turned[0]
            if ring:
                before = turned[-1] if tiles == every else pltpu.roll(sums[way, every - 1, here, :], shift, 1)
            previous = [before] + turned[:-1]
            return [jnp.where(lane >= shift, turned[t], previous[t]) for t in range(tiles)]

        shares = zip(
            ahead(LAST_X, NXY), behind(NEXT_X, NXY, True), ahead(LAST_Y, 1), behind(NEXT_Y, 1, False)
        )
        for tile, (a, b, c, d) in enumerate(shares):
            value = sums[ALL, tile, here, :] - a - b
            value = value - spread(masks_ref[0, tile]) * c - spread(masks_ref[1, tile]) * d
            write(tile, here, value)


def measure_plane(values, plane, tables_ref, weights_ref, mixed, sums, tiles):
    mix(tables_ref, values, mixed)
    weigh(mixed, weights_ref, plane, range(6), sums, range(tiles))
    weigh(mixed, weights_ref, plane, (NEXT_X,), sums, range(tiles, sums.shape[1]))


def outer(low, high, tables_ref, weights_ref, masks_ref, low_out, high_out, middle_out, mixed, sums, tiles):
    last = weights_ref.shape[0] - 1
    for plane, values, out_ref, way in ((0, low, low_out, NEXT_Z), (last, high, high_out, LAST_Z)):
        measure_plane(values, plane, tables_ref, weights_ref, mixed.at[min(plane, 1)], sums, tiles)

        def write(tile, here, value):
            out_ref[tile, here, :] = value
            given = sums[way, tile, here, :]
            middle_out[tile, here, :] = -given if plane == 0 else middle_out[tile, here, :] - given

        settle(sums, masks_ref, tiles, write)


def inner(
    values, low_in, high_in, middle_in, tables_ref, weights_ref, masks_ref, low_out, high_out, out, mixed, sums, tiles
):
    measure_plane(values, 1, tables_ref, weights_ref, mixed.at[0], sums, tiles)

    def write(tile, here, value):
        out[tile, here, :] = SCALE * (value + middle_in[tile, here, :])
        low_out[tile, here, :] = low_in[tile, here, :] - sums[LAST_Z, tile, here, :]
        high_out[tile, here, :] = high_in[tile, here, :] - sums[NEXT_Z, tile, here, :]

    settle(sums, masks_ref, tiles, write)


def fill(result, masks_ref, out_ref):
    tiles, rows, _ = result.shape
    for tile in range(tiles):
        inside = jnp.broadcast_to(masks_ref[2, tile][None], (rows // 8, 8, LANES)).reshape(rows, LANES)
        out_ref[:, tile * LANES : (tile + 1) * LANES] = (result[tile] * inside).astype(BF16)


def packing(planes, chunk):
    full, odd = divmod(chunk, LANES)
    beside = LANES // odd if odd else 0
    return full, odd, beside, planes * full + (-(-planes // beside) if odd else 0)


def emit(results, chunk, piece_refs):
    full, odd, beside, _ = packing(len(results), chunk)
    padded = piece_refs[0].shape[1]
    lane = lax.broadcasted_iota(jnp.int32, (padded, LANES), 1)
    for step, piece_ref in enumerate(piece_refs):
        here = slice(step * padded, (step + 1) * padded)
        for plane, result in enumerate(results):
            for tile in range(full):
                piece_ref[plane * full + tile] = result[tile, here, :].astype(BF16)
        for first in range(0, len(results) if odd else 0, beside or 1):
            packed = results[first][full, here, :]
            for place in range(1, min(beside, len(results) - first)):
                turned = pltpu.roll(results[first + place][full, here, :], place * odd, 1)
                packed = jnp.where(lane < place * odd, packed, turned)
            piece_ref[len(results) * full + first // beside] = packed.astype(BF16)


def own_kernel(tiles, first, low_ref, values_ref, high_ref, tables_ref, weights_ref, masks_ref, *refs):
    low_out, high_out, middle_out, *whole_ref, mixed, sums, low, high, middle = refs
    shared = (tables_ref, weights_ref, masks_ref)
    outer(low_ref[...], high_ref[...], *shared, low, high, middle, mixed, sums, tiles)
    inner(values_ref[...], low, high, middle, *shared, low_out, high_out, middle_out, mixed, sums, tiles)
    if first:
        fill(middle_out, masks_ref, whole_ref[0])


def fix_kernel(count, chunk, first, before_ref, after_ref, low_in, high_in, middle_in, *refs):
    tables_ref, weights_ref, masks_ref, *refs = refs
    if first:
        wholes, nears, refs = refs[:2], refs[2:4], refs[4:]
    pieces, (mixed, sums, low, high) = refs[:count], refs[count:]
    last = weights_ref.shape[0] - 1
    sides = ((before_ref, low_in, low, 0, LAST_Z), (after_ref, high_in, high, last, NEXT_Z))
    for side, (halo_ref, share_ref, result, plane, way) in enumerate(sides):
        mix(tables_ref, halo_ref[...], mixed.at[side])
        weigh(mixed.at[side], weights_ref, plane, (way,), sums, range(sums.shape[1]))
        for tile in range(sums.shape[1]):
            result[tile] = SCALE * (share_ref[tile] - sums[way, tile])
        if first:
            fill(result, masks_ref, wholes[side])
            nears[side][...] = wholes[side][:, : nears[side].shape[1]]
    emit((low, middle_in, high), chunk, pieces)


def join_kernel(count, chunk, place_ref, *refs):
    piece_refs, (out_ref, held) = refs[:count], refs[count:]
    planes, own, _ = out_ref.shape
    full, odd, beside, _ = packing(planes, chunk)
    me, turn = place_ref[0], place_ref[1]
    for step in range(count):
        held[lax.bitwise_xor(me, step)] = piece_refs[step][...].astype(F32)
    for plane in range(planes):
        parts = []
        for source in range(count):
            parts += [held[source, plane * full + tile] for tile in range(full)]
            if odd:
                tile, place = planes * full + plane // beside, plane % beside
                parts.append(held[source, tile][:, place * odd : (place + 1) * odd])
        out_ref[plane + turn * (planes - 1 - 2 * plane)] = jnp.concatenate(parts, axis=1)[:own].astype(BF16)


def shards(panels, mean_field, fluctuations, products, triples, owner_slot):
    count, slabs = lax.axis_size("chaos"), lax.axis_size("space")
    me = lax.axis_index("chaos")
    own, planes, cells = panels.shape
    assert planes == 3
    chunk, halo = cells // count, REACH * NXY
    width = up(chunk + 2 * halo, LANES)
    near = up(chunk, LANES)
    padded = up(own, 8)
    rows = count * padded
    fields = 1 + fluctuations.shape[0]
    turn = lax.axis_index("space") % 2
    place = jnp.stack([me, turn]).astype(jnp.int32)
    tiles = width // LANES

    def exchange(block, step):
        return lax.ppermute(block, "chaos", [(i, i ^ step) for i in range(count)])

    def exchanged(blocks):
        return [blocks[0]] + [exchange(blocks[step], step) for step in range(1, count)]

    def neighbours(first_plane, last_plane):
        pairs = [(i, i ^ 1) for i in range(slabs)]
        others = [(i, i - 1 if i % 2 == 0 else i + 1) for i in range(1, slabs - 1)]
        after = lax.ppermute(last_plane, "space", pairs)
        return lax.ppermute(first_plane, "space", others), after

    def shape(*dims, dtype=BF16):
        return jax.ShapeDtypeStruct(dims, dtype)

    cut = call(
        functools.partial(cut_kernel, count, chunk),
        "cut",
        1,
        [shape(planes, padded, width)] * count,
        (place, jnp.transpose(panels, (1, 0, 2))),
        [VMEM((padded, cells), F32)],
        scalars=1,
    )
    parts = exchanged(cut)

    (tables,) = call(
        functools.partial(tables_kernel, fields, own),
        "tables",
        5,
        [shape(fields * rows, rows)],
        (place, triples.T, products[None], owner_slot[None], cut[0]),
        [VMEM((8, up(products.shape[0], 2 * LANES)), F32), VMEM((3, rows, up(products.shape[0], 2 * LANES)), BF16)],
        scalars=1,
        unread=1,
    )

    sides = call(
        sides_kernel,
        "sides",
        0.2,
        [shape(fields, cells, dtype=F32)] * 2,
        (place, mean_field, fluctuations, tables),
        scalars=1,
        unread=1,
    )
    before, after = neighbours(*sides)
    conduct = jnp.concatenate([mean_field[:, None], fluctuations.transpose(1, 0, 2)], axis=1)
    conduct = jnp.where(turn > 0, conduct[::-1], conduct)
    conduct = jnp.concatenate([before[None], conduct, after[None]], axis=0)
    conduct = jnp.pad(conduct, ((0, 0), (0, 0), (halo, halo)))
    conduct = lax.dynamic_slice_in_dim(conduct, me * chunk, chunk + 2 * halo, 2)
    gap = jnp.zeros(conduct.shape[:-1] + (width - chunk - 2 * halo,), F32)
    conduct = jnp.concatenate([conduct[..., halo:], gap, conduct[..., :halo]], axis=-1)

    lane = jnp.arange(width)
    cell = jnp.where(lane < width - halo, lane, lane - width) + halo
    row = cell // NXY - REACH + me * (chunk // NXY)
    inside = (row >= 0) & (row < NXY) & ((lane < chunk + halo) | (lane >= width - halo))
    masks = jnp.stack([cell % NXY < NXY - 1, cell % NXY > 0, inside]).astype(F32)
    masks = jnp.broadcast_to(masks.reshape(3, tiles, 1, LANES), (3, tiles, 8, LANES))
    (weights,) = call(
        weights_kernel, "weights", 0.3, [shape(planes, fields, 6, tiles, 8, LANES, dtype=F32)], (conduct, masks)
    )

    common = (tables, weights, masks)
    plane_whole = shape(rows, width)
    share = shape(tiles, rows, LANES, dtype=F32)
    pieces = [shape(packing(planes, chunk)[-1], padded, LANES)] * count
    near_tiles = near // LANES

    def scratch(tiles, held):
        held = [VMEM((tiles, rows, LANES), F32)] * held
        return [VMEM((2, tiles, fields * rows, LANES), BF16), VMEM((7, tiles, rows, LANES), F32)] + held

    low, middle_whole, high = call(
        functools.partial(gather_kernel, count), "gather", 0.5, [plane_whole] * planes, (*parts, tables, weights), unread=2
    )
    before, after = neighbours(low, high)
    low, high, middle, middle_whole = call(
        functools.partial(own_kernel, tiles, True),
        "first",
        9,
        [share] * 3 + [plane_whole],
        (low, middle_whole, high, *common),
        scratch(tiles, 3),
    )
    low, high, low_near, high_near, *sent = call(
        functools.partial(fix_kernel, count, chunk, True),
        "fix",
        3,
        [plane_whole] * 2 + [shape(rows, near)] * 2 + pieces,
        (before, after, low, high, middle, *common),
        scratch(tiles, 2),
    )
    before, after = neighbours(low_near, high_near)
    sent = exchanged(sent)
    low, high, middle = call(
        functools.partial(own_kernel, near_tiles, False),
        "second",
        8,
        [share] * 3,
        (low, middle_whole, high, *common),
        scratch(tiles, 3),
    )
    second = call(
        functools.partial(fix_kernel, count, chunk, False),
        "last",
        3,
        pieces,
        (before, after, low, high, middle, *common),
        scratch(near_tiles, 2),
    )
    second = exchanged(second)

    def join(parts):
        (result,) = call(
            functools.partial(join_kernel, count, chunk),
            "join",
            1,
            [shape(planes, own, cells)],
            (place, *parts),
            [VMEM((count,) + pieces[0].shape, F32)],
            scalars=1,
        )
        return jnp.transpose(result, (1, 0, 2))

    return join(sent), join(second)


def solution(mesh):
    in_specs = (P("chaos", "space", None), P("space", None), P(None, "space", None), P(), P(), P())
    out_specs = (P("chaos", "space", None), P("chaos", "space", None))
    return jax.shard_map(shards, mesh=mesh, in_specs=in_specs, out_specs=out_specs, check_vma=False)
```

```python
import functools

import jax
import jax.numpy as jnp
from jax import lax
from jax.experimental import pallas as pl
from jax.experimental.pallas import tpu as pltpu
from jax.sharding import PartitionSpec as P

NXY = 48
SCALE = 0.15
LANES = 128
JOINT = 8
REACH = 2
BLOCK = 32
VMEM = pltpu.VMEM
F32, BF16 = jnp.float32, jnp.bfloat16
NEXT_X, LAST_X, NEXT_Y, LAST_Y, NEXT_Z, LAST_Z, ALL = range(7)


def up(value, step):
    return -(-value // step) * step


def call(kernel, name, micros, out_shape, args, scratch=(), scalars=0, unread=0):
    in_specs = [pl.BlockSpec(memory_space=pltpu.SMEM)] * scalars
    in_specs += [pl.BlockSpec(memory_space=VMEM)] * (len(args) - scalars - unread)
    in_specs += [pl.BlockSpec(memory_space=pl.ANY)] * unread
    return pl.pallas_call(
        kernel,
        out_shape=out_shape,
        in_specs=in_specs,
        out_specs=[pl.BlockSpec(memory_space=VMEM)] * len(out_shape),
        scratch_shapes=scratch,
        compiler_params=pltpu.CompilerParams(vmem_limit_bytes=40 << 20),
        cost_estimate=pl.CostEstimate(flops=int(micros * 1.1e9), bytes_accessed=int(micros * 3.6e6), transcendentals=0),
        name=name,
    )(*args)


def cut_kernel(count, chunk, place_ref, x_ref, *refs):
    out_refs, middle_refs, held = refs[:count], refs[count:-1], refs[-1]
    planes, own, cells = x_ref.shape
    _, padded, width = out_refs[0].shape
    halo = REACH * NXY
    me = place_ref[0]
    held[...] = jnp.zeros_like(held)
    lane = lax.broadcasted_iota(jnp.int32, (padded, LANES), 1)
    for plane in range(planes):
        held[0:own, :] = x_ref[plane].astype(F32)
        values = held[...]
        for target in range(count):
            turned = values if target == 0 else pltpu.roll(values, cells - target * chunk, 1)
            body = turned[:, : up(chunk + halo, LANES)]
            column = lax.broadcasted_iota(jnp.int32, body.shape, 1)
            end = chunk if target == count - 1 else chunk + halo
            body = jnp.where(column < end, body, 0.0)
            if body.shape[1] < width:
                body = jnp.concatenate([body, jnp.zeros((padded, width - body.shape[1]), F32)], axis=1)
            before = turned[:, cells - LANES :]
            if target == 0:
                before = jnp.zeros_like(before)
            last = jnp.where(lane < LANES - halo, body[:, width - LANES :], before)
            window = jnp.concatenate([body[:, : width - LANES], last], axis=1).astype(BF16)
            for step in range(count):

                @pl.when(lax.bitwise_xor(me, target) == step)
                def _():
                    if out_refs[step].shape[0] == planes:
                        out_refs[step][plane] = window
                    elif plane == 0 or plane == planes - 1:
                        out_refs[step][min(plane, 1)] = window
                    else:
                        middle_refs[step - JOINT][...] = window


def sides_kernel(place_ref, mean_ref, other_ref, _, low_ref, high_ref):
    turn = place_ref[1]
    last = mean_ref.shape[0] - 1
    for plane, turned, out_ref in ((0, last, low_ref), (last, 0, high_ref)):

        def facing(ref):
            return jnp.where(turn > 0, ref[turned : turned + 1, :], ref[plane : plane + 1, :])

        out_ref[0:1, :] = facing(mean_ref)
        for field in range(other_ref.shape[0]):
            out_ref[field + 1 : field + 2, :] = facing(other_ref.at[field])


def tables_kernel(fields, own, place_ref, triples_ref, products_ref, owners_ref, _, out_ref, held, by_column):
    rows, total = by_column.shape[1:]
    entries, factors = triples_ref.shape[1], products_ref.shape[1]
    named = owners_ref.shape[1]
    names = up(named, LANES)
    padded = up(own, 8)
    held[...] = jnp.zeros_like(held)
    held[0:3, :entries] = triples_ref[...].astype(F32)
    held[3:4, :factors] = products_ref[...]
    held[4:5, :named] = owners_ref[...].astype(F32)
    owners = held[4:5, :names].astype(jnp.int32)
    group = owners // own
    slots = lax.bitwise_xor(group, place_ref[0]) * padded + owners - group * own
    slots = jnp.broadcast_to(slots.astype(F32), (16, names)).astype(BF16)

    def placed(which):
        name = lax.broadcasted_iota(jnp.int32, (names, total), 0)
        chosen = jnp.where(name == held[which : which + 1, :].astype(jnp.int32), 1.0, 0.0).astype(BF16)
        return jnp.dot(slots, chosen, preferred_element_type=F32)[0:1].astype(jnp.int32)

    row, column = placed(0), placed(1)
    field = held[2:3, :].astype(jnp.int32)
    place = (row // BLOCK) * (fields * BLOCK) + field * BLOCK + row % BLOCK
    rest = held[3:4, :]
    here = lax.broadcasted_iota(jnp.int32, (rows, total), 0) == column
    for part in range(3):
        piece = rest.astype(BF16).astype(F32)
        rest = rest - piece
        by_column[part] = jnp.where(here, piece, 0.0).astype(BF16)
    size = fields * BLOCK

    @pl.loop(0, rows // BLOCK)
    def _(block):
        index = lax.broadcasted_iota(jnp.int32, (size, total), 0) + block * size
        chosen = jnp.where(index == place, 1.0, 0.0).astype(BF16)
        acc = jnp.zeros((size, rows), F32)
        for part in range(3):
            acc += lax.dot_general(
                chosen, by_column[part], (((1,), (1,)), ((), ())), preferred_element_type=F32
            )
        out_ref[pl.ds(pl.multiple_of(block * size, size), size), :] = acc.astype(BF16)


def weights_kernel(conduct_ref, masks_ref, out_ref):
    planes, fields, _, tiles = out_ref.shape[:4]
    width = tiles * LANES

    def mask(which):
        return jnp.concatenate([masks_ref[which, tile, 0:1, :] for tile in range(tiles)], axis=1)

    for plane in range(planes):
        own = conduct_ref[plane + 1]
        others = (
            pltpu.roll(own, width - NXY, 1),
            pltpu.roll(own, NXY, 1),
            pltpu.roll(own, width - 1, 1) * mask(0),
            pltpu.roll(own, 1, 1) * mask(1),
            conduct_ref[plane + 2],
            conduct_ref[plane],
        )
        for way, other in enumerate(others):
            face = 0.5 * (own + other)
            for field in range(fields):
                for tile in range(tiles):
                    out_ref[plane, field, way, tile] = jnp.broadcast_to(
                        face[field : field + 1, tile * LANES : (tile + 1) * LANES], (8, LANES)
                    )


def joined(parts):
    return jnp.concatenate([part.astype(F32) for part in parts], axis=0).astype(BF16)


def gather_kernel(count, place_ref, *refs):
    parts, (low_ref, high_ref) = refs[:count], refs[-2:]
    turn = place_ref[1]
    low_ref[...] = joined([part[turn * (part.shape[0] - 1)] for part in parts])
    high_ref[...] = joined([part[(1 - turn) * (part.shape[0] - 1)] for part in parts])


def spread(value):
    return jnp.broadcast_to(value[None], (BLOCK // 8, 8, LANES)).reshape(BLOCK, LANES)


def mix(tables_ref, values, mixed):
    result = jnp.dot(tables_ref[...], values, preferred_element_type=F32).astype(BF16)
    for tile in range(values.shape[1] // LANES):
        mixed[tile] = result[:, tile * LANES : (tile + 1) * LANES]


def weigh(mixed, weights_ref, plane, ways, sums, tiles):
    rows = sums.shape[2]
    fields = weights_ref.shape[1]
    for tile in tiles:
        for block in range(rows // BLOCK):
            totals = [None] * len(ways)
            for field in range(fields):
                start = (block * fields + field) * BLOCK
                values = mixed[tile, start : start + BLOCK, :].astype(F32)
                for i, way in enumerate(ways):
                    term = spread(weights_ref[plane, field, way, tile]) * values
                    totals[i] = term if field == 0 else totals[i] + term
            here = slice(block * BLOCK, (block + 1) * BLOCK)
            for i, way in enumerate(ways):
                sums[way, tile, here, :] = totals[i]
            if len(ways) == 6:
                sums[ALL, tile, here, :] = functools.reduce(jnp.add, totals)


def settle(sums, masks_ref, tiles, write):
    every, rows = sums.shape[1], sums.shape[2]
    lane = lax.broadcasted_iota(jnp.int32, (BLOCK, LANES), 1)
    for block in range(rows // BLOCK):
        here = slice(block * BLOCK, (block + 1) * BLOCK)

        def ahead(way, shift):
            turned = [pltpu.roll(sums[way, tile, here, :], LANES - shift, 1) for tile in range(tiles)]
            following = turned[1:] + turned[: 1 if tiles == every else 0]
            following += turned[-1:] * (tiles - len(following))
            return [jnp.where(lane < LANES - shift, turned[t], following[t]) for t in range(tiles)]

        def behind(way, shift, ring):
            turned = [pltpu.roll(sums[way, tile, here, :], shift, 1) for tile in range(tiles)]
            before = turned[0]
            if ring:
                before = turned[-1] if tiles == every else pltpu.roll(sums[way, every - 1, here, :], shift, 1)
            previous = [before] + turned[:-1]
            return [jnp.where(lane >= shift, turned[t], previous[t]) for t in range(tiles)]

        shares = zip(
            ahead(LAST_X, NXY), behind(NEXT_X, NXY, True), ahead(LAST_Y, 1), behind(NEXT_Y, 1, False)
        )
        for tile, (a, b, c, d) in enumerate(shares):
            value = sums[ALL, tile, here, :] - a - b
            value = value - spread(masks_ref[0, tile]) * c - spread(masks_ref[1, tile]) * d
            write(tile, here, value)


def measure_plane(values, plane, tables_ref, weights_ref, mixed, sums, tiles):
    mix(tables_ref, values, mixed)
    weigh(mixed, weights_ref, plane, range(6), sums, range(tiles))
    weigh(mixed, weights_ref, plane, (NEXT_X,), sums, range(tiles, sums.shape[1]))


def outer(low, high, tables_ref, weights_ref, masks_ref, low_out, high_out, middle_out, mixed, sums, tiles):
    last = weights_ref.shape[0] - 1
    for plane, values, out_ref, way in ((0, low, low_out, NEXT_Z), (last, high, high_out, LAST_Z)):
        measure_plane(values, plane, tables_ref, weights_ref, mixed.at[min(plane, 1)], sums, tiles)

        def write(tile, here, value):
            out_ref[tile, here, :] = value
            given = sums[way, tile, here, :]
            middle_out[tile, here, :] = -given if plane == 0 else middle_out[tile, here, :] - given

        settle(sums, masks_ref, tiles, write)


def inner(
    values, low_in, high_in, middle_in, tables_ref, weights_ref, masks_ref, low_out, high_out, out, mixed, sums, tiles
):
    measure_plane(values, 1, tables_ref, weights_ref, mixed.at[0], sums, tiles)

    def write(tile, here, value):
        out[tile, here, :] = SCALE * (value + middle_in[tile, here, :])
        low_out[tile, here, :] = low_in[tile, here, :] - sums[LAST_Z, tile, here, :]
        high_out[tile, here, :] = high_in[tile, here, :] - sums[NEXT_Z, tile, here, :]

    settle(sums, masks_ref, tiles, write)


def fill(result, masks_ref, out_ref):
    tiles, rows, _ = result.shape
    for tile in range(tiles):
        inside = jnp.broadcast_to(masks_ref[2, tile][None], (rows // 8, 8, LANES)).reshape(rows, LANES)
        out_ref[:, tile * LANES : (tile + 1) * LANES] = (result[tile] * inside).astype(BF16)


def packing(planes, chunk):
    full, odd = divmod(chunk, LANES)
    beside = LANES // odd if odd else 0
    return full, odd, beside, planes * full + (-(-planes // beside) if odd else 0)


def emit(results, chunk, piece_refs):
    full, odd, beside, _ = packing(len(results), chunk)
    padded = piece_refs[0].shape[1]
    lane = lax.broadcasted_iota(jnp.int32, (padded, LANES), 1)
    for step, piece_ref in enumerate(piece_refs):
        here = slice(step * padded, (step + 1) * padded)
        for plane, result in enumerate(results):
            for tile in range(full):
                piece_ref[plane * full + tile] = result[tile, here, :].astype(BF16)
        for first in range(0, len(results) if odd else 0, beside or 1):
            packed = results[first][full, here, :]
            for place in range(1, min(beside, len(results) - first)):
                turned = pltpu.roll(results[first + place][full, here, :], place * odd, 1)
                packed = jnp.where(lane < place * odd, packed, turned)
            piece_ref[len(results) * full + first // beside] = packed.astype(BF16)


def outer_kernel(low_ref, high_ref, tables_ref, weights_ref, masks_ref, *outs):
    outer(low_ref[...], high_ref[...], tables_ref, weights_ref, masks_ref, *outs, weights_ref.shape[3])


def inner_kernel(count, *refs):
    parts = [part[1] if len(part.shape) == 3 else part[...] for part in refs[:count]]
    low_in, high_in, middle_in, tables_ref, weights_ref, masks_ref, *outs = refs[count:]
    low_out, high_out, middle_out, whole_ref, mixed, sums = outs
    shared = (tables_ref, weights_ref, masks_ref, low_out, high_out, middle_out, mixed, sums)
    inner(joined(parts), low_in, high_in, middle_in, *shared, weights_ref.shape[3])
    fill(middle_out, masks_ref, whole_ref)


def own_kernel(tiles, low_ref, values_ref, high_ref, tables_ref, weights_ref, masks_ref, *refs):
    low_out, high_out, middle_out, mixed, sums, low, high, middle = refs
    shared = (tables_ref, weights_ref, masks_ref)
    outer(low_ref[...], high_ref[...], *shared, low, high, middle, mixed, sums, tiles)
    inner(values_ref[...], low, high, middle, *shared, low_out, high_out, middle_out, mixed, sums, tiles)


def fix_kernel(count, chunk, first, before_ref, after_ref, low_in, high_in, middle_in, *refs):
    tables_ref, weights_ref, masks_ref, *refs = refs
    if first:
        wholes, nears, refs = refs[:2], refs[2:4], refs[4:]
    pieces, (mixed, sums, low, high) = refs[:count], refs[count:]
    last = weights_ref.shape[0] - 1
    sides = ((before_ref, low_in, low, 0, LAST_Z), (after_ref, high_in, high, last, NEXT_Z))
    for side, (halo_ref, share_ref, result, plane, way) in enumerate(sides):
        mix(tables_ref, halo_ref[...], mixed.at[side])
        weigh(mixed.at[side], weights_ref, plane, (way,), sums, range(sums.shape[1]))
        for tile in range(sums.shape[1]):
            result[tile] = SCALE * (share_ref[tile] - sums[way, tile])
        if first:
            fill(result, masks_ref, wholes[side])
            nears[side][...] = wholes[side][:, : nears[side].shape[1]]
    emit((low, middle_in, high), chunk, pieces)


def join_kernel(count, chunk, place_ref, *refs):
    piece_refs, (out_ref, held) = refs[:count], refs[count:]
    planes, own, _ = out_ref.shape
    full, odd, beside, _ = packing(planes, chunk)
    me, turn = place_ref[0], place_ref[1]
    for step in range(count):
        held[lax.bitwise_xor(me, step)] = piece_refs[step][...].astype(F32)
    for plane in range(planes):
        parts = []
        for source in range(count):
            parts += [held[source, plane * full + tile] for tile in range(full)]
            if odd:
                tile, spot = planes * full + plane // beside, plane % beside
                parts.append(held[source, tile][:, spot * odd : (spot + 1) * odd])
        line = jnp.concatenate(parts, axis=1)[:own].astype(BF16)
        for turned in range(2):

            @pl.when(turn == turned)
            def _():
                out_ref[planes - 1 - plane if turned else plane] = line


def shards(panels, mean_field, fluctuations, products, triples, owner_slot):
    count, slabs = lax.axis_size("chaos"), lax.axis_size("space")
    me = lax.axis_index("chaos")
    own, planes, cells = panels.shape
    assert planes == 3
    chunk, halo = cells // count, REACH * NXY
    width = up(chunk + 2 * halo, LANES)
    near = up(chunk, LANES)
    padded = up(own, 8)
    rows = count * padded
    fields = 1 + fluctuations.shape[0]
    turn = lax.axis_index("space") % 2
    place = jnp.stack([me, turn]).astype(jnp.int32)
    tiles = width // LANES

    def exchange(block, step):
        return lax.ppermute(block, "chaos", [(i, i ^ step) for i in range(count)])

    def exchanged(blocks):
        arrived = {step: exchange(blocks[step], step) for step in range(count - 1, 0, -1)}
        return [blocks[0]] + [arrived[step] for step in range(1, count)]

    def neighbours(first_plane, last_plane):
        pairs = [(i, i ^ 1) for i in range(slabs)]
        others = [(i, i - 1 if i % 2 == 0 else i + 1) for i in range(1, slabs - 1)]
        after = lax.ppermute(last_plane, "space", pairs)
        return lax.ppermute(first_plane, "space", others), after

    def shape(*dims, dtype=BF16):
        return jax.ShapeDtypeStruct(dims, dtype)

    joint = min(JOINT, count)
    cut = call(
        functools.partial(cut_kernel, count, chunk),
        "cut",
        1,
        [shape(planes if step < joint else 2, padded, width) for step in range(count)]
        + [shape(padded, width)] * (count - joint),
        (place, jnp.transpose(panels, (1, 0, 2))),
        [VMEM((padded, cells), F32)],
        scalars=1,
    )
    parts = exchanged(cut[:count])
    middles = parts[:joint] + [exchange(cut[count + step - joint], step) for step in range(joint, count)]

    (tables,) = call(
        functools.partial(tables_kernel, fields, own),
        "tables",
        5,
        [shape(fields * rows, rows)],
        (place, triples.T, products[None], owner_slot[None], cut[0]),
        [VMEM((8, up(products.shape[0], 2 * LANES)), F32), VMEM((3, rows, up(products.shape[0], 2 * LANES)), BF16)],
        scalars=1,
        unread=1,
    )

    sides = call(
        sides_kernel,
        "sides",
        0.2,
        [shape(fields, cells, dtype=F32)] * 2,
        (place, mean_field, fluctuations, tables),
        scalars=1,
        unread=1,
    )
    before, after = neighbours(*sides)
    conduct = jnp.concatenate([mean_field[:, None], fluctuations.transpose(1, 0, 2)], axis=1)
    conduct = jnp.where(turn > 0, conduct[::-1], conduct)
    conduct = jnp.concatenate([before[None], conduct, after[None]], axis=0)
    conduct = jnp.pad(conduct, ((0, 0), (0, 0), (halo, halo)))
    conduct = lax.dynamic_slice_in_dim(conduct, me * chunk, chunk + 2 * halo, 2)
    gap = jnp.zeros(conduct.shape[:-1] + (width - chunk - 2 * halo,), F32)
    conduct = jnp.concatenate([conduct[..., halo:], gap, conduct[..., :halo]], axis=-1)

    lane = jnp.arange(width)
    cell = jnp.where(lane < width - halo, lane, lane - width) + halo
    row = cell // NXY - REACH + me * (chunk // NXY)
    inside = (row >= 0) & (row < NXY) & ((lane < chunk + halo) | (lane >= width - halo))
    masks = jnp.stack([cell % NXY < NXY - 1, cell % NXY > 0, inside]).astype(F32)
    masks = jnp.broadcast_to(masks.reshape(3, tiles, 1, LANES), (3, tiles, 8, LANES))
    (weights,) = call(
        weights_kernel, "weights", 0.3, [shape(planes, fields, 6, tiles, 8, LANES, dtype=F32)], (conduct, masks)
    )

    common = (tables, weights, masks)
    plane_whole = shape(rows, width)
    share = shape(tiles, rows, LANES, dtype=F32)
    pieces = [shape(packing(planes, chunk)[-1], padded, LANES)] * count
    near_tiles = near // LANES

    def scratch(tiles, held):
        held = [VMEM((tiles, rows, LANES), F32)] * held
        return [VMEM((2, tiles, fields * rows, LANES), BF16), VMEM((7, tiles, rows, LANES), F32)] + held

    low, high = call(
        functools.partial(gather_kernel, count),
        "gather",
        0.5,
        [plane_whole] * 2,
        (place, *parts, tables, weights),
        scalars=1,
        unread=2,
    )
    before, after = neighbours(low, high)
    low, high, middle = call(outer_kernel, "outer", 6, [share] * 3, (low, high, *common), scratch(tiles, 0))
    low, high, middle, middle_whole = call(
        functools.partial(inner_kernel, count),
        "inner",
        3,
        [share] * 3 + [plane_whole],
        (*middles, low, high, middle, *common),
        scratch(tiles, 0),
    )
    low, high, low_near, high_near, *sent = call(
        functools.partial(fix_kernel, count, chunk, True),
        "fix",
        3,
        [plane_whole] * 2 + [shape(rows, near)] * 2 + pieces,
        (before, after, low, high, middle, *common),
        scratch(tiles, 2),
    )
    sent = exchanged(sent)
    before, after = neighbours(low_near, high_near)
    low, high, middle = call(
        functools.partial(own_kernel, near_tiles),
        "second",
        8,
        [share] * 3,
        (low, middle_whole, high, *common),
        scratch(tiles, 3),
    )
    second = call(
        functools.partial(fix_kernel, count, chunk, False),
        "last",
        3,
        pieces,
        (before, after, low, high, middle, *common),
        scratch(near_tiles, 2),
    )
    second = exchanged(second)

    def join(parts):
        (result,) = call(
            functools.partial(join_kernel, count, chunk),
            "join",
            1,
            [shape(planes, own, cells)],
            (place, *parts),
            [VMEM((count,) + parts[0].shape, F32)],
            scalars=1,
        )
        return jnp.transpose(result, (1, 0, 2))

    return join(sent), join(second)


def solution(mesh):
    in_specs = (P("chaos", "space", None), P("space", None), P(None, "space", None), P(), P(), P())
    out_specs = (P("chaos", "space", None), P("chaos", "space", None))
    return jax.shard_map(shards, mesh=mesh, in_specs=in_specs, out_specs=out_specs, check_vma=False)
```

```python
import functools

import jax
import jax.numpy as jnp
from jax import lax
from jax.experimental import pallas as pl
from jax.experimental.pallas import tpu as pltpu
from jax.sharding import PartitionSpec as P

NXY = 48
SCALE = 0.15
LANES = 128
JOINT = 2
EXTRA = 32
REACH = 2
BLOCK = 32
VMEM = pltpu.VMEM
F32, BF16 = jnp.float32, jnp.bfloat16
NEXT_X, LAST_X, NEXT_Y, LAST_Y, NEXT_Z, LAST_Z, ALL = range(7)


def up(value, step):
    return -(-value // step) * step


def call(kernel, name, micros, out_shape, args, scratch=(), scalars=0, unread=0):
    in_specs = [pl.BlockSpec(memory_space=pltpu.SMEM)] * scalars
    in_specs += [pl.BlockSpec(memory_space=VMEM)] * (len(args) - scalars - unread)
    in_specs += [pl.BlockSpec(memory_space=pl.ANY)] * unread
    return pl.pallas_call(
        kernel,
        out_shape=out_shape,
        in_specs=in_specs,
        out_specs=[pl.BlockSpec(memory_space=VMEM)] * len(out_shape),
        scratch_shapes=scratch,
        compiler_params=pltpu.CompilerParams(vmem_limit_bytes=40 << 20),
        cost_estimate=pl.CostEstimate(flops=int(micros * 1.1e9), bytes_accessed=int(micros * 3.6e6), transcendentals=0),
        name=name,
    )(*args)


def cut_kernel(count, chunk, me_ref, x_ref, *refs):
    out_refs, middle_refs, held = refs[:count], refs[count:-1], refs[-1]
    planes, own, cells = x_ref.shape
    _, padded, width = out_refs[0].shape
    halo = REACH * NXY
    me = me_ref[0]
    held[...] = jnp.zeros_like(held)
    lane = lax.broadcasted_iota(jnp.int32, (padded, LANES), 1)
    for plane in range(planes):
        held[0:own, :] = x_ref[plane].astype(F32)
        values = held[...]
        for target in range(count):
            turned = values if target == 0 else pltpu.roll(values, cells - target * chunk, 1)
            body = turned[:, : up(chunk + halo, LANES)]
            column = lax.broadcasted_iota(jnp.int32, body.shape, 1)
            end = chunk if target == count - 1 else chunk + halo
            body = jnp.where(column < end, body, 0.0)
            if body.shape[1] < width:
                body = jnp.concatenate([body, jnp.zeros((padded, width - body.shape[1]), F32)], axis=1)
            before = turned[:, cells - LANES :]
            if target == 0:
                before = jnp.zeros_like(before)
            last = jnp.where(lane < LANES - halo, body[:, width - LANES :], before)
            window = jnp.concatenate([body[:, : width - LANES], last], axis=1).astype(BF16)
            for step in range(count):

                @pl.when(lax.bitwise_xor(me, target) == step)
                def _():
                    if out_refs[step].shape[0] == planes:
                        out_refs[step][plane] = window
                    elif plane == 0 or plane == planes - 1:
                        out_refs[step][min(plane, 1)] = window
                    else:
                        middle_refs[step - JOINT][...] = window


def tables_kernel(fields, own, me_ref, triples_ref, products_ref, owners_ref, _, out_ref, held, by_column):
    rows, total = by_column.shape[1:]
    entries, factors = triples_ref.shape[1], products_ref.shape[1]
    named = owners_ref.shape[1]
    names = up(named, LANES)
    padded = up(own, 8)
    held[...] = jnp.zeros_like(held)
    held[0:3, :entries] = triples_ref[...].astype(F32)
    held[3:4, :factors] = products_ref[...]
    held[4:5, :named] = owners_ref[...].astype(F32)
    owners = held[4:5, :names].astype(jnp.int32)
    group = owners // own
    slots = lax.bitwise_xor(group, me_ref[0]) * padded + owners - group * own
    slots = jnp.broadcast_to(slots.astype(F32), (16, names)).astype(BF16)

    def placed(which):
        name = lax.broadcasted_iota(jnp.int32, (names, total), 0)
        chosen = jnp.where(name == held[which : which + 1, :].astype(jnp.int32), 1.0, 0.0).astype(BF16)
        return jnp.dot(slots, chosen, preferred_element_type=F32)[0:1].astype(jnp.int32)

    row, column = placed(0), placed(1)
    field = held[2:3, :].astype(jnp.int32)
    place = (row // BLOCK) * (fields * BLOCK) + field * BLOCK + row % BLOCK
    rest = held[3:4, :]
    here = lax.broadcasted_iota(jnp.int32, (rows, total), 0) == column
    for part in range(3):
        piece = rest.astype(BF16).astype(F32)
        rest = rest - piece
        by_column[part] = jnp.where(here, piece, 0.0).astype(BF16)
    size = fields * BLOCK

    @pl.loop(0, rows // BLOCK)
    def _(block):
        index = lax.broadcasted_iota(jnp.int32, (size, total), 0) + block * size
        chosen = jnp.where(index == place, 1.0, 0.0).astype(BF16)
        acc = jnp.zeros((size, rows), F32)
        for part in range(3):
            acc += lax.dot_general(
                chosen, by_column[part], (((1,), (1,)), ((), ())), preferred_element_type=F32
            )
        out_ref[pl.ds(pl.multiple_of(block * size, size), size), :] = acc.astype(BF16)


def spread_face(face, out_ref):
    for field in range(out_ref.shape[0]):
        for tile in range(out_ref.shape[1]):
            out_ref[field, tile] = jnp.broadcast_to(
                face[field : field + 1, tile * LANES : (tile + 1) * LANES], (8, LANES)
            )


def weights_kernel(conduct_ref, masks_ref, *refs):
    out_ref = refs[-1 - (len(refs) - 2) // 2]
    passed, passed_out = refs[: (len(refs) - 2) // 2], refs[len(refs) - (len(refs) - 2) // 2 :]
    for in_ref, to_ref in zip(passed, passed_out):
        to_ref[...] = in_ref[...]
    planes, _, _, tiles = out_ref.shape[:4]
    width = tiles * LANES

    def mask(which):
        return jnp.concatenate([masks_ref[which, tile, 0:1, :] for tile in range(tiles)], axis=1)

    for plane in range(planes):
        own = conduct_ref[plane]
        others = (
            pltpu.roll(own, width - NXY, 1),
            pltpu.roll(own, NXY, 1),
            pltpu.roll(own, width - 1, 1) * mask(0),
            pltpu.roll(own, 1, 1) * mask(1),
            conduct_ref[min(plane + 1, planes - 1)],
            conduct_ref[max(plane - 1, 0)],
        )
        for way, other in enumerate(others):
            spread_face(0.5 * (own + other), out_ref.at[plane, way])


def joined(parts):
    return jnp.concatenate([part.astype(F32) for part in parts], axis=0).astype(BF16)


def gather_kernel(count, turn_ref, conduct_ref, *refs):
    parts, out_refs = refs[:count], refs[-2:]
    for side, out_ref in enumerate(out_refs):
        place = lax.bitwise_xor(turn_ref[0], side)
        rest = conduct_ref[side * (conduct_ref.shape[0] - 1)]
        pieces = []
        for _ in range(3):
            pieces.append(rest.astype(BF16))
            rest = rest - pieces[-1].astype(F32)
        pieces.append(jnp.zeros_like(pieces[0]))
        out_ref[...] = joined([part[place * (part.shape[0] - 1)] for part in parts] + pieces)


def spread(value):
    return jnp.broadcast_to(value[None], (BLOCK // 8, 8, LANES)).reshape(BLOCK, LANES)


def mix(tables_ref, values, mixed):
    result = jnp.dot(tables_ref[...], values, preferred_element_type=F32).astype(BF16)
    for tile in range(values.shape[1] // LANES):
        mixed[tile] = result[:, tile * LANES : (tile + 1) * LANES]


def weigh(values_of, face_of, ways, fields, sums, tiles):
    rows = sums.shape[2]
    for tile in tiles:
        for block in range(rows // BLOCK):
            totals = [None] * len(ways)
            for field in range(fields):
                start = (block * fields + field) * BLOCK
                values = values_of(tile, slice(start, start + BLOCK))
                for i, way in enumerate(ways):
                    term = spread(face_of(way, field, tile)) * values
                    totals[i] = term if field == 0 else totals[i] + term
            here = slice(block * BLOCK, (block + 1) * BLOCK)
            for i, way in enumerate(ways):
                sums[way, tile, here, :] = totals[i]
            if len(ways) > 1:
                sums[ALL, tile, here, :] = functools.reduce(jnp.add, totals)


def settle(sums, masks_ref, tiles, write):
    every, rows = sums.shape[1], sums.shape[2]
    lane = lax.broadcasted_iota(jnp.int32, (BLOCK, LANES), 1)
    for block in range(rows // BLOCK):
        here = slice(block * BLOCK, (block + 1) * BLOCK)

        def ahead(way, shift):
            turned = [pltpu.roll(sums[way, tile, here, :], LANES - shift, 1) for tile in range(tiles)]
            following = turned[1:] + turned[: 1 if tiles == every else 0]
            following += turned[-1:] * (tiles - len(following))
            return [jnp.where(lane < LANES - shift, turned[t], following[t]) for t in range(tiles)]

        def behind(way, shift, ring):
            turned = [pltpu.roll(sums[way, tile, here, :], shift, 1) for tile in range(tiles)]
            before = turned[0]
            if ring:
                before = turned[-1] if tiles == every else pltpu.roll(sums[way, every - 1, here, :], shift, 1)
            previous = [before] + turned[:-1]
            return [jnp.where(lane >= shift, turned[t], previous[t]) for t in range(tiles)]

        shares = zip(
            ahead(LAST_X, NXY), behind(NEXT_X, NXY, True), ahead(LAST_Y, 1), behind(NEXT_Y, 1, False)
        )
        for tile, (a, b, c, d) in enumerate(shares):
            value = sums[ALL, tile, here, :] - a - b
            value = value - spread(masks_ref[0, tile]) * c - spread(masks_ref[1, tile]) * d
            write(tile, here, value)


def measure_plane(values, plane, tables_ref, weights_ref, faces_ref, mixed, sums, tiles):
    planes, _, fields = weights_ref.shape[:3]
    outside = {0: LAST_Z, planes - 1: NEXT_Z}.get(plane)
    ways = [way for way in range(6) if way != outside or faces_ref is not None]

    def values_of(tile, rows):
        return mixed[tile, rows, :].astype(F32)

    def face_of(way, field, tile):
        if way == outside:
            return faces_ref[min(plane, 1), field, tile]
        return weights_ref[plane, way, field, tile]

    mix(tables_ref, values, mixed)
    weigh(values_of, face_of, ways, fields, sums, range(tiles))
    weigh(values_of, face_of, (NEXT_X,), fields, sums, range(tiles, sums.shape[1]))


def outer(low, high, tables_ref, weights_ref, masks_ref, faces_ref, low_out, high_out, middle_out, mixed, sums, tiles):
    last = weights_ref.shape[0] - 1
    for plane, values, out_ref, way in ((0, low, low_out, NEXT_Z), (last, high, high_out, LAST_Z)):
        measure_plane(values, plane, tables_ref, weights_ref, faces_ref, mixed.at[min(plane, 1)], sums, tiles)

        def write(tile, here, value):
            out_ref[tile, here, :] = value
            given = sums[way, tile, here, :]
            middle_out[tile, here, :] = -given if plane == 0 else middle_out[tile, here, :] - given

        settle(sums, masks_ref, tiles, write)


def inner(
    values, low_in, high_in, middle_in, tables_ref, weights_ref, masks_ref, low_out, high_out, out, mixed, sums, tiles
):
    measure_plane(values, 1, tables_ref, weights_ref, None, mixed.at[0], sums, tiles)

    def write(tile, here, value):
        out[tile, here, :] = SCALE * (value + middle_in[tile, here, :])
        low_out[tile, here, :] = low_in[tile, here, :] - sums[LAST_Z, tile, here, :]
        high_out[tile, here, :] = high_in[tile, here, :] - sums[NEXT_Z, tile, here, :]

    settle(sums, masks_ref, tiles, write)


def fill(result, masks_ref, out_ref):
    tiles, rows, _ = result.shape
    for tile in range(tiles):
        inside = jnp.broadcast_to(masks_ref[2, tile][None], (rows // 8, 8, LANES)).reshape(rows, LANES)
        out_ref[:, tile * LANES : (tile + 1) * LANES] = (result[tile] * inside).astype(BF16)


def packing(planes, chunk):
    full, odd = divmod(chunk, LANES)
    beside = LANES // odd if odd else 0
    return full, odd, beside, planes * full + (-(-planes // beside) if odd else 0)


def emit(results, chunk, piece_refs):
    full, odd, beside, _ = packing(len(results), chunk)
    padded = piece_refs[0].shape[1]
    lane = lax.broadcasted_iota(jnp.int32, (padded, LANES), 1)
    for step, piece_ref in enumerate(piece_refs):
        here = slice(step * padded, (step + 1) * padded)
        for plane, result in enumerate(results):
            for tile in range(full):
                piece_ref[plane * full + tile] = result[tile, here, :].astype(BF16)
        for first in range(0, len(results) if odd else 0, beside or 1):
            packed = results[first][full, here, :]
            for place in range(1, min(beside, len(results) - first)):
                turned = pltpu.roll(results[first + place][full, here, :], place * odd, 1)
                packed = jnp.where(lane < place * odd, packed, turned)
            piece_ref[len(results) * full + first // beside] = packed.astype(BF16)


def outer_kernel(low_ref, high_ref, tables_ref, weights_ref, masks_ref, *outs):
    rows = tables_ref.shape[1]
    shared = (tables_ref, weights_ref, masks_ref, None)
    outer(low_ref[0:rows, :], high_ref[0:rows, :], *shared, *outs, weights_ref.shape[3])


def inner_kernel(count, *refs):
    parts = [part[1] if len(part.shape) == 3 else part[...] for part in refs[:count]]
    low_in, high_in, middle_in, tables_ref, weights_ref, masks_ref, *outs = refs[count:]
    low_out, high_out, middle_out, whole_ref, mixed, sums = outs
    shared = (tables_ref, weights_ref, masks_ref, low_out, high_out, middle_out, mixed, sums)
    inner(joined(parts), low_in, high_in, middle_in, *shared, weights_ref.shape[3])
    fill(middle_out, masks_ref, whole_ref)


def own_kernel(tiles, low_ref, values_ref, high_ref, tables_ref, weights_ref, masks_ref, faces_ref, *refs):
    low_out, high_out, middle_out, mixed, sums, low, high, middle = refs
    shared = (tables_ref, weights_ref, masks_ref)
    outer(low_ref[...], high_ref[...], *shared, faces_ref, low, high, middle, mixed, sums, tiles)
    inner(values_ref[...], low, high, middle, *shared, low_out, high_out, middle_out, mixed, sums, tiles)


def first_fix_kernel(count, chunk, turn_ref, *refs):
    halo_refs, own_refs, share_refs, (middle_in, tables_ref, masks_ref), refs = (
        refs[0:2], refs[2:4], refs[4:6], refs[6:9], refs[9:]
    )
    wholes, nears, faces_ref, pieces, (mixed, sums, ends) = refs[:2], refs[2:4], refs[4], refs[5:-3], refs[-3:]
    rows, (_, fields, tiles, _, _) = tables_ref.shape[1], faces_ref.shape
    for side in range(2):
        coefficient = 0.0
        for ref in (own_refs[side], halo_refs[side]):
            parts = ref[rows : rows + EXTRA, :].astype(F32)
            coefficient = coefficient + ((parts[16:24] + parts[8:16]) + parts[0:8])
        spread_face(0.5 * coefficient, faces_ref.at[side])
        for index, ref in enumerate((own_refs[side], halo_refs[side])):
            mix(tables_ref, ref[0:rows, :], mixed.at[index])

        def values_of(tile, here):
            return mixed[0, tile, here, :].astype(F32) - mixed[1, tile, here, :].astype(F32)

        def face_of(way, field, tile):
            return faces_ref[side, field, tile]

        weigh(values_of, face_of, (0,), fields, sums, range(tiles))
        result = ends.at[lax.bitwise_xor(turn_ref[0], side)]
        for tile in range(tiles):
            result[tile] = SCALE * (share_refs[side][tile] + sums[0, tile])
        fill(result, masks_ref, wholes[side])
        nears[side][...] = wholes[side][:, : nears[side].shape[1]]
    emit((ends.at[0], middle_in, ends.at[1]), chunk, pieces)


def last_fix_kernel(count, chunk, turn_ref, *refs):
    halo_refs, share_refs, (middle_in, tables_ref, faces_ref), refs = refs[0:2], refs[2:4], refs[4:7], refs[7:]
    pieces, (mixed, sums, ends) = refs[:-3], refs[-3:]
    fields, tiles = faces_ref.shape[1], sums.shape[1]
    for side in range(2):
        mix(tables_ref, halo_refs[side][...], mixed.at[side])

        def values_of(tile, here):
            return mixed[side, tile, here, :].astype(F32)

        def face_of(way, field, tile):
            return faces_ref[side, field, tile]

        weigh(values_of, face_of, (0,), fields, sums, range(tiles))
        result = ends.at[lax.bitwise_xor(turn_ref[0], side)]
        for tile in range(tiles):
            result[tile] = SCALE * (share_refs[side][tile] - sums[0, tile])
    emit((ends.at[0], middle_in, ends.at[1]), chunk, pieces)


def join_kernel(count, chunk, me_ref, *refs):
    piece_refs, (out_ref, held) = refs[:count], refs[count:]
    planes, own, _ = out_ref.shape
    full, odd, beside, _ = packing(planes, chunk)
    me = me_ref[0]
    for step in range(count):
        held[lax.bitwise_xor(me, step)] = piece_refs[step][...].astype(F32)
    for plane in range(planes):
        parts = []
        for source in range(count):
            parts += [held[source, plane * full + tile] for tile in range(full)]
            if odd:
                tile, spot = planes * full + plane // beside, plane % beside
                parts.append(held[source, tile][:, spot * odd : (spot + 1) * odd])
        out_ref[plane] = jnp.concatenate(parts, axis=1)[:own].astype(BF16)


def shards(panels, mean_field, fluctuations, products, triples, owner_slot):
    count, slabs = lax.axis_size("chaos"), lax.axis_size("space")
    me = lax.axis_index("chaos")
    own, planes, cells = panels.shape
    assert planes == 3
    chunk, halo = cells // count, REACH * NXY
    width = up(chunk + 2 * halo, LANES)
    near = up(chunk, LANES)
    padded = up(own, 8)
    rows = count * padded
    fields = 1 + fluctuations.shape[0]
    turn = lax.bitwise_and(lax.axis_index("space"), 1)
    me_alone, turn_alone = me.astype(jnp.int32).reshape(1), turn.astype(jnp.int32).reshape(1)
    tiles = width // LANES

    def exchange(block, step):
        return lax.ppermute(block, "chaos", [(i, i ^ step) for i in range(count)])

    def exchanged(blocks):
        arrived = {step: exchange(blocks[step], step) for step in range(count - 1, 0, -1)}
        return [blocks[0]] + [arrived[step] for step in range(1, count)]

    def neighbours(first_plane, last_plane):
        pairs = [(i, i ^ 1) for i in range(slabs)]
        others = [(i, i - 1 if i % 2 == 0 else i + 1) for i in range(1, slabs - 1)]
        after = lax.ppermute(last_plane, "space", pairs)
        return lax.ppermute(first_plane, "space", others), after

    def shape(*dims, dtype=BF16):
        return jax.ShapeDtypeStruct(dims, dtype)

    joint = min(JOINT, count)
    cut = call(
        functools.partial(cut_kernel, count, chunk),
        "cut",
        1,
        [shape(planes if step < joint else 2, padded, width) for step in range(count)]
        + [shape(padded, width)] * (count - joint),
        (me_alone, jnp.transpose(panels, (1, 0, 2))),
        [VMEM((padded, cells), F32)],
        scalars=1,
    )
    parts = exchanged(cut[:count])

    (tables,) = call(
        functools.partial(tables_kernel, fields, own),
        "tables",
        5,
        [shape(fields * rows, rows)],
        (me_alone, triples.T, products[None], owner_slot[None], cut[0]),
        [VMEM((8, up(products.shape[0], 2 * LANES)), F32), VMEM((3, rows, up(products.shape[0], 2 * LANES)), BF16)],
        scalars=1,
        unread=1,
    )

    conduct = jnp.concatenate([mean_field[:, None], fluctuations.transpose(1, 0, 2)], axis=1)
    conduct = jnp.where(turn > 0, conduct[::-1], conduct)
    conduct = jnp.pad(conduct, ((0, 0), (0, up(fields, 8) - fields), (halo, halo)))
    conduct = lax.dynamic_slice_in_dim(conduct, me * chunk, chunk + 2 * halo, 2)
    gap = jnp.zeros(conduct.shape[:-1] + (width - chunk - 2 * halo,), F32)
    conduct = jnp.concatenate([conduct[..., halo:], gap, conduct[..., :halo]], axis=-1)

    lane = jnp.arange(width)
    cell = jnp.where(lane < width - halo, lane, lane - width) + halo
    row = cell // NXY - REACH + me * (chunk // NXY)
    inside = (row >= 0) & (row < NXY) & ((lane < chunk + halo) | (lane >= width - halo))
    masks = jnp.stack([cell % NXY < NXY - 1, cell % NXY > 0, inside]).astype(F32)
    masks = jnp.broadcast_to(masks.reshape(3, tiles, 1, LANES), (3, tiles, 8, LANES))
    weights, *middles = call(
        weights_kernel,
        "weights",
        0.5,
        [shape(planes, 6, fields, tiles, 8, LANES, dtype=F32)] + [shape(padded, width)] * (count - joint),
        (conduct, masks, *cut[count:], tables),
        unread=1,
    )
    middles = parts[:joint] + [exchange(middles[step - joint], step) for step in range(joint, count)]

    common = (tables, weights, masks)
    plane_whole = shape(rows, width)
    share = shape(tiles, rows, LANES, dtype=F32)
    pieces = [shape(packing(planes, chunk)[-1], padded, LANES)] * count
    near_tiles = near // LANES

    def scratch(tiles, kinds=7):
        return [VMEM((2, tiles, fields * rows, LANES), BF16), VMEM((kinds, tiles, rows, LANES), F32)]

    low, high = call(
        functools.partial(gather_kernel, count),
        "gather",
        0.5,
        [shape(rows + EXTRA, width)] * 2,
        (turn_alone, conduct, *parts, tables, weights),
        scalars=1,
        unread=2,
    )
    halos = neighbours(low, high)
    edges = (low, high)
    low, high, middle = call(outer_kernel, "outer", 6, [share] * 3, (low, high, *common), scratch(tiles))
    low, high, middle, middle_whole = call(
        functools.partial(inner_kernel, count),
        "inner",
        3,
        [share] * 3 + [plane_whole],
        (*middles, low, high, middle, *common),
        scratch(tiles),
    )
    low, high, low_near, high_near, faces, *sent = call(
        functools.partial(first_fix_kernel, count, chunk),
        "fix",
        3,
        [plane_whole] * 2
        + [shape(rows, near)] * 2
        + [shape(2, fields, tiles, 8, LANES, dtype=F32)]
        + pieces,
        (turn_alone, *halos, *edges, low, high, middle, tables, masks),
        scratch(tiles, 1) + [VMEM((2, tiles, rows, LANES), F32)],
        scalars=1,
    )
    sent = exchanged(sent)
    halos = neighbours(low_near, high_near)
    low, high, middle = call(
        functools.partial(own_kernel, near_tiles),
        "second",
        8,
        [share] * 3,
        (low, middle_whole, high, *common, faces),
        scratch(tiles) + [VMEM((tiles, rows, LANES), F32)] * 3,
    )
    second = call(
        functools.partial(last_fix_kernel, count, chunk),
        "last",
        3,
        pieces,
        (turn_alone, *halos, low, high, middle, tables, faces),
        scratch(near_tiles, 1) + [VMEM((2, near_tiles, rows, LANES), F32)],
        scalars=1,
    )
    second = exchanged(second)

    def join(parts):
        (result,) = call(
            functools.partial(join_kernel, count, chunk),
            "join",
            1,
            [shape(planes, own, cells)],
            (me_alone, *parts),
            [VMEM((count,) + parts[0].shape, F32)],
            scalars=1,
        )
        return jnp.transpose(result, (1, 0, 2))

    return join(sent), join(second)


def solution(mesh):
    in_specs = (P("chaos", "space", None), P("space", None), P(None, "space", None), P(), P(), P())
    out_specs = (P("chaos", "space", None), P("chaos", "space", None))
    return jax.shard_map(shards, mesh=mesh, in_specs=in_specs, out_specs=out_specs, check_vma=False)
```

```python
import functools

import jax
import jax.numpy as jnp
from jax import lax
from jax.experimental import pallas as pl
from jax.experimental.pallas import tpu as pltpu
from jax.sharding import PartitionSpec as P

NXY = 48
SCALE = 0.15
LANES = 128
JOINT = 2
EXTRA = 32
REACH = 2
BLOCK = 32
VMEM = pltpu.VMEM
F32, BF16 = jnp.float32, jnp.bfloat16
NEXT_X, LAST_X, NEXT_Y, LAST_Y, NEXT_Z, LAST_Z, ALL = range(7)


def up(value, step):
    return -(-value // step) * step


def call(kernel, name, micros, out_shape, args, scratch=(), scalars=0, unread=0):
    in_specs = [pl.BlockSpec(memory_space=pltpu.SMEM)] * scalars
    in_specs += [pl.BlockSpec(memory_space=VMEM)] * (len(args) - scalars - unread)
    in_specs += [pl.BlockSpec(memory_space=pl.ANY)] * unread
    return pl.pallas_call(
        kernel,
        out_shape=out_shape,
        in_specs=in_specs,
        out_specs=[pl.BlockSpec(memory_space=VMEM)] * len(out_shape),
        scratch_shapes=scratch,
        compiler_params=pltpu.CompilerParams(vmem_limit_bytes=40 << 20),
        cost_estimate=pl.CostEstimate(flops=int(micros * 1.1e9), bytes_accessed=int(micros * 3.6e6), transcendentals=0),
        name=name,
    )(*args)


def cut_kernel(count, chunk, me_ref, x_ref, *refs):
    out_refs, middle_refs, held = refs[:count], refs[count:-1], refs[-1]
    planes, own, cells = x_ref.shape
    _, padded, width = out_refs[0].shape
    halo = REACH * NXY
    me = me_ref[0]
    held[...] = jnp.zeros_like(held)
    lane = lax.broadcasted_iota(jnp.int32, (padded, LANES), 1)
    for plane in range(planes):
        held[0:own, :] = x_ref[plane].astype(F32)
        values = held[...]
        for target in range(count):
            turned = values if target == 0 else pltpu.roll(values, cells - target * chunk, 1)
            body = turned[:, : up(chunk + halo, LANES)]
            column = lax.broadcasted_iota(jnp.int32, body.shape, 1)
            end = chunk if target == count - 1 else chunk + halo
            body = jnp.where(column < end, body, 0.0)
            if body.shape[1] < width:
                body = jnp.concatenate([body, jnp.zeros((padded, width - body.shape[1]), F32)], axis=1)
            before = turned[:, cells - LANES :]
            if target == 0:
                before = jnp.zeros_like(before)
            last = jnp.where(lane < LANES - halo, body[:, width - LANES :], before)
            window = jnp.concatenate([body[:, : width - LANES], last], axis=1).astype(BF16)
            for step in range(count):

                @pl.when(lax.bitwise_xor(me, target) == step)
                def _():
                    if out_refs[step].shape[0] == planes:
                        out_refs[step][plane] = window
                    elif plane == 0 or plane == planes - 1:
                        out_refs[step][min(plane, 1)] = window
                    else:
                        middle_refs[step - JOINT][...] = window


def tables_kernel(fields, own, me_ref, triples_ref, products_ref, owners_ref, _, out_ref, held, by_column):
    rows, total = by_column.shape[1:]
    entries, factors = triples_ref.shape[1], products_ref.shape[1]
    named = owners_ref.shape[1]
    names = up(named, LANES)
    padded = up(own, 8)
    held[...] = jnp.zeros_like(held)
    held[0:3, :entries] = triples_ref[...].astype(F32)
    held[3:4, :factors] = products_ref[...]
    held[4:5, :named] = owners_ref[...].astype(F32)
    owners = held[4:5, :names].astype(jnp.int32)
    group = owners // own
    slots = lax.bitwise_xor(group, me_ref[0]) * padded + owners - group * own
    slots = jnp.broadcast_to(slots.astype(F32), (16, names)).astype(BF16)

    def placed(which):
        name = lax.broadcasted_iota(jnp.int32, (names, total), 0)
        chosen = jnp.where(name == held[which : which + 1, :].astype(jnp.int32), 1.0, 0.0).astype(BF16)
        return jnp.dot(slots, chosen, preferred_element_type=F32)[0:1].astype(jnp.int32)

    row, column = placed(0), placed(1)
    field = held[2:3, :].astype(jnp.int32)
    place = (row // BLOCK) * (fields * BLOCK) + field * BLOCK + row % BLOCK
    rest = held[3:4, :]
    here = lax.broadcasted_iota(jnp.int32, (rows, total), 0) == column
    for part in range(3):
        piece = rest.astype(BF16).astype(F32)
        rest = rest - piece
        by_column[part] = jnp.where(here, piece, 0.0).astype(BF16)
    size = fields * BLOCK

    @pl.loop(0, rows // BLOCK)
    def _(block):
        index = lax.broadcasted_iota(jnp.int32, (size, total), 0) + block * size
        chosen = jnp.where(index == place, 1.0, 0.0).astype(BF16)
        acc = jnp.zeros((size, rows), F32)
        for part in range(3):
            acc += lax.dot_general(
                chosen, by_column[part], (((1,), (1,)), ((), ())), preferred_element_type=F32
            )
        out_ref[pl.ds(pl.multiple_of(block * size, size), size), :] = acc.astype(BF16)


def spread_face(face, out_ref):
    for field in range(out_ref.shape[0]):
        for tile in range(out_ref.shape[1]):
            out_ref[field, tile] = jnp.broadcast_to(
                face[field : field + 1, tile * LANES : (tile + 1) * LANES], (8, LANES)
            )


def weights_kernel(conduct_ref, masks_ref, *refs):
    number = (len(refs) - 3) // 2
    passed, out_ref, passed_out = refs[:number], refs[number + 2], refs[number + 3 :]
    for in_ref, to_ref in zip(passed, passed_out):
        to_ref[...] = in_ref[...]
    planes, _, _, tiles = out_ref.shape[:4]
    width = tiles * LANES

    def mask(which):
        return jnp.concatenate([masks_ref[which, tile, 0:1, :] for tile in range(tiles)], axis=1)

    for plane in range(planes):
        own = conduct_ref[plane]
        others = (
            pltpu.roll(own, width - NXY, 1),
            pltpu.roll(own, NXY, 1),
            pltpu.roll(own, width - 1, 1) * mask(0),
            pltpu.roll(own, 1, 1) * mask(1),
            conduct_ref[min(plane + 1, planes - 1)],
            conduct_ref[max(plane - 1, 0)],
        )
        for way, other in enumerate(others):
            spread_face(0.5 * (own + other), out_ref.at[plane, way])


def joined(parts):
    return jnp.concatenate([part.astype(F32) for part in parts], axis=0).astype(BF16)


def gather_kernel(count, turn_ref, conduct_ref, *refs):
    parts, out_refs = refs[:count], refs[-2:]
    for side, out_ref in enumerate(out_refs):
        place = lax.bitwise_xor(turn_ref[0], side)
        rest = conduct_ref[side * (conduct_ref.shape[0] - 1)]
        pieces = []
        for _ in range(3):
            pieces.append(rest.astype(BF16))
            rest = rest - pieces[-1].astype(F32)
        pieces.append(jnp.zeros_like(pieces[0]))
        out_ref[...] = joined([part[place * (part.shape[0] - 1)] for part in parts] + pieces)


def spread(value):
    return jnp.broadcast_to(value[None], (BLOCK // 8, 8, LANES)).reshape(BLOCK, LANES)


def mix(tables_ref, values, mixed):
    result = jnp.dot(tables_ref[...], values, preferred_element_type=F32).astype(BF16)
    for tile in range(values.shape[1] // LANES):
        mixed[tile] = result[:, tile * LANES : (tile + 1) * LANES]


def weigh(values_of, face_of, ways, fields, sums, tiles):
    rows = sums.shape[2]
    for tile in tiles:
        for block in range(rows // BLOCK):
            totals = [None] * len(ways)
            for field in range(fields):
                start = (block * fields + field) * BLOCK
                values = values_of(tile, slice(start, start + BLOCK))
                for i, way in enumerate(ways):
                    term = spread(face_of(way, field, tile)) * values
                    totals[i] = term if field == 0 else totals[i] + term
            here = slice(block * BLOCK, (block + 1) * BLOCK)
            for i, way in enumerate(ways):
                sums[way, tile, here, :] = totals[i]
            if len(ways) > 1:
                sums[ALL, tile, here, :] = functools.reduce(jnp.add, totals)


def settle(sums, masks_ref, tiles, write):
    every, rows = sums.shape[1], sums.shape[2]
    lane = lax.broadcasted_iota(jnp.int32, (BLOCK, LANES), 1)
    for block in range(rows // BLOCK):
        here = slice(block * BLOCK, (block + 1) * BLOCK)

        def ahead(way, shift):
            turned = [pltpu.roll(sums[way, tile, here, :], LANES - shift, 1) for tile in range(tiles)]
            following = turned[1:] + turned[: 1 if tiles == every else 0]
            following += turned[-1:] * (tiles - len(following))
            return [jnp.where(lane < LANES - shift, turned[t], following[t]) for t in range(tiles)]

        def behind(way, shift, ring):
            turned = [pltpu.roll(sums[way, tile, here, :], shift, 1) for tile in range(tiles)]
            before = turned[0]
            if ring:
                before = turned[-1] if tiles == every else pltpu.roll(sums[way, every - 1, here, :], shift, 1)
            previous = [before] + turned[:-1]
            return [jnp.where(lane >= shift, turned[t], previous[t]) for t in range(tiles)]

        shares = zip(
            ahead(LAST_X, NXY), behind(NEXT_X, NXY, True), ahead(LAST_Y, 1), behind(NEXT_Y, 1, False)
        )
        for tile, (a, b, c, d) in enumerate(shares):
            value = sums[ALL, tile, here, :] - a - b
            value = value - spread(masks_ref[0, tile]) * c - spread(masks_ref[1, tile]) * d
            write(tile, here, value)


def measure_plane(values, plane, tables_ref, weights_ref, faces_ref, mixed, sums, tiles):
    planes, _, fields = weights_ref.shape[:3]
    outside = {0: LAST_Z, planes - 1: NEXT_Z}.get(plane)
    ways = [way for way in range(6) if way != outside or faces_ref is not None]

    def values_of(tile, rows):
        return mixed[tile, rows, :].astype(F32)

    def face_of(way, field, tile):
        if way == outside:
            return faces_ref[min(plane, 1), field, tile]
        return weights_ref[plane, way, field, tile]

    mix(tables_ref, values, mixed)
    weigh(values_of, face_of, ways, fields, sums, range(tiles))
    weigh(values_of, face_of, (NEXT_X,), fields, sums, range(tiles, sums.shape[1]))


def outer(low, high, tables_ref, weights_ref, masks_ref, faces_ref, low_out, high_out, middle_out, mixed, sums, tiles):
    last = weights_ref.shape[0] - 1
    for plane, values, out_ref, way in ((0, low, low_out, NEXT_Z), (last, high, high_out, LAST_Z)):
        measure_plane(values, plane, tables_ref, weights_ref, faces_ref, mixed.at[min(plane, 1)], sums, tiles)

        def write(tile, here, value):
            out_ref[tile, here, :] = value
            given = sums[way, tile, here, :]
            middle_out[tile, here, :] = -given if plane == 0 else middle_out[tile, here, :] - given

        settle(sums, masks_ref, tiles, write)


def inner(
    values, low_in, high_in, middle_in, tables_ref, weights_ref, masks_ref, low_out, high_out, out, mixed, sums, tiles
):
    measure_plane(values, 1, tables_ref, weights_ref, None, mixed.at[0], sums, tiles)

    def write(tile, here, value):
        out[tile, here, :] = SCALE * (value + middle_in[tile, here, :])
        low_out[tile, here, :] = low_in[tile, here, :] - sums[LAST_Z, tile, here, :]
        high_out[tile, here, :] = high_in[tile, here, :] - sums[NEXT_Z, tile, here, :]

    settle(sums, masks_ref, tiles, write)


def fill(result, masks_ref, out_ref):
    tiles, rows, _ = result.shape
    for tile in range(tiles):
        inside = jnp.broadcast_to(masks_ref[2, tile][None], (rows // 8, 8, LANES)).reshape(rows, LANES)
        out_ref[:, tile * LANES : (tile + 1) * LANES] = (result[tile] * inside).astype(BF16)


class Packing:
    def __init__(self, planes, chunk, own):
        self.planes, self.own, self.padded = planes, own, up(own, 8)
        self.full, self.odd = divmod(chunk, LANES)
        self.beside = LANES // self.odd if self.odd else 1
        last = planes % self.beside * self.odd if self.odd else 0
        images = planes * self.full + (-(-planes // self.beside) if self.odd else 0)
        self.fold = up(-(-self.padded // 2), 8) if 0 < last <= LANES // 2 else 0
        self.plain = images - 1 if self.fold else images
        self.main = own // 8 * 8
        self.rest = own - self.main
        self.folded = self.plain * self.main
        self.later = self.folded + self.fold
        self.rows = up(self.later + self.plain * self.rest + 8, 16)


def emit(results, packing, line, piece_refs):
    full, odd, beside, padded = packing.full, packing.odd, packing.beside, packing.padded
    lane = lax.broadcasted_iota(jnp.int32, (padded, LANES), 1)
    line[...] = jnp.zeros_like(line)
    for step, piece_ref in enumerate(piece_refs):
        here = slice(step * padded, (step + 1) * padded)
        images = [result[tile, here, :] for result in results for tile in range(full)]
        for first in range(0, len(results) if odd else 0, beside):
            packed = results[first][full, here, :]
            for spot in range(1, min(beside, len(results) - first)):
                turned = pltpu.roll(results[first + spot][full, here, :], spot * odd, 1)
                packed = jnp.where(lane < spot * odd, packed, turned)
            images.append(packed)
        if packing.fold:
            image = images.pop()
            later = pltpu.roll(image[padded - packing.fold :], LANES // 2, 1)
            block = jnp.where(lane[: packing.fold] < LANES // 2, image[: packing.fold], later)
            line[packing.folded : packing.later, :] = block
        for index, image in enumerate(images):
            line[index * packing.main : (index + 1) * packing.main, :] = image[: packing.main]
            if packing.rest:
                place = packing.later + index * packing.rest
                line[place : place + packing.rest, :] = image[packing.main : packing.own]
        piece_ref[...] = line[...].astype(BF16)


def images_of(held, packing):
    images = []
    for index in range(packing.plain):
        image = held[index * packing.main : (index + 1) * packing.main, :]
        if packing.rest:
            place = packing.later + index * packing.rest
            image = jnp.concatenate([image, held[place : place + 8, :]], axis=0)
        images.append(image)
    if packing.fold:
        block = held[packing.folded : packing.later, :]
        later = pltpu.roll(block, LANES // 2, 1)[2 * packing.fold - packing.padded :]
        images.append(jnp.concatenate([block, later], axis=0))
    return images


def outer_kernel(low_ref, high_ref, tables_ref, weights_ref, masks_ref, *outs):
    rows = tables_ref.shape[1]
    shared = (tables_ref, weights_ref, masks_ref, None)
    outer(low_ref[0:rows, :], high_ref[0:rows, :], *shared, *outs, weights_ref.shape[3])


def inner_kernel(count, *refs):
    parts = [part[1] if len(part.shape) == 3 else part[...] for part in refs[:count]]
    low_in, high_in, middle_in, tables_ref, weights_ref, masks_ref, *outs = refs[count:]
    low_out, high_out, middle_out, whole_ref, mixed, sums = outs
    shared = (tables_ref, weights_ref, masks_ref, low_out, high_out, middle_out, mixed, sums)
    inner(joined(parts), low_in, high_in, middle_in, *shared, weights_ref.shape[3])
    fill(middle_out, masks_ref, whole_ref)


def own_kernel(tiles, low_ref, values_ref, high_ref, tables_ref, weights_ref, masks_ref, faces_ref, *refs):
    low_out, high_out, middle_out, mixed, sums, low, high, middle = refs
    shared = (tables_ref, weights_ref, masks_ref)
    outer(low_ref[...], high_ref[...], *shared, faces_ref, low, high, middle, mixed, sums, tiles)
    inner(values_ref[...], low, high, middle, *shared, low_out, high_out, middle_out, mixed, sums, tiles)


def first_fix_kernel(packing, turn_ref, *refs):
    halo_refs, own_refs, share_refs, (middle_in, tables_ref, masks_ref), refs = (
        refs[0:2], refs[2:4], refs[4:6], refs[6:9], refs[9:]
    )
    wholes, nears, faces_ref, pieces, (mixed, sums, ends, line) = refs[:2], refs[2:4], refs[4], refs[5:-4], refs[-4:]
    rows, (_, fields, tiles, _, _) = tables_ref.shape[1], faces_ref.shape
    for side in range(2):
        coefficient = 0.0
        for ref in (own_refs[side], halo_refs[side]):
            parts = ref[rows : rows + EXTRA, :].astype(F32)
            coefficient = coefficient + ((parts[16:24] + parts[8:16]) + parts[0:8])
        spread_face(0.5 * coefficient, faces_ref.at[side])
        for index, ref in enumerate((own_refs[side], halo_refs[side])):
            mix(tables_ref, ref[0:rows, :], mixed.at[index])

        def values_of(tile, here):
            return mixed[0, tile, here, :].astype(F32) - mixed[1, tile, here, :].astype(F32)

        def face_of(way, field, tile):
            return faces_ref[side, field, tile]

        weigh(values_of, face_of, (0,), fields, sums, range(tiles))
        result = ends.at[lax.bitwise_xor(turn_ref[0], side)]
        for tile in range(tiles):
            result[tile] = SCALE * (share_refs[side][tile] + sums[0, tile])
        fill(result, masks_ref, wholes[side])
        nears[side][...] = wholes[side][:, : nears[side].shape[1]]
    emit((ends.at[0], middle_in, ends.at[1]), packing, line, pieces)


def last_fix_kernel(packing, turn_ref, *refs):
    halo_refs, share_refs, (middle_in, tables_ref, faces_ref), refs = refs[0:2], refs[2:4], refs[4:7], refs[7:]
    pieces, (mixed, sums, ends, line) = refs[:-4], refs[-4:]
    fields, tiles = faces_ref.shape[1], sums.shape[1]
    for side in range(2):
        mix(tables_ref, halo_refs[side][...], mixed.at[side])

        def values_of(tile, here):
            return mixed[side, tile, here, :].astype(F32)

        def face_of(way, field, tile):
            return faces_ref[side, field, tile]

        weigh(values_of, face_of, (0,), fields, sums, range(tiles))
        result = ends.at[lax.bitwise_xor(turn_ref[0], side)]
        for tile in range(tiles):
            result[tile] = SCALE * (share_refs[side][tile] - sums[0, tile])
    emit((ends.at[0], middle_in, ends.at[1]), packing, line, pieces)


def join_kernel(count, packing, me_ref, *refs):
    piece_refs, (out_ref, held) = refs[:count], refs[count:]
    full, odd, beside = packing.full, packing.odd, packing.beside
    me = me_ref[0]
    for step in range(count):
        held[lax.bitwise_xor(me, step)] = piece_refs[step][...].astype(F32)
    pieces = [images_of(held.at[source], packing) for source in range(count)]
    for plane in range(packing.planes):
        parts = []
        for images in pieces:
            parts += images[plane * full : (plane + 1) * full]
            if odd:
                spot = plane % beside
                parts.append(images[packing.planes * full + plane // beside][:, spot * odd : (spot + 1) * odd])
        out_ref[plane] = jnp.concatenate(parts, axis=1)[: packing.own].astype(BF16)


def shards(panels, mean_field, fluctuations, products, triples, owner_slot):
    count, slabs = lax.axis_size("chaos"), lax.axis_size("space")
    me = lax.axis_index("chaos")
    own, planes, cells = panels.shape
    assert planes == 3
    chunk, halo = cells // count, REACH * NXY
    width = up(chunk + 2 * halo, LANES)
    near = up(chunk, LANES)
    padded = up(own, 8)
    rows = count * padded
    fields = 1 + fluctuations.shape[0]
    turn = lax.bitwise_and(lax.axis_index("space"), 1)
    me_alone, turn_alone = me.astype(jnp.int32).reshape(1), turn.astype(jnp.int32).reshape(1)
    tiles = width // LANES

    def exchange(block, step):
        return lax.ppermute(block, "chaos", [(i, i ^ step) for i in range(count)])

    def exchanged(blocks):
        arrived = {step: exchange(blocks[step], step) for step in range(count - 1, 0, -1)}
        return [blocks[0]] + [arrived[step] for step in range(1, count)]

    def neighbours(first_plane, last_plane):
        pairs = [(i, i ^ 1) for i in range(slabs)]
        others = [(i, i - 1 if i % 2 == 0 else i + 1) for i in range(1, slabs - 1)]
        after = lax.ppermute(last_plane, "space", pairs)
        return lax.ppermute(first_plane, "space", others), after

    def shape(*dims, dtype=BF16):
        return jax.ShapeDtypeStruct(dims, dtype)

    joint = min(JOINT, count)
    cut = call(
        functools.partial(cut_kernel, count, chunk),
        "cut",
        1,
        [shape(planes if step < joint else 2, padded, width) for step in range(count)]
        + [shape(padded, width)] * (count - joint),
        (me_alone, jnp.transpose(panels, (1, 0, 2))),
        [VMEM((padded, cells), F32)],
        scalars=1,
    )
    parts = exchanged(cut[:count])

    (tables,) = call(
        functools.partial(tables_kernel, fields, own),
        "tables",
        5,
        [shape(fields * rows, rows)],
        (me_alone, triples.T, products[None], owner_slot[None], cut[0]),
        [VMEM((8, up(products.shape[0], 2 * LANES)), F32), VMEM((3, rows, up(products.shape[0], 2 * LANES)), BF16)],
        scalars=1,
        unread=1,
    )

    conduct = jnp.concatenate([mean_field[:, None], fluctuations.transpose(1, 0, 2)], axis=1)
    conduct = jnp.where(turn > 0, conduct[::-1], conduct)
    conduct = jnp.pad(conduct, ((0, 0), (0, up(fields, 8) - fields), (halo, halo)))
    conduct = lax.dynamic_slice_in_dim(conduct, me * chunk, chunk + 2 * halo, 2)
    gap = jnp.zeros(conduct.shape[:-1] + (width - chunk - 2 * halo,), F32)
    conduct = jnp.concatenate([conduct[..., halo:], gap, conduct[..., :halo]], axis=-1)

    lane = jnp.arange(width)
    cell = jnp.where(lane < width - halo, lane, lane - width) + halo
    row = cell // NXY - REACH + me * (chunk // NXY)
    inside = (row >= 0) & (row < NXY) & ((lane < chunk + halo) | (lane >= width - halo))
    masks = jnp.stack([cell % NXY < NXY - 1, cell % NXY > 0, inside]).astype(F32)
    masks = jnp.broadcast_to(masks.reshape(3, tiles, 1, LANES), (3, tiles, 8, LANES))
    weights, *middles = call(
        weights_kernel,
        "weights",
        0.5,
        [shape(planes, 6, fields, tiles, 8, LANES, dtype=F32)] + [shape(padded, width)] * (count - joint),
        (conduct, masks, *cut[count:], tables, parts[-1] if count <= joint else parts[joint]),
        unread=2,
    )
    middles = parts[:joint] + [exchange(middles[step - joint], step) for step in range(joint, count)]

    common = (tables, weights, masks)
    plane_whole = shape(rows, width)
    share = shape(tiles, rows, LANES, dtype=F32)
    packing = Packing(planes, chunk, own)
    pieces = [shape(packing.rows, LANES)] * count
    line = VMEM((packing.rows, LANES), F32)
    near_tiles = near // LANES

    def scratch(tiles, kinds=7):
        return [VMEM((2, tiles, fields * rows, LANES), BF16), VMEM((kinds, tiles, rows, LANES), F32)]

    low, high = call(
        functools.partial(gather_kernel, count),
        "gather",
        0.5,
        [shape(rows + EXTRA, width)] * 2,
        (turn_alone, conduct, *parts, tables, weights),
        scalars=1,
        unread=2,
    )
    halos = neighbours(low, high)
    edges = (low, high)
    low, high, middle = call(outer_kernel, "outer", 6, [share] * 3, (low, high, *common), scratch(tiles))
    low, high, middle, middle_whole = call(
        functools.partial(inner_kernel, count),
        "inner",
        3,
        [share] * 3 + [plane_whole],
        (*middles, low, high, middle, *common),
        scratch(tiles),
    )
    low, high, low_near, high_near, faces, *sent = call(
        functools.partial(first_fix_kernel, packing),
        "fix",
        3,
        [plane_whole] * 2
        + [shape(rows, near)] * 2
        + [shape(2, fields, tiles, 8, LANES, dtype=F32)]
        + pieces,
        (turn_alone, *halos, *edges, low, high, middle, tables, masks),
        scratch(tiles, 1) + [VMEM((2, tiles, rows, LANES), F32), line],
        scalars=1,
    )
    sent = exchanged(sent)
    halos = neighbours(low_near, high_near)
    low, high, middle = call(
        functools.partial(own_kernel, near_tiles),
        "second",
        8,
        [share] * 3,
        (low, middle_whole, high, *common, faces),
        scratch(tiles) + [VMEM((tiles, rows, LANES), F32)] * 3,
    )
    second = call(
        functools.partial(last_fix_kernel, packing),
        "last",
        3,
        pieces,
        (turn_alone, *halos, low, high, middle, tables, faces),
        scratch(near_tiles, 1) + [VMEM((2, near_tiles, rows, LANES), F32), line],
        scalars=1,
    )
    second = exchanged(second)

    def join(parts):
        (result,) = call(
            functools.partial(join_kernel, count, packing),
            "join",
            1,
            [shape(planes, own, cells)],
            (me_alone, *parts),
            [VMEM((count,) + parts[0].shape, F32)],
            scalars=1,
        )
        return jnp.transpose(result, (1, 0, 2))

    return join(sent), join(second)


def solution(mesh):
    in_specs = (P("chaos", "space", None), P("space", None), P(None, "space", None), P(), P(), P())
    out_specs = (P("chaos", "space", None), P("chaos", "space", None))
    return jax.shard_map(shards, mesh=mesh, in_specs=in_specs, out_specs=out_specs, check_vma=False)
```

```python
import functools

import jax
import jax.numpy as jnp
from jax import lax
from jax.experimental import pallas as pl
from jax.experimental.pallas import tpu as pltpu
from jax.sharding import PartitionSpec as P

NXY = 48
SCALE = 0.15
LANES = 128
JOINT = 2
EXTRA = 32
REACH = 2
BLOCK = 32
VMEM = pltpu.VMEM
F32, BF16 = jnp.float32, jnp.bfloat16
NEXT_X, LAST_X, NEXT_Y, LAST_Y, NEXT_Z, LAST_Z, ALL = range(7)


def up(value, step):
    return -(-value // step) * step


def call(kernel, name, micros, out_shape, args, scratch=(), scalars=0, unread=0):
    in_specs = [pl.BlockSpec(memory_space=pltpu.SMEM)] * scalars
    in_specs += [pl.BlockSpec(memory_space=VMEM)] * (len(args) - scalars - unread)
    in_specs += [pl.BlockSpec(memory_space=pl.ANY)] * unread
    return pl.pallas_call(
        kernel,
        out_shape=out_shape,
        in_specs=in_specs,
        out_specs=[pl.BlockSpec(memory_space=VMEM)] * len(out_shape),
        scratch_shapes=scratch,
        compiler_params=pltpu.CompilerParams(vmem_limit_bytes=40 << 20),
        cost_estimate=pl.CostEstimate(flops=int(micros * 1.1e9), bytes_accessed=int(micros * 3.6e6), transcendentals=0),
        name=name,
    )(*args)


def cut_kernel(count, chunk, me_ref, x_ref, *refs):
    out_refs, middle_refs, held = refs[:count], refs[count:-1], refs[-1]
    planes, own, cells = x_ref.shape
    _, padded, width = out_refs[0].shape
    halo = REACH * NXY
    me = me_ref[0]
    held[...] = jnp.zeros_like(held)
    lane = lax.broadcasted_iota(jnp.int32, (padded, LANES), 1)
    for plane in range(planes):
        held[0:own, :] = x_ref[plane].astype(F32)
        values = held[...]
        for target in range(count):
            turned = values if target == 0 else pltpu.roll(values, cells - target * chunk, 1)
            body = turned[:, : up(chunk + halo, LANES)]
            column = lax.broadcasted_iota(jnp.int32, body.shape, 1)
            end = chunk if target == count - 1 else chunk + halo
            body = jnp.where(column < end, body, 0.0)
            if body.shape[1] < width:
                body = jnp.concatenate([body, jnp.zeros((padded, width - body.shape[1]), F32)], axis=1)
            before = turned[:, cells - LANES :]
            if target == 0:
                before = jnp.zeros_like(before)
            last = jnp.where(lane < LANES - halo, body[:, width - LANES :], before)
            window = jnp.concatenate([body[:, : width - LANES], last], axis=1).astype(BF16)
            for step in range(count):

                @pl.when(lax.bitwise_xor(me, target) == step)
                def _():
                    if out_refs[step].shape[0] == planes:
                        out_refs[step][plane] = window
                    elif plane == 0 or plane == planes - 1:
                        out_refs[step][min(plane, 1)] = window
                    else:
                        middle_refs[step - JOINT][...] = window


def tables_kernel(fields, own, me_ref, triples_ref, products_ref, owners_ref, _, out_ref, held, by_column):
    rows, total = by_column.shape[1:]
    entries, factors = triples_ref.shape[1], products_ref.shape[1]
    named = owners_ref.shape[1]
    names = up(named, LANES)
    padded = up(own, 8)
    held[...] = jnp.zeros_like(held)
    held[0:3, :entries] = triples_ref[...].astype(F32)
    held[3:4, :factors] = products_ref[...]
    held[4:5, :named] = owners_ref[...].astype(F32)
    owners = held[4:5, :names].astype(jnp.int32)
    group = owners // own
    slots = lax.bitwise_xor(group, me_ref[0]) * padded + owners - group * own
    slots = jnp.broadcast_to(slots.astype(F32), (16, names)).astype(BF16)

    def placed(which):
        name = lax.broadcasted_iota(jnp.int32, (names, total), 0)
        chosen = jnp.where(name == held[which : which + 1, :].astype(jnp.int32), 1.0, 0.0).astype(BF16)
        return jnp.dot(slots, chosen, preferred_element_type=F32)[0:1].astype(jnp.int32)

    row, column = placed(0), placed(1)
    field = held[2:3, :].astype(jnp.int32)
    place = (row // BLOCK) * (fields * BLOCK) + field * BLOCK + row % BLOCK
    rest = held[3:4, :]
    here = lax.broadcasted_iota(jnp.int32, (rows, total), 0) == column
    for part in range(3):
        piece = rest.astype(BF16).astype(F32)
        rest = rest - piece
        by_column[part] = jnp.where(here, piece, 0.0).astype(BF16)
    size = fields * BLOCK

    @pl.loop(0, rows // BLOCK)
    def _(block):
        index = lax.broadcasted_iota(jnp.int32, (size, total), 0) + block * size
        chosen = jnp.where(index == place, 1.0, 0.0).astype(BF16)
        acc = jnp.zeros((size, rows), F32)
        for part in range(3):
            acc += lax.dot_general(
                chosen, by_column[part], (((1,), (1,)), ((), ())), preferred_element_type=F32
            )
        out_ref[pl.ds(pl.multiple_of(block * size, size), size), :] = acc.astype(BF16)


def spread_face(face, out_ref):
    for field in range(out_ref.shape[0]):
        for tile in range(out_ref.shape[1]):
            out_ref[field, tile] = jnp.broadcast_to(
                face[field : field + 1, tile * LANES : (tile + 1) * LANES], (8, LANES)
            )


def weights_kernel(conduct_ref, masks_ref, *refs):
    number = (len(refs) - 3) // 2
    passed, out_ref, passed_out = refs[:number], refs[number + 2], refs[number + 3 :]
    for in_ref, to_ref in zip(passed, passed_out):
        to_ref[...] = in_ref[...]
    planes, _, _, tiles = out_ref.shape[:4]
    width = tiles * LANES

    def mask(which):
        return jnp.concatenate([masks_ref[which, tile, 0:1, :] for tile in range(tiles)], axis=1)

    for plane in range(planes):
        own = conduct_ref[plane]
        others = (
            pltpu.roll(own, width - NXY, 1),
            pltpu.roll(own, NXY, 1),
            pltpu.roll(own, width - 1, 1) * mask(0),
            pltpu.roll(own, 1, 1) * mask(1),
            conduct_ref[min(plane + 1, planes - 1)],
            conduct_ref[max(plane - 1, 0)],
        )
        for way, other in enumerate(others):
            spread_face(0.5 * (own + other), out_ref.at[plane, way])


def joined(parts):
    return jnp.concatenate([part.astype(F32) for part in parts], axis=0).astype(BF16)


def gather_kernel(count, turn_ref, conduct_ref, *refs):
    parts, out_refs = refs[:count], refs[-2:]
    for side, out_ref in enumerate(out_refs):
        place = lax.bitwise_xor(turn_ref[0], side)
        rest = conduct_ref[side * (conduct_ref.shape[0] - 1)]
        pieces = []
        for _ in range(3):
            pieces.append(rest.astype(BF16))
            rest = rest - pieces[-1].astype(F32)
        pieces.append(jnp.zeros_like(pieces[0]))
        out_ref[...] = joined([part[place * (part.shape[0] - 1)] for part in parts] + pieces)


def spread(value):
    return jnp.broadcast_to(value[None], (BLOCK // 8, 8, LANES)).reshape(BLOCK, LANES)


def mix(tables_ref, values, mixed):
    result = jnp.dot(tables_ref[...], values, preferred_element_type=F32).astype(BF16)
    for tile in range(values.shape[1] // LANES):
        mixed[tile] = result[:, tile * LANES : (tile + 1) * LANES]


def weigh(values_of, face_of, ways, fields, sums, tiles):
    rows = sums.shape[2]
    for tile in tiles:
        for block in range(rows // BLOCK):
            totals = [None] * len(ways)
            for field in range(fields):
                start = (block * fields + field) * BLOCK
                values = values_of(tile, slice(start, start + BLOCK))
                for i, way in enumerate(ways):
                    term = spread(face_of(way, field, tile)) * values
                    totals[i] = term if field == 0 else totals[i] + term
            here = slice(block * BLOCK, (block + 1) * BLOCK)
            for i, way in enumerate(ways):
                sums[way, tile, here, :] = totals[i]
            if len(ways) > 1:
                sums[ALL, tile, here, :] = functools.reduce(jnp.add, totals)


def settle(sums, masks_ref, tiles, write):
    every, rows = sums.shape[1], sums.shape[2]
    lane = lax.broadcasted_iota(jnp.int32, (BLOCK, LANES), 1)
    for block in range(rows // BLOCK):
        here = slice(block * BLOCK, (block + 1) * BLOCK)

        def ahead(way, shift):
            turned = [pltpu.roll(sums[way, tile, here, :], LANES - shift, 1) for tile in range(tiles)]
            following = turned[1:] + turned[: 1 if tiles == every else 0]
            following += turned[-1:] * (tiles - len(following))
            return [jnp.where(lane < LANES - shift, turned[t], following[t]) for t in range(tiles)]

        def behind(way, shift, ring):
            turned = [pltpu.roll(sums[way, tile, here, :], shift, 1) for tile in range(tiles)]
            before = turned[0]
            if ring:
                before = turned[-1] if tiles == every else pltpu.roll(sums[way, every - 1, here, :], shift, 1)
            previous = [before] + turned[:-1]
            return [jnp.where(lane >= shift, turned[t], previous[t]) for t in range(tiles)]

        shares = zip(
            ahead(LAST_X, NXY), behind(NEXT_X, NXY, True), ahead(LAST_Y, 1), behind(NEXT_Y, 1, False)
        )
        for tile, (a, b, c, d) in enumerate(shares):
            value = sums[ALL, tile, here, :] - a - b
            value = value - spread(masks_ref[0, tile]) * c - spread(masks_ref[1, tile]) * d
            write(tile, here, value)


def measure_plane(values, plane, tables_ref, weights_ref, faces_ref, mixed, sums, tiles):
    planes, _, fields = weights_ref.shape[:3]
    outside = {0: LAST_Z, planes - 1: NEXT_Z}.get(plane)
    ways = [way for way in range(6) if way != outside or faces_ref is not None]

    def values_of(tile, rows):
        return mixed[tile, rows, :].astype(F32)

    def face_of(way, field, tile):
        if way == outside:
            return faces_ref[min(plane, 1), field, tile]
        return weights_ref[plane, way, field, tile]

    mix(tables_ref, values, mixed)
    weigh(values_of, face_of, ways, fields, sums, range(tiles))
    weigh(values_of, face_of, (NEXT_X,), fields, sums, range(tiles, sums.shape[1]))


def outer(low, high, tables_ref, weights_ref, masks_ref, faces_ref, low_out, high_out, middle_out, mixed, sums, tiles):
    last = weights_ref.shape[0] - 1
    for plane, values, out_ref, way in ((0, low, low_out, NEXT_Z), (last, high, high_out, LAST_Z)):
        measure_plane(values, plane, tables_ref, weights_ref, faces_ref, mixed.at[min(plane, 1)], sums, tiles)

        def write(tile, here, value):
            out_ref[tile, here, :] = value
            given = sums[way, tile, here, :]
            middle_out[tile, here, :] = -given if plane == 0 else middle_out[tile, here, :] - given

        settle(sums, masks_ref, tiles, write)


def inner(
    values, low_in, high_in, middle_in, tables_ref, weights_ref, masks_ref, low_out, high_out, out, mixed, sums, tiles
):
    measure_plane(values, 1, tables_ref, weights_ref, None, mixed.at[0], sums, tiles)

    def write(tile, here, value):
        out[tile, here, :] = SCALE * (value + middle_in[tile, here, :])
        low_out[tile, here, :] = low_in[tile, here, :] - sums[LAST_Z, tile, here, :]
        high_out[tile, here, :] = high_in[tile, here, :] - sums[NEXT_Z, tile, here, :]

    settle(sums, masks_ref, tiles, write)


def fill(result, masks_ref, out_ref):
    tiles, rows, _ = result.shape
    for tile in range(tiles):
        inside = jnp.broadcast_to(masks_ref[2, tile][None], (rows // 8, 8, LANES)).reshape(rows, LANES)
        out_ref[:, tile * LANES : (tile + 1) * LANES] = (result[tile] * inside).astype(BF16)


class Packing:
    def __init__(self, planes, chunk, own):
        self.planes, self.own, self.padded = planes, own, up(own, 8)
        self.full, self.odd = divmod(chunk, LANES)
        self.beside = LANES // self.odd if self.odd else 1
        last = planes % self.beside * self.odd if self.odd else 0
        images = planes * self.full + (-(-planes // self.beside) if self.odd else 0)
        self.fold = up(-(-self.padded // 2), 8) if 0 < last <= LANES // 2 else 0
        self.plain = images - 1 if self.fold else images
        self.main = own // 8 * 8
        self.rest = own - self.main
        self.folded = self.plain * self.main
        self.later = self.folded + self.fold
        self.rows = up(self.later + self.plain * self.rest + 8, 16)


def emit(results, packing, line, piece_refs):
    full, odd, beside, padded = packing.full, packing.odd, packing.beside, packing.padded
    lane = lax.broadcasted_iota(jnp.int32, (padded, LANES), 1)
    line[...] = jnp.zeros_like(line)
    for step, piece_ref in enumerate(piece_refs):
        here = slice(step * padded, (step + 1) * padded)
        images = [result[tile, here, :] for result in results for tile in range(full)]
        for first in range(0, len(results) if odd else 0, beside):
            packed = results[first][full, here, :]
            for spot in range(1, min(beside, len(results) - first)):
                turned = pltpu.roll(results[first + spot][full, here, :], spot * odd, 1)
                packed = jnp.where(lane < spot * odd, packed, turned)
            images.append(packed)
        if packing.fold:
            image = images.pop()
            later = pltpu.roll(image[padded - packing.fold :], LANES // 2, 1)
            block = jnp.where(lane[: packing.fold] < LANES // 2, image[: packing.fold], later)
            line[packing.folded : packing.later, :] = block
        for index, image in enumerate(images):
            line[index * packing.main : (index + 1) * packing.main, :] = image[: packing.main]
            if packing.rest:
                place = packing.later + index * packing.rest
                line[place : place + packing.rest, :] = image[packing.main : packing.own]
        piece_ref[...] = line[...].astype(BF16)


def images_of(held, packing):
    images = []
    for index in range(packing.plain):
        image = held[index * packing.main : (index + 1) * packing.main, :]
        if packing.rest:
            place = packing.later + index * packing.rest
            image = jnp.concatenate([image, held[place : place + 8, :]], axis=0)
        images.append(image)
    if packing.fold:
        block = held[packing.folded : packing.later, :]
        later = pltpu.roll(block, LANES // 2, 1)[2 * packing.fold - packing.padded :]
        images.append(jnp.concatenate([block, later], axis=0))
    return images


def outer_kernel(low_ref, high_ref, tables_ref, weights_ref, masks_ref, *outs):
    rows = tables_ref.shape[1]
    shared = (tables_ref, weights_ref, masks_ref, None)
    outer(low_ref[0:rows, :], high_ref[0:rows, :], *shared, *outs, weights_ref.shape[3])


def inner_kernel(count, *refs):
    parts = [part[1] if len(part.shape) == 3 else part[...] for part in refs[:count]]
    low_in, high_in, middle_in, tables_ref, weights_ref, masks_ref, *outs = refs[count:]
    low_out, high_out, middle_out, whole_ref, mixed, sums = outs
    shared = (tables_ref, weights_ref, masks_ref, low_out, high_out, middle_out, mixed, sums)
    inner(joined(parts), low_in, high_in, middle_in, *shared, weights_ref.shape[3])
    fill(middle_out, masks_ref, whole_ref)


def own_kernel(tiles, low_ref, values_ref, high_ref, tables_ref, weights_ref, masks_ref, faces_ref, *refs):
    low_out, high_out, middle_out, mixed, sums, low, high, middle = refs
    shared = (tables_ref, weights_ref, masks_ref)
    outer(low_ref[...], high_ref[...], *shared, faces_ref, low, high, middle, mixed, sums, tiles)
    inner(values_ref[...], low, high, middle, *shared, low_out, high_out, middle_out, mixed, sums, tiles)


def first_fix_kernel(packing, turn_ref, *refs):
    halo_refs, (conduct_ref, own_ref), share_refs, (middle_in, tables_ref, masks_ref), refs = (
        refs[0:2], refs[2:4], refs[4:6], refs[6:9], refs[9:]
    )
    wholes, nears, faces_ref, pieces, (mixed, sums, ends, line) = refs[:2], refs[2:4], refs[4], refs[5:-4], refs[-4:]
    rows, (_, fields, tiles, _, _) = tables_ref.shape[1], faces_ref.shape
    for side in range(2):
        parts = halo_refs[side][rows : rows + EXTRA, :].astype(F32)
        coefficient = (parts[16:24] + parts[8:16]) + parts[0:8]
        spread_face(0.5 * (conduct_ref[side * (conduct_ref.shape[0] - 1)] + coefficient), faces_ref.at[side])
        mix(tables_ref, halo_refs[side][0:rows, :], mixed.at[side])

        def values_of(tile, here):
            return own_ref[side, tile, here, :].astype(F32) - mixed[side, tile, here, :].astype(F32)

        def face_of(way, field, tile):
            return faces_ref[side, field, tile]

        weigh(values_of, face_of, (0,), fields, sums, range(tiles))
        result = ends.at[lax.bitwise_xor(turn_ref[0], side)]
        for tile in range(tiles):
            result[tile] = SCALE * (share_refs[side][tile] + sums[0, tile])
        fill(result, masks_ref, wholes[side])
        nears[side][...] = wholes[side][:, : nears[side].shape[1]]
    emit((ends.at[0], middle_in, ends.at[1]), packing, line, pieces)


def last_fix_kernel(packing, turn_ref, *refs):
    halo_refs, share_refs, (middle_in, tables_ref, faces_ref), refs = refs[0:2], refs[2:4], refs[4:7], refs[7:]
    pieces, (mixed, sums, ends, line) = refs[:-4], refs[-4:]
    fields, tiles = faces_ref.shape[1], sums.shape[1]
    for side in range(2):
        mix(tables_ref, halo_refs[side][...], mixed.at[side])

        def values_of(tile, here):
            return mixed[side, tile, here, :].astype(F32)

        def face_of(way, field, tile):
            return faces_ref[side, field, tile]

        weigh(values_of, face_of, (0,), fields, sums, range(tiles))
        result = ends.at[lax.bitwise_xor(turn_ref[0], side)]
        for tile in range(tiles):
            result[tile] = SCALE * (share_refs[side][tile] - sums[0, tile])
    emit((ends.at[0], middle_in, ends.at[1]), packing, line, pieces)


def join_kernel(count, packing, order, me_ref, *refs):
    out_ref, held = refs[count:]
    full, odd, beside = packing.full, packing.odd, packing.beside
    me = me_ref[0]
    for step, piece_ref in zip(order, refs):
        held[lax.bitwise_xor(me, step)] = piece_ref[...].astype(F32)
    pieces = [images_of(held.at[source], packing) for source in range(count)]
    for plane in range(packing.planes):
        parts = []
        for images in pieces:
            parts += images[plane * full : (plane + 1) * full]
            if odd:
                spot = plane % beside
                parts.append(images[packing.planes * full + plane // beside][:, spot * odd : (spot + 1) * odd])
        out_ref[plane] = jnp.concatenate(parts, axis=1)[: packing.own].astype(BF16)


def shards(panels, mean_field, fluctuations, products, triples, owner_slot):
    count, slabs = lax.axis_size("chaos"), lax.axis_size("space")
    me = lax.axis_index("chaos")
    own, planes, cells = panels.shape
    assert planes == 3
    chunk, halo = cells // count, REACH * NXY
    width = up(chunk + 2 * halo, LANES)
    near = up(chunk, LANES)
    padded = up(own, 8)
    rows = count * padded
    fields = 1 + fluctuations.shape[0]
    turn = lax.bitwise_and(lax.axis_index("space"), 1)
    me_alone, turn_alone = me.astype(jnp.int32).reshape(1), turn.astype(jnp.int32).reshape(1)
    tiles = width // LANES

    def exchange(block, step):
        return lax.ppermute(block, "chaos", [(i, i ^ step) for i in range(count)])

    def exchanged(blocks):
        arrived = {step: exchange(blocks[step], step) for step in range(count - 1, 0, -1)}
        return [blocks[0]] + [arrived[step] for step in range(1, count)]

    def neighbours(first_plane, last_plane):
        pairs = [(i, i ^ 1) for i in range(slabs)]
        others = [(i, i - 1 if i % 2 == 0 else i + 1) for i in range(1, slabs - 1)]
        after = lax.ppermute(last_plane, "space", pairs)
        return lax.ppermute(first_plane, "space", others), after

    def shape(*dims, dtype=BF16):
        return jax.ShapeDtypeStruct(dims, dtype)

    joint = min(JOINT, count)
    cut = call(
        functools.partial(cut_kernel, count, chunk),
        "cut",
        1,
        [shape(planes if step < joint else 2, padded, width) for step in range(count)]
        + [shape(padded, width)] * (count - joint),
        (me_alone, jnp.transpose(panels, (1, 0, 2))),
        [VMEM((padded, cells), F32)],
        scalars=1,
    )
    parts = exchanged(cut[:count])

    (tables,) = call(
        functools.partial(tables_kernel, fields, own),
        "tables",
        5,
        [shape(fields * rows, rows)],
        (me_alone, triples.T, products[None], owner_slot[None], cut[0]),
        [VMEM((8, up(products.shape[0], 2 * LANES)), F32), VMEM((3, rows, up(products.shape[0], 2 * LANES)), BF16)],
        scalars=1,
        unread=1,
    )

    conduct = jnp.concatenate([mean_field[:, None], fluctuations.transpose(1, 0, 2)], axis=1)
    conduct = jnp.where(turn > 0, conduct[::-1], conduct)
    conduct = jnp.pad(conduct, ((0, 0), (0, up(fields, 8) - fields), (halo, halo)))
    conduct = lax.dynamic_slice_in_dim(conduct, me * chunk, chunk + 2 * halo, 2)
    gap = jnp.zeros(conduct.shape[:-1] + (width - chunk - 2 * halo,), F32)
    conduct = jnp.concatenate([conduct[..., halo:], gap, conduct[..., :halo]], axis=-1)

    lane = jnp.arange(width)
    cell = jnp.where(lane < width - halo, lane, lane - width) + halo
    row = cell // NXY - REACH + me * (chunk // NXY)
    inside = (row >= 0) & (row < NXY) & ((lane < chunk + halo) | (lane >= width - halo))
    masks = jnp.stack([cell % NXY < NXY - 1, cell % NXY > 0, inside]).astype(F32)
    masks = jnp.broadcast_to(masks.reshape(3, tiles, 1, LANES), (3, tiles, 8, LANES))
    weights, *middles = call(
        weights_kernel,
        "weights",
        0.5,
        [shape(planes, 6, fields, tiles, 8, LANES, dtype=F32)] + [shape(padded, width)] * (count - joint),
        (conduct, masks, *cut[count:], tables, parts[-1] if count <= joint else parts[joint]),
        unread=2,
    )
    middles = parts[:joint] + [exchange(middles[step - joint], step) for step in range(joint, count)]

    common = (tables, weights, masks)
    plane_whole = shape(rows, width)
    share = shape(tiles, rows, LANES, dtype=F32)
    packing = Packing(planes, chunk, own)
    pieces = [shape(packing.rows, LANES)] * count
    line = VMEM((packing.rows, LANES), F32)
    near_tiles = near // LANES

    def scratch(tiles, kinds=7):
        return [VMEM((2, tiles, fields * rows, LANES), BF16), VMEM((kinds, tiles, rows, LANES), F32)]

    low, high = call(
        functools.partial(gather_kernel, count),
        "gather",
        0.5,
        [shape(rows + EXTRA, width)] * 2,
        (turn_alone, conduct, *parts, tables, weights),
        scalars=1,
        unread=2,
    )
    halos = neighbours(low, high)
    low, high, middle, mixed = call(
        outer_kernel,
        "outer",
        6,
        [share] * 3 + [shape(2, tiles, fields * rows, LANES)],
        (low, high, *common),
        scratch(tiles)[1:],
    )
    low, high, middle, middle_whole = call(
        functools.partial(inner_kernel, count),
        "inner",
        3,
        [share] * 3 + [plane_whole],
        (*middles, low, high, middle, *common),
        scratch(tiles),
    )
    low, high, low_near, high_near, faces, *sent = call(
        functools.partial(first_fix_kernel, packing),
        "fix",
        3,
        [plane_whole] * 2
        + [shape(rows, near)] * 2
        + [shape(2, fields, tiles, 8, LANES, dtype=F32)]
        + pieces,
        (turn_alone, *halos, conduct, mixed, low, high, middle, tables, masks),
        scratch(tiles, 1) + [VMEM((2, tiles, rows, LANES), F32), line],
        scalars=1,
    )
    sent = exchanged(sent)
    halos = neighbours(low_near, high_near)
    low, high, middle = call(
        functools.partial(own_kernel, near_tiles),
        "second",
        8,
        [share] * 3,
        (low, middle_whole, high, *common, faces),
        scratch(tiles) + [VMEM((tiles, rows, LANES), F32)] * 3,
    )
    second = call(
        functools.partial(last_fix_kernel, packing),
        "last",
        3,
        pieces,
        (turn_alone, *halos, low, high, middle, tables, faces),
        scratch(near_tiles, 1) + [VMEM((2, near_tiles, rows, LANES), F32), line],
        scalars=1,
    )
    second = exchanged(second)

    def join(parts, order):
        (result,) = call(
            functools.partial(join_kernel, count, packing, order),
            "join",
            1,
            [shape(planes, own, cells)],
            (me_alone, *(parts[step] for step in order)),
            [VMEM((count,) + parts[0].shape, F32)],
            scalars=1,
        )
        return jnp.transpose(result, (1, 0, 2))

    return join(sent, tuple(range(count))), join(second, tuple(range(count - 1, -1, -1)))


def solution(mesh):
    in_specs = (P("chaos", "space", None), P("space", None), P(None, "space", None), P(), P(), P())
    out_specs = (P("chaos", "space", None), P("chaos", "space", None))
    return jax.shard_map(shards, mesh=mesh, in_specs=in_specs, out_specs=out_specs, check_vma=False)
```

```python
import functools

import jax
import jax.numpy as jnp
from jax import lax
from jax.experimental import pallas as pl
from jax.experimental.pallas import tpu as pltpu
from jax.sharding import PartitionSpec as P

NXY = 48
SCALE = 0.15
LANES = 128
JOINT = 2
EXTRA = 32
REACH = 2
BLOCK = 32
VMEM = pltpu.VMEM
F32, BF16 = jnp.float32, jnp.bfloat16
NEXT_X, LAST_X, NEXT_Y, LAST_Y, NEXT_Z, LAST_Z, ALL = range(7)


def up(value, step):
    return -(-value // step) * step


def call(kernel, name, micros, out_shape, args, scratch=(), scalars=0, unread=0):
    in_specs = [pl.BlockSpec(memory_space=pltpu.SMEM)] * scalars
    in_specs += [pl.BlockSpec(memory_space=VMEM)] * (len(args) - scalars - unread)
    in_specs += [pl.BlockSpec(memory_space=pl.ANY)] * unread
    return pl.pallas_call(
        kernel,
        out_shape=out_shape,
        in_specs=in_specs,
        out_specs=[pl.BlockSpec(memory_space=VMEM)] * len(out_shape),
        scratch_shapes=scratch,
        compiler_params=pltpu.CompilerParams(vmem_limit_bytes=40 << 20),
        cost_estimate=pl.CostEstimate(flops=int(micros * 1.1e9), bytes_accessed=int(micros * 3.6e6), transcendentals=0),
        name=name,
    )(*args)


def cut_kernel(count, chunk, me_ref, x_ref, *refs):
    out_refs, middle_refs, held = refs[:count], refs[count:-1], refs[-1]
    planes, own, cells = x_ref.shape
    _, padded, width = out_refs[0].shape
    halo = REACH * NXY
    me = me_ref[0]
    held[...] = jnp.zeros_like(held)
    lane = lax.broadcasted_iota(jnp.int32, (padded, LANES), 1)
    for plane in range(planes):
        held[0:own, :] = x_ref[plane].astype(F32)
        values = held[...]
        for target in range(count):
            turned = values if target == 0 else pltpu.roll(values, cells - target * chunk, 1)
            body = turned[:, : up(chunk + halo, LANES)]
            column = lax.broadcasted_iota(jnp.int32, body.shape, 1)
            end = chunk if target == count - 1 else chunk + halo
            body = jnp.where(column < end, body, 0.0)
            if body.shape[1] < width:
                body = jnp.concatenate([body, jnp.zeros((padded, width - body.shape[1]), F32)], axis=1)
            before = turned[:, cells - LANES :]
            if target == 0:
                before = jnp.zeros_like(before)
            last = jnp.where(lane < LANES - halo, body[:, width - LANES :], before)
            window = jnp.concatenate([body[:, : width - LANES], last], axis=1).astype(BF16)
            for step in range(count):

                @pl.when(lax.bitwise_xor(me, target) == step)
                def _():
                    if out_refs[step].shape[0] == planes:
                        out_refs[step][plane] = window
                    elif plane == 0 or plane == planes - 1:
                        out_refs[step][min(plane, 1)] = window
                    else:
                        middle_refs[step - JOINT][...] = window


def tables_kernel(fields, own, me_ref, triples_ref, products_ref, owners_ref, _, out_ref, held, by_column):
    rows, total = by_column.shape[1:]
    entries, factors = triples_ref.shape[1], products_ref.shape[1]
    named = owners_ref.shape[1]
    names = up(named, LANES)
    padded = up(own, 8)
    held[...] = jnp.zeros_like(held)
    held[0:3, :entries] = triples_ref[...].astype(F32)
    held[3:4, :factors] = products_ref[...]
    held[4:5, :named] = owners_ref[...].astype(F32)
    owners = held[4:5, :names].astype(jnp.int32)
    group = owners // own
    slots = lax.bitwise_xor(group, me_ref[0]) * padded + owners - group * own
    slots = jnp.broadcast_to(slots.astype(F32), (16, names)).astype(BF16)

    def placed(which):
        name = lax.broadcasted_iota(jnp.int32, (names, total), 0)
        chosen = jnp.where(name == held[which : which + 1, :].astype(jnp.int32), 1.0, 0.0).astype(BF16)
        return jnp.dot(slots, chosen, preferred_element_type=F32)[0:1].astype(jnp.int32)

    row, column = placed(0), placed(1)
    field = held[2:3, :].astype(jnp.int32)
    place = (row // BLOCK) * (fields * BLOCK) + field * BLOCK + row % BLOCK
    rest = held[3:4, :]
    here = lax.broadcasted_iota(jnp.int32, (rows, total), 0) == column
    for part in range(3):
        piece = rest.astype(BF16).astype(F32)
        rest = rest - piece
        by_column[part] = jnp.where(here, piece, 0.0).astype(BF16)
    size = fields * BLOCK

    @pl.loop(0, rows // BLOCK)
    def _(block):
        index = lax.broadcasted_iota(jnp.int32, (size, total), 0) + block * size
        chosen = jnp.where(index == place, 1.0, 0.0).astype(BF16)
        acc = jnp.zeros((size, rows), F32)
        for part in range(3):
            acc += lax.dot_general(
                chosen, by_column[part], (((1,), (1,)), ((), ())), preferred_element_type=F32
            )
        out_ref[pl.ds(pl.multiple_of(block * size, size), size), :] = acc.astype(BF16)


def spread_face(face, out_ref):
    for field in range(out_ref.shape[0]):
        for tile in range(out_ref.shape[1]):
            out_ref[field, tile] = jnp.broadcast_to(
                face[field : field + 1, tile * LANES : (tile + 1) * LANES], (8, LANES)
            )


def weights_kernel(conduct_ref, masks_ref, *refs):
    number = (len(refs) - 3) // 2
    passed, out_ref, passed_out = refs[:number], refs[number + 2], refs[number + 3 :]
    for in_ref, to_ref in zip(passed, passed_out):
        to_ref[...] = in_ref[...]
    planes, _, _, tiles = out_ref.shape[:4]
    width = tiles * LANES

    def mask(which):
        return jnp.concatenate([masks_ref[which, tile, 0:1, :] for tile in range(tiles)], axis=1)

    for plane in range(planes):
        own = conduct_ref[plane]
        others = (
            pltpu.roll(own, width - NXY, 1),
            pltpu.roll(own, NXY, 1),
            pltpu.roll(own, width - 1, 1) * mask(0),
            pltpu.roll(own, 1, 1) * mask(1),
            conduct_ref[min(plane + 1, planes - 1)],
            conduct_ref[max(plane - 1, 0)],
        )
        for way, other in enumerate(others):
            spread_face(0.5 * (own + other), out_ref.at[plane, way])


def joined(parts):
    return jnp.concatenate([part.astype(F32) for part in parts], axis=0).astype(BF16)


def gather_kernel(count, turn_ref, conduct_ref, *refs):
    parts, out_refs = refs[:count], refs[-2:]
    for side, out_ref in enumerate(out_refs):
        place = lax.bitwise_xor(turn_ref[0], side)
        rest = conduct_ref[side * (conduct_ref.shape[0] - 1)]
        pieces = []
        for _ in range(3):
            pieces.append(rest.astype(BF16))
            rest = rest - pieces[-1].astype(F32)
        pieces.append(jnp.zeros_like(pieces[0]))
        out_ref[...] = joined([part[place * (part.shape[0] - 1)] for part in parts] + pieces)


def spread(value):
    return jnp.broadcast_to(value[None], (BLOCK // 8, 8, LANES)).reshape(BLOCK, LANES)


def mix(tables_ref, values, mixed):
    result = jnp.dot(tables_ref[...], values, preferred_element_type=F32).astype(BF16)
    for tile in range(values.shape[1] // LANES):
        mixed[tile] = result[:, tile * LANES : (tile + 1) * LANES]


def weigh(values_of, face_of, ways, fields, sums, tiles):
    rows = sums.shape[2]
    for tile in tiles:
        for block in range(rows // BLOCK):
            totals = [None] * len(ways)
            for field in range(fields):
                start = (block * fields + field) * BLOCK
                values = values_of(tile, slice(start, start + BLOCK))
                for i, way in enumerate(ways):
                    term = spread(face_of(way, field, tile)) * values
                    totals[i] = term if field == 0 else totals[i] + term
            here = slice(block * BLOCK, (block + 1) * BLOCK)
            for i, way in enumerate(ways):
                sums[way, tile, here, :] = totals[i]
            if len(ways) > 1:
                sums[ALL, tile, here, :] = functools.reduce(jnp.add, totals)
            yield


def settle(sums, masks_ref, tiles, write):
    every, rows = sums.shape[1], sums.shape[2]
    lane = lax.broadcasted_iota(jnp.int32, (BLOCK, LANES), 1)
    for block in range(rows // BLOCK):
        here = slice(block * BLOCK, (block + 1) * BLOCK)

        def ahead(way, shift):
            turned = [pltpu.roll(sums[way, tile, here, :], LANES - shift, 1) for tile in range(tiles)]
            following = turned[1:] + turned[: 1 if tiles == every else 0]
            following += turned[-1:] * (tiles - len(following))
            return [jnp.where(lane < LANES - shift, turned[t], following[t]) for t in range(tiles)]

        def behind(way, shift, ring):
            turned = [pltpu.roll(sums[way, tile, here, :], shift, 1) for tile in range(tiles)]
            before = turned[0]
            if ring:
                before = turned[-1] if tiles == every else pltpu.roll(sums[way, every - 1, here, :], shift, 1)
            previous = [before] + turned[:-1]
            return [jnp.where(lane >= shift, turned[t], previous[t]) for t in range(tiles)]

        shares = zip(
            ahead(LAST_X, NXY), behind(NEXT_X, NXY, True), ahead(LAST_Y, 1), behind(NEXT_Y, 1, False)
        )
        for tile, (a, b, c, d) in enumerate(shares):
            value = sums[ALL, tile, here, :] - a - b
            value = value - spread(masks_ref[0, tile]) * c - spread(masks_ref[1, tile]) * d
            write(tile, here, value)
        yield


def run(steps, beside=()):
    beside = iter(beside)
    for index, _ in enumerate(steps):
        if index % 5 == 4:
            next(beside, None)
    for _ in beside:
        pass


def measure_plane(values, plane, tables_ref, weights_ref, faces_ref, mixed, sums, tiles):
    planes, _, fields = weights_ref.shape[:3]
    outside = {0: LAST_Z, planes - 1: NEXT_Z}.get(plane)
    ways = [way for way in range(6) if way != outside or faces_ref is not None]

    def values_of(tile, rows):
        return mixed[tile, rows, :].astype(F32)

    def face_of(way, field, tile):
        if way == outside:
            return faces_ref[min(plane, 1), field, tile]
        return weights_ref[plane, way, field, tile]

    mix(tables_ref, values, mixed)
    yield from weigh(values_of, face_of, ways, fields, sums, range(tiles))
    yield from weigh(values_of, face_of, (NEXT_X,), fields, sums, range(tiles, sums.shape[1]))


def side_steps(values, side, tables_ref, weights_ref, masks_ref, faces_ref, out_ref, middle_out, mixed, sums, tiles):
    plane, way = (0, NEXT_Z) if side == 0 else (weights_ref.shape[0] - 1, LAST_Z)

    def write(tile, here, value):
        out_ref[tile, here, :] = value
        given = sums[way, tile, here, :]
        middle_out[tile, here, :] = -given if side == 0 else middle_out[tile, here, :] - given

    measured = measure_plane(values, plane, tables_ref, weights_ref, faces_ref, mixed, sums, tiles)
    return measured, settle(sums, masks_ref, tiles, write)


def middle_steps(
    values, low_in, high_in, middle_in, tables_ref, weights_ref, masks_ref, low_out, high_out, out, mixed, sums, tiles
):
    def write(tile, here, value):
        out[tile, here, :] = SCALE * (value + middle_in[tile, here, :])
        low_out[tile, here, :] = low_in[tile, here, :] - sums[LAST_Z, tile, here, :]
        high_out[tile, here, :] = high_in[tile, here, :] - sums[NEXT_Z, tile, here, :]

    measured = measure_plane(values, 1, tables_ref, weights_ref, None, mixed, sums, tiles)
    return measured, settle(sums, masks_ref, tiles, write)


def fill(result, masks_ref, out_ref):
    tiles, rows, _ = result.shape
    for tile in range(tiles):
        inside = jnp.broadcast_to(masks_ref[2, tile][None], (rows // 8, 8, LANES)).reshape(rows, LANES)
        out_ref[:, tile * LANES : (tile + 1) * LANES] = (result[tile] * inside).astype(BF16)


class Packing:
    def __init__(self, planes, chunk, own):
        self.planes, self.own, self.padded = planes, own, up(own, 8)
        self.full, self.odd = divmod(chunk, LANES)
        self.beside = LANES // self.odd if self.odd else 1
        last = planes % self.beside * self.odd if self.odd else 0
        images = planes * self.full + (-(-planes // self.beside) if self.odd else 0)
        self.fold = up(-(-self.padded // 2), 8) if 0 < last <= LANES // 2 else 0
        self.plain = images - 1 if self.fold else images
        self.main = own // 8 * 8
        self.rest = own - self.main
        self.folded = self.plain * self.main
        self.later = self.folded + self.fold
        self.rows = up(self.later + self.plain * self.rest + 8, 16)


def emit(results, packing, line, piece_refs):
    full, odd, beside, padded = packing.full, packing.odd, packing.beside, packing.padded
    lane = lax.broadcasted_iota(jnp.int32, (padded, LANES), 1)
    line[...] = jnp.zeros_like(line)
    for step, piece_ref in enumerate(piece_refs):
        here = slice(step * padded, (step + 1) * padded)
        images = [result[tile, here, :] for result in results for tile in range(full)]
        for first in range(0, len(results) if odd else 0, beside):
            packed = results[first][full, here, :]
            for spot in range(1, min(beside, len(results) - first)):
                turned = pltpu.roll(results[first + spot][full, here, :], spot * odd, 1)
                packed = jnp.where(lane < spot * odd, packed, turned)
            images.append(packed)
        if packing.fold:
            image = images.pop()
            later = pltpu.roll(image[padded - packing.fold :], LANES // 2, 1)
            block = jnp.where(lane[: packing.fold] < LANES // 2, image[: packing.fold], later)
            line[packing.folded : packing.later, :] = block
        for index, image in enumerate(images):
            line[index * packing.main : (index + 1) * packing.main, :] = image[: packing.main]
            if packing.rest:
                place = packing.later + index * packing.rest
                line[place : place + packing.rest, :] = image[packing.main : packing.own]
        piece_ref[...] = line[...].astype(BF16)


def images_of(held, packing):
    images = []
    for index in range(packing.plain):
        image = held[index * packing.main : (index + 1) * packing.main, :]
        if packing.rest:
            place = packing.later + index * packing.rest
            image = jnp.concatenate([image, held[place : place + 8, :]], axis=0)
        images.append(image)
    if packing.fold:
        block = held[packing.folded : packing.later, :]
        later = pltpu.roll(block, LANES // 2, 1)[2 * packing.fold - packing.padded :]
        images.append(jnp.concatenate([block, later], axis=0))
    return images


def outer_kernel(low_ref, high_ref, tables_ref, weights_ref, masks_ref, low_out, high_out, middle_out, mixed, sums):
    rows, tiles = tables_ref.shape[1], weights_ref.shape[3]
    shared = (tables_ref, weights_ref, masks_ref, None)
    low = side_steps(low_ref[0:rows, :], 0, *shared, low_out, middle_out, mixed.at[0], sums.at[0], tiles)
    high = side_steps(high_ref[0:rows, :], 1, *shared, high_out, middle_out, mixed.at[1], sums.at[1], tiles)
    run(low[0])
    run(high[0], low[1])
    run(high[1])


def inner_kernel(count, *refs):
    parts = [part[1] if len(part.shape) == 3 else part[...] for part in refs[:count]]
    low_in, high_in, middle_in, tables_ref, weights_ref, masks_ref, *outs = refs[count:]
    low_out, high_out, middle_out, whole_ref, mixed, sums = outs
    shared = (tables_ref, weights_ref, masks_ref, low_out, high_out, middle_out, mixed.at[0], sums)
    middle = middle_steps(joined(parts), low_in, high_in, middle_in, *shared, weights_ref.shape[3])
    run(middle[0])
    run(middle[1])
    fill(middle_out, masks_ref, whole_ref)


def own_kernel(tiles, low_ref, values_ref, high_ref, tables_ref, weights_ref, masks_ref, faces_ref, *refs):
    low_out, high_out, middle_out, mixed, sums, low_share, high_share, given = refs
    shared = (tables_ref, weights_ref, masks_ref)
    low = side_steps(low_ref[...], 0, *shared, faces_ref, low_share, given, mixed.at[0], sums.at[0], tiles)
    high = side_steps(high_ref[...], 1, *shared, faces_ref, high_share, given, mixed.at[1], sums.at[1], tiles)
    ins, outs = (low_share, high_share, given), (low_out, high_out, middle_out)
    middle = middle_steps(values_ref[...], *ins, *shared, *outs, mixed.at[0], sums.at[0], tiles)
    run(low[0])
    run(high[0], low[1])
    run(middle[0], high[1])
    run(middle[1])


def first_fix_kernel(packing, turn_ref, *refs):
    halo_refs, (conduct_ref, own_ref), share_refs, (middle_in, tables_ref, masks_ref), refs = (
        refs[0:2], refs[2:4], refs[4:6], refs[6:9], refs[9:]
    )
    wholes, nears, faces_ref, pieces, (mixed, sums, ends, line) = refs[:2], refs[2:4], refs[4], refs[5:-4], refs[-4:]
    rows, (_, fields, tiles, _, _) = tables_ref.shape[1], faces_ref.shape
    for side in range(2):
        parts = halo_refs[side][rows : rows + EXTRA, :].astype(F32)
        coefficient = (parts[16:24] + parts[8:16]) + parts[0:8]
        spread_face(0.5 * (conduct_ref[side * (conduct_ref.shape[0] - 1)] + coefficient), faces_ref.at[side])
        mix(tables_ref, halo_refs[side][0:rows, :], mixed.at[side])

        def values_of(tile, here):
            return own_ref[side, tile, here, :].astype(F32) - mixed[side, tile, here, :].astype(F32)

        def face_of(way, field, tile):
            return faces_ref[side, field, tile]

        run(weigh(values_of, face_of, (0,), fields, sums, range(tiles)))
        result = ends.at[lax.bitwise_xor(turn_ref[0], side)]
        for tile in range(tiles):
            result[tile] = SCALE * (share_refs[side][tile] + sums[0, tile])
        fill(result, masks_ref, wholes[side])
        nears[side][...] = wholes[side][:, : nears[side].shape[1]]
    emit((ends.at[0], middle_in, ends.at[1]), packing, line, pieces)


def last_fix_kernel(packing, turn_ref, *refs):
    halo_refs, share_refs, (middle_in, tables_ref, faces_ref), refs = refs[0:2], refs[2:4], refs[4:7], refs[7:]
    pieces, (mixed, sums, ends, line) = refs[:-4], refs[-4:]
    fields, tiles = faces_ref.shape[1], sums.shape[1]
    for side in range(2):
        mix(tables_ref, halo_refs[side][...], mixed.at[side])

        def values_of(tile, here):
            return mixed[side, tile, here, :].astype(F32)

        def face_of(way, field, tile):
            return faces_ref[side, field, tile]

        run(weigh(values_of, face_of, (0,), fields, sums, range(tiles)))
        result = ends.at[lax.bitwise_xor(turn_ref[0], side)]
        for tile in range(tiles):
            result[tile] = SCALE * (share_refs[side][tile] - sums[0, tile])
    emit((ends.at[0], middle_in, ends.at[1]), packing, line, pieces)


def join_kernel(count, packing, order, me_ref, *refs):
    out_ref, held = refs[count:]
    full, odd, beside = packing.full, packing.odd, packing.beside
    me = me_ref[0]
    for step, piece_ref in zip(order, refs):
        held[lax.bitwise_xor(me, step)] = piece_ref[...].astype(F32)
    pieces = [images_of(held.at[source], packing) for source in range(count)]
    for plane in range(packing.planes):
        parts = []
        for images in pieces:
            parts += images[plane * full : (plane + 1) * full]
            if odd:
                spot = plane % beside
                parts.append(images[packing.planes * full + plane // beside][:, spot * odd : (spot + 1) * odd])
        out_ref[plane] = jnp.concatenate(parts, axis=1)[: packing.own].astype(BF16)


def shards(panels, mean_field, fluctuations, products, triples, owner_slot):
    count, slabs = lax.axis_size("chaos"), lax.axis_size("space")
    me = lax.axis_index("chaos")
    own, planes, cells = panels.shape
    assert planes == 3
    chunk, halo = cells // count, REACH * NXY
    width = up(chunk + 2 * halo, LANES)
    near = up(chunk, LANES)
    padded = up(own, 8)
    rows = count * padded
    fields = 1 + fluctuations.shape[0]
    turn = lax.bitwise_and(lax.axis_index("space"), 1)
    me_alone, turn_alone = me.astype(jnp.int32).reshape(1), turn.astype(jnp.int32).reshape(1)
    tiles = width // LANES

    def exchange(block, step):
        return lax.ppermute(block, "chaos", [(i, i ^ step) for i in range(count)])

    def exchanged(blocks):
        arrived = {step: exchange(blocks[step], step) for step in range(count - 1, 0, -1)}
        return [blocks[0]] + [arrived[step] for step in range(1, count)]

    def neighbours(first_plane, last_plane):
        pairs = [(i, i ^ 1) for i in range(slabs)]
        others = [(i, i - 1 if i % 2 == 0 else i + 1) for i in range(1, slabs - 1)]
        after = lax.ppermute(last_plane, "space", pairs)
        return lax.ppermute(first_plane, "space", others), after

    def shape(*dims, dtype=BF16):
        return jax.ShapeDtypeStruct(dims, dtype)

    joint = min(JOINT, count)
    cut = call(
        functools.partial(cut_kernel, count, chunk),
        "cut",
        1,
        [shape(planes if step < joint else 2, padded, width) for step in range(count)]
        + [shape(padded, width)] * (count - joint),
        (me_alone, jnp.transpose(panels, (1, 0, 2))),
        [VMEM((padded, cells), F32)],
        scalars=1,
    )
    parts = exchanged(cut[:count])

    (tables,) = call(
        functools.partial(tables_kernel, fields, own),
        "tables",
        5,
        [shape(fields * rows, rows)],
        (me_alone, triples.T, products[None], owner_slot[None], cut[0]),
        [VMEM((8, up(products.shape[0], 2 * LANES)), F32), VMEM((3, rows, up(products.shape[0], 2 * LANES)), BF16)],
        scalars=1,
        unread=1,
    )

    conduct = jnp.concatenate([mean_field[:, None], fluctuations.transpose(1, 0, 2)], axis=1)
    conduct = jnp.where(turn > 0, conduct[::-1], conduct)
    conduct = jnp.pad(conduct, ((0, 0), (0, up(fields, 8) - fields), (halo, halo)))
    conduct = lax.dynamic_slice_in_dim(conduct, me * chunk, chunk + 2 * halo, 2)
    gap = jnp.zeros(conduct.shape[:-1] + (width - chunk - 2 * halo,), F32)
    conduct = jnp.concatenate([conduct[..., halo:], gap, conduct[..., :halo]], axis=-1)

    lane = jnp.arange(width)
    cell = jnp.where(lane < width - halo, lane, lane - width) + halo
    row = cell // NXY - REACH + me * (chunk // NXY)
    inside = (row >= 0) & (row < NXY) & ((lane < chunk + halo) | (lane >= width - halo))
    masks = jnp.stack([cell % NXY < NXY - 1, cell % NXY > 0, inside]).astype(F32)
    masks = jnp.broadcast_to(masks.reshape(3, tiles, 1, LANES), (3, tiles, 8, LANES))
    weights, *middles = call(
        weights_kernel,
        "weights",
        0.5,
        [shape(planes, 6, fields, tiles, 8, LANES, dtype=F32)] + [shape(padded, width)] * (count - joint),
        (conduct, masks, *cut[count:], tables, parts[-1] if count <= joint else parts[joint]),
        unread=2,
    )
    middles = parts[:joint] + [exchange(middles[step - joint], step) for step in range(joint, count)]

    common = (tables, weights, masks)
    plane_whole = shape(rows, width)
    share = shape(tiles, rows, LANES, dtype=F32)
    packing = Packing(planes, chunk, own)
    pieces = [shape(packing.rows, LANES)] * count
    line = VMEM((packing.rows, LANES), F32)
    near_tiles = near // LANES

    def scratch(tiles, kinds=7):
        return [VMEM((2, tiles, fields * rows, LANES), BF16), VMEM((kinds, tiles, rows, LANES), F32)]

    low, high = call(
        functools.partial(gather_kernel, count),
        "gather",
        0.5,
        [shape(rows + EXTRA, width)] * 2,
        (turn_alone, conduct, *parts, tables, weights),
        scalars=1,
        unread=2,
    )
    halos = neighbours(low, high)
    low, high, middle, mixed = call(
        outer_kernel,
        "outer",
        6,
        [share] * 3 + [shape(2, tiles, fields * rows, LANES)],
        (low, high, *common),
        [VMEM((2, 7, tiles, rows, LANES), F32)],
    )
    low, high, middle, middle_whole = call(
        functools.partial(inner_kernel, count),
        "inner",
        3,
        [share] * 3 + [plane_whole],
        (*middles, low, high, middle, *common),
        scratch(tiles),
    )
    low, high, low_near, high_near, faces, *sent = call(
        functools.partial(first_fix_kernel, packing),
        "fix",
        3,
        [plane_whole] * 2
        + [shape(rows, near)] * 2
        + [shape(2, fields, tiles, 8, LANES, dtype=F32)]
        + pieces,
        (turn_alone, *halos, conduct, mixed, low, high, middle, tables, masks),
        scratch(tiles, 1) + [VMEM((2, tiles, rows, LANES), F32), line],
        scalars=1,
    )
    sent = exchanged(sent)
    halos = neighbours(low_near, high_near)
    low, high, middle = call(
        functools.partial(own_kernel, near_tiles),
        "second",
        8,
        [share] * 3,
        (low, middle_whole, high, *common, faces),
        scratch(tiles)[:1] + [VMEM((2, 7, tiles, rows, LANES), F32)] + [VMEM((tiles, rows, LANES), F32)] * 3,
    )
    second = call(
        functools.partial(last_fix_kernel, packing),
        "last",
        3,
        pieces,
        (turn_alone, *halos, low, high, middle, tables, faces),
        scratch(near_tiles, 1) + [VMEM((2, near_tiles, rows, LANES), F32), line],
        scalars=1,
    )
    second = exchanged(second)

    def join(parts, order):
        (result,) = call(
            functools.partial(join_kernel, count, packing, order),
            "join",
            1,
            [shape(planes, own, cells)],
            (me_alone, *(parts[step] for step in order)),
            [VMEM((count,) + parts[0].shape, F32)],
            scalars=1,
        )
        return jnp.transpose(result, (1, 0, 2))

    return join(sent, tuple(range(count))), join(second, tuple(range(count - 1, -1, -1)))


def solution(mesh):
    in_specs = (P("chaos", "space", None), P("space", None), P(None, "space", None), P(), P(), P())
    out_specs = (P("chaos", "space", None), P("chaos", "space", None))
    return jax.shard_map(shards, mesh=mesh, in_specs=in_specs, out_specs=out_specs, check_vma=False)
```

```python
import functools

import jax
import jax.numpy as jnp
from jax import lax
from jax.experimental import pallas as pl
from jax.experimental.pallas import tpu as pltpu
from jax.sharding import PartitionSpec as P

NXY = 48
SCALE = 0.15
LANES = 128
JOINT = 2
EXTRA = 32
REACH = 2
BLOCK = 32
VMEM = pltpu.VMEM
F32, BF16 = jnp.float32, jnp.bfloat16
NEXT_X, LAST_X, NEXT_Y, LAST_Y, NEXT_Z, LAST_Z, ALL = range(7)


def up(value, step):
    return -(-value // step) * step


def call(kernel, name, micros, out_shape, args, scratch=(), scalars=0, unread=0, space=pl.ANY, out_space=VMEM):
    in_specs = [pl.BlockSpec(memory_space=pltpu.SMEM)] * scalars
    in_specs += [pl.BlockSpec(memory_space=VMEM)] * (len(args) - scalars - unread)
    in_specs += [pl.BlockSpec(memory_space=space)] * unread
    return pl.pallas_call(
        kernel,
        out_shape=out_shape,
        in_specs=in_specs,
        out_specs=[pl.BlockSpec(memory_space=out_space)] * len(out_shape),
        scratch_shapes=scratch,
        compiler_params=pltpu.CompilerParams(vmem_limit_bytes=40 << 20),
        cost_estimate=pl.CostEstimate(flops=int(micros * 1.1e9), bytes_accessed=int(micros * 3.6e6), transcendentals=0),
        name=name,
    )(*args)


def cut_kernel(count, chunk, me_ref, x_ref, *refs):
    out_refs, middle_refs, (held, fetched, arrived) = refs[:count], refs[count:-3], refs[-3:]
    planes, own, cells = x_ref.shape
    copies = [pltpu.make_async_copy(x_ref.at[i], fetched.at[i], arrived.at[i]) for i in range(planes)]
    for copy in copies:
        copy.start()
    _, padded, width = out_refs[0].shape
    halo = REACH * NXY
    me = me_ref[0]
    held[...] = jnp.zeros_like(held)
    lane = lax.broadcasted_iota(jnp.int32, (padded, LANES), 1)
    for plane in range(planes):
        copies[plane].wait()
        held[0:own, :] = fetched[plane].astype(F32)
        values = held[...]
        for target in range(count):
            turned = values if target == 0 else pltpu.roll(values, cells - target * chunk, 1)
            body = turned[:, : up(chunk + halo, LANES)]
            column = lax.broadcasted_iota(jnp.int32, body.shape, 1)
            end = chunk if target == count - 1 else chunk + halo
            body = jnp.where(column < end, body, 0.0)
            if body.shape[1] < width:
                body = jnp.concatenate([body, jnp.zeros((padded, width - body.shape[1]), F32)], axis=1)
            before = turned[:, cells - LANES :]
            if target == 0:
                before = jnp.zeros_like(before)
            last = jnp.where(lane < LANES - halo, body[:, width - LANES :], before)
            window = jnp.concatenate([body[:, : width - LANES], last], axis=1).astype(BF16)
            for step in range(count):

                @pl.when(lax.bitwise_xor(me, target) == step)
                def _():
                    if out_refs[step].shape[0] == planes:
                        out_refs[step][plane] = window
                    elif plane == 0 or plane == planes - 1:
                        out_refs[step][min(plane, 1)] = window
                    else:
                        middle_refs[step - JOINT][...] = window


def tables_kernel(fields, own, me_ref, triples_ref, products_ref, owners_ref, _, out_ref, held, by_column):
    rows, total = by_column.shape[1:]
    entries, factors = triples_ref.shape[1], products_ref.shape[1]
    named = owners_ref.shape[1]
    names = up(named, LANES)
    padded = up(own, 8)
    held[...] = jnp.zeros_like(held)
    held[0:3, :entries] = triples_ref[...].astype(F32)
    held[3:4, :factors] = products_ref[...]
    held[4:5, :named] = owners_ref[...].astype(F32)
    owners = held[4:5, :names].astype(jnp.int32)
    group = owners // own
    slots = lax.bitwise_xor(group, me_ref[0]) * padded + owners - group * own
    slots = jnp.broadcast_to(slots.astype(F32), (16, names)).astype(BF16)

    def placed(which):
        name = lax.broadcasted_iota(jnp.int32, (names, total), 0)
        chosen = jnp.where(name == held[which : which + 1, :].astype(jnp.int32), 1.0, 0.0).astype(BF16)
        return jnp.dot(slots, chosen, preferred_element_type=F32)[0:1].astype(jnp.int32)

    row, column = placed(0), placed(1)
    field = held[2:3, :].astype(jnp.int32)
    place = (row // BLOCK) * (fields * BLOCK) + field * BLOCK + row % BLOCK
    rest = held[3:4, :]
    here = lax.broadcasted_iota(jnp.int32, (rows, total), 0) == column
    for part in range(3):
        piece = rest.astype(BF16).astype(F32)
        rest = rest - piece
        by_column[part] = jnp.where(here, piece, 0.0).astype(BF16)
    size = fields * BLOCK

    @pl.loop(0, rows // BLOCK)
    def _(block):
        index = lax.broadcasted_iota(jnp.int32, (size, total), 0) + block * size
        chosen = jnp.where(index == place, 1.0, 0.0).astype(BF16)
        acc = jnp.zeros((size, rows), F32)
        for part in range(3):
            acc += lax.dot_general(
                chosen, by_column[part], (((1,), (1,)), ((), ())), preferred_element_type=F32
            )
        out_ref[pl.ds(pl.multiple_of(block * size, size), size), :] = acc.astype(BF16)


def spread_face(face, out_ref):
    for field in range(out_ref.shape[0]):
        for tile in range(out_ref.shape[1]):
            out_ref[field, tile] = jnp.broadcast_to(
                face[field : field + 1, tile * LANES : (tile + 1) * LANES], (8, LANES)
            )


def weights_kernel(conduct_ref, masks_ref, *refs):
    number = (len(refs) - 3) // 2
    passed, out_ref, passed_out = refs[:number], refs[number + 2], refs[number + 3 :]
    for in_ref, to_ref in zip(passed, passed_out):
        to_ref[...] = in_ref[...]
    planes, _, _, tiles = out_ref.shape[:4]
    width = tiles * LANES

    def mask(which):
        return jnp.concatenate([masks_ref[which, tile, 0:1, :] for tile in range(tiles)], axis=1)

    for plane in range(planes):
        own = conduct_ref[plane]
        others = (
            pltpu.roll(own, width - NXY, 1),
            pltpu.roll(own, NXY, 1),
            pltpu.roll(own, width - 1, 1) * mask(0),
            pltpu.roll(own, 1, 1) * mask(1),
            conduct_ref[min(plane + 1, planes - 1)],
            conduct_ref[max(plane - 1, 0)],
        )
        for way, other in enumerate(others):
            spread_face(0.5 * (own + other), out_ref.at[plane, way])


def joined(parts):
    return jnp.concatenate([part.astype(F32) for part in parts], axis=0).astype(BF16)


def gather_kernel(count, turn_ref, conduct_ref, *refs):
    parts, out_refs = refs[:count], refs[-2:]
    for side, out_ref in enumerate(out_refs):
        place = lax.bitwise_xor(turn_ref[0], side)
        rest = conduct_ref[side * (conduct_ref.shape[0] - 1)]
        pieces = []
        for _ in range(3):
            pieces.append(rest.astype(BF16))
            rest = rest - pieces[-1].astype(F32)
        pieces.append(jnp.zeros_like(pieces[0]))
        out_ref[...] = joined([part[place * (part.shape[0] - 1)] for part in parts] + pieces)


def spread(value):
    return jnp.broadcast_to(value[None], (BLOCK // 8, 8, LANES)).reshape(BLOCK, LANES)


def mix(tables_ref, values, mixed):
    result = jnp.dot(tables_ref[...], values, preferred_element_type=F32).astype(BF16)
    for tile in range(values.shape[1] // LANES):
        mixed[tile] = result[:, tile * LANES : (tile + 1) * LANES]


def weigh(values_of, face_of, ways, fields, sums, tiles):
    rows = sums.shape[2]
    for tile in tiles:
        for block in range(rows // BLOCK):
            totals = [None] * len(ways)
            for field in range(fields):
                start = (block * fields + field) * BLOCK
                values = values_of(tile, slice(start, start + BLOCK))
                for i, way in enumerate(ways):
                    term = spread(face_of(way, field, tile)) * values
                    totals[i] = term if field == 0 else totals[i] + term
            here = slice(block * BLOCK, (block + 1) * BLOCK)
            for i, way in enumerate(ways):
                sums[way, tile, here, :] = totals[i]
            if len(ways) > 1:
                sums[ALL, tile, here, :] = functools.reduce(jnp.add, totals)
            yield


def settle(sums, masks_ref, tiles, write):
    every, rows = sums.shape[1], sums.shape[2]
    lane = lax.broadcasted_iota(jnp.int32, (BLOCK, LANES), 1)
    for block in range(rows // BLOCK):
        here = slice(block * BLOCK, (block + 1) * BLOCK)

        def ahead(way, shift):
            turned = [pltpu.roll(sums[way, tile, here, :], LANES - shift, 1) for tile in range(tiles)]
            following = turned[1:] + turned[: 1 if tiles == every else 0]
            following += turned[-1:] * (tiles - len(following))
            return [jnp.where(lane < LANES - shift, turned[t], following[t]) for t in range(tiles)]

        def behind(way, shift, ring):
            turned = [pltpu.roll(sums[way, tile, here, :], shift, 1) for tile in range(tiles)]
            before = turned[0]
            if ring:
                before = turned[-1] if tiles == every else pltpu.roll(sums[way, every - 1, here, :], shift, 1)
            previous = [before] + turned[:-1]
            return [jnp.where(lane >= shift, turned[t], previous[t]) for t in range(tiles)]

        shares = zip(
            ahead(LAST_X, NXY), behind(NEXT_X, NXY, True), ahead(LAST_Y, 1), behind(NEXT_Y, 1, False)
        )
        for tile, (a, b, c, d) in enumerate(shares):
            value = sums[ALL, tile, here, :] - a - b
            value = value - spread(masks_ref[0, tile]) * c - spread(masks_ref[1, tile]) * d
            write(tile, here, value)
        yield


def run(steps, beside=()):
    beside = iter(beside)
    for index, _ in enumerate(steps):
        if index % 5 == 4:
            next(beside, None)
    for _ in beside:
        pass


def measure_plane(values, plane, tables_ref, weights_ref, faces_ref, mixed, sums, tiles):
    planes, _, fields = weights_ref.shape[:3]
    outside = {0: LAST_Z, planes - 1: NEXT_Z}.get(plane)
    ways = [way for way in range(6) if way != outside or faces_ref is not None]

    def values_of(tile, rows):
        return mixed[tile, rows, :].astype(F32)

    def face_of(way, field, tile):
        if way == outside:
            return faces_ref[min(plane, 1), field, tile]
        return weights_ref[plane, way, field, tile]

    mix(tables_ref, values, mixed)
    yield from weigh(values_of, face_of, ways, fields, sums, range(tiles))
    yield from weigh(values_of, face_of, (NEXT_X,), fields, sums, range(tiles, sums.shape[1]))


def side_steps(values, side, tables_ref, weights_ref, masks_ref, faces_ref, out_ref, middle_out, mixed, sums, tiles):
    plane, way = (0, NEXT_Z) if side == 0 else (weights_ref.shape[0] - 1, LAST_Z)

    def write(tile, here, value):
        out_ref[tile, here, :] = value
        given = sums[way, tile, here, :]
        middle_out[tile, here, :] = -given if side == 0 else middle_out[tile, here, :] - given

    measured = measure_plane(values, plane, tables_ref, weights_ref, faces_ref, mixed, sums, tiles)
    return measured, settle(sums, masks_ref, tiles, write)


def middle_steps(
    values, low_in, high_in, middle_in, tables_ref, weights_ref, masks_ref, low_out, high_out, out, mixed, sums, tiles
):
    def write(tile, here, value):
        out[tile, here, :] = SCALE * (value + middle_in[tile, here, :])
        low_out[tile, here, :] = low_in[tile, here, :] - sums[LAST_Z, tile, here, :]
        high_out[tile, here, :] = high_in[tile, here, :] - sums[NEXT_Z, tile, here, :]

    measured = measure_plane(values, 1, tables_ref, weights_ref, None, mixed, sums, tiles)
    return measured, settle(sums, masks_ref, tiles, write)


def fill(result, masks_ref, out_ref):
    tiles, rows, _ = result.shape
    for tile in range(tiles):
        inside = jnp.broadcast_to(masks_ref[2, tile][None], (rows // 8, 8, LANES)).reshape(rows, LANES)
        out_ref[:, tile * LANES : (tile + 1) * LANES] = (result[tile] * inside).astype(BF16)


class Packing:
    def __init__(self, planes, chunk, own):
        self.planes, self.own, self.padded = planes, own, up(own, 8)
        self.full, self.odd = divmod(chunk, LANES)
        self.beside = LANES // self.odd if self.odd else 1
        last = planes % self.beside * self.odd if self.odd else 0
        images = planes * self.full + (-(-planes // self.beside) if self.odd else 0)
        self.fold = up(-(-self.padded // 2), 8) if 0 < last <= LANES // 2 else 0
        self.plain = images - 1 if self.fold else images
        self.main = own // 8 * 8
        self.rest = own - self.main
        self.folded = self.plain * self.main
        self.later = self.folded + self.fold
        self.rows = up(self.later + self.plain * self.rest + 8, 16)


def emit(results, packing, line, piece_refs):
    full, odd, beside, padded = packing.full, packing.odd, packing.beside, packing.padded
    lane = lax.broadcasted_iota(jnp.int32, (padded, LANES), 1)
    line[...] = jnp.zeros_like(line)
    for step, piece_ref in enumerate(piece_refs):
        here = slice(step * padded, (step + 1) * padded)
        images = [result[tile, here, :] for result in results for tile in range(full)]
        for first in range(0, len(results) if odd else 0, beside):
            packed = results[first][full, here, :]
            for spot in range(1, min(beside, len(results) - first)):
                turned = pltpu.roll(results[first + spot][full, here, :], spot * odd, 1)
                packed = jnp.where(lane < spot * odd, packed, turned)
            images.append(packed)
        if packing.fold:
            image = images.pop()
            later = pltpu.roll(image[padded - packing.fold :], LANES // 2, 1)
            block = jnp.where(lane[: packing.fold] < LANES // 2, image[: packing.fold], later)
            line[packing.folded : packing.later, :] = block
        for index, image in enumerate(images):
            line[index * packing.main : (index + 1) * packing.main, :] = image[: packing.main]
            if packing.rest:
                place = packing.later + index * packing.rest
                line[place : place + packing.rest, :] = image[packing.main : packing.own]
        piece_ref[...] = line[...].astype(BF16)


def images_of(held, packing):
    images = []
    for index in range(packing.plain):
        image = held[index * packing.main : (index + 1) * packing.main, :]
        if packing.rest:
            place = packing.later + index * packing.rest
            image = jnp.concatenate([image, held[place : place + 8, :]], axis=0)
        images.append(image)
    if packing.fold:
        block = held[packing.folded : packing.later, :]
        later = pltpu.roll(block, LANES // 2, 1)[2 * packing.fold - packing.padded :]
        images.append(jnp.concatenate([block, later], axis=0))
    return images


def outer_kernel(low_ref, high_ref, tables_ref, weights_ref, masks_ref, low_out, high_out, middle_out, mixed, sums):
    rows, tiles = tables_ref.shape[1], weights_ref.shape[3]
    shared = (tables_ref, weights_ref, masks_ref, None)
    low = side_steps(low_ref[0:rows, :], 0, *shared, low_out, middle_out, mixed.at[0], sums.at[0], tiles)
    high = side_steps(high_ref[0:rows, :], 1, *shared, high_out, middle_out, mixed.at[1], sums.at[1], tiles)
    run(low[0])
    run(high[0], low[1])
    run(high[1])


def inner_kernel(count, *refs):
    parts = [part[1] if len(part.shape) == 3 else part[...] for part in refs[:count]]
    low_in, high_in, middle_in, tables_ref, weights_ref, masks_ref, *outs = refs[count:]
    low_out, high_out, middle_out, whole_ref, mixed, sums = outs
    shared = (tables_ref, weights_ref, masks_ref, low_out, high_out, middle_out, mixed.at[0], sums)
    middle = middle_steps(joined(parts), low_in, high_in, middle_in, *shared, weights_ref.shape[3])
    run(middle[0])
    run(middle[1])
    fill(middle_out, masks_ref, whole_ref)


def own_kernel(tiles, low_ref, values_ref, high_ref, tables_ref, weights_ref, masks_ref, faces_ref, *refs):
    low_out, high_out, middle_out, mixed, sums, low_share, high_share, given = refs
    shared = (tables_ref, weights_ref, masks_ref)
    low = side_steps(low_ref[...], 0, *shared, faces_ref, low_share, given, mixed.at[0], sums.at[0], tiles)
    high = side_steps(high_ref[...], 1, *shared, faces_ref, high_share, given, mixed.at[1], sums.at[1], tiles)
    ins, outs = (low_share, high_share, given), (low_out, high_out, middle_out)
    middle = middle_steps(values_ref[...], *ins, *shared, *outs, mixed.at[0], sums.at[0], tiles)
    run(low[0])
    run(high[0], low[1])
    run(middle[0], high[1])
    run(middle[1])


def first_fix_kernel(packing, turn_ref, *refs):
    halo_refs, (conduct_ref, own_ref), share_refs, (middle_in, tables_ref, masks_ref), refs = (
        refs[0:2], refs[2:4], refs[4:6], refs[6:9], refs[9:]
    )
    wholes, nears, faces_ref, pieces, (mixed, sums, ends, line) = refs[:2], refs[2:4], refs[4], refs[5:-4], refs[-4:]
    rows, (_, fields, tiles, _, _) = tables_ref.shape[1], faces_ref.shape
    for side in range(2):
        parts = halo_refs[side][rows : rows + EXTRA, :].astype(F32)
        coefficient = (parts[16:24] + parts[8:16]) + parts[0:8]
        spread_face(0.5 * (conduct_ref[side * (conduct_ref.shape[0] - 1)] + coefficient), faces_ref.at[side])
        mix(tables_ref, halo_refs[side][0:rows, :], mixed.at[side])

        def values_of(tile, here):
            return own_ref[side, tile, here, :].astype(F32) - mixed[side, tile, here, :].astype(F32)

        def face_of(way, field, tile):
            return faces_ref[side, field, tile]

        run(weigh(values_of, face_of, (0,), fields, sums, range(tiles)))
        result = ends.at[lax.bitwise_xor(turn_ref[0], side)]
        for tile in range(tiles):
            result[tile] = SCALE * (share_refs[side][tile] + sums[0, tile])
        fill(result, masks_ref, wholes[side])
        nears[side][...] = wholes[side][:, : nears[side].shape[1]]
    emit((ends.at[0], middle_in, ends.at[1]), packing, line, pieces)


def last_fix_kernel(packing, turn_ref, *refs):
    halo_refs, share_refs, (middle_in, tables_ref, faces_ref), refs = refs[0:2], refs[2:4], refs[4:7], refs[7:]
    pieces, (mixed, sums, ends, line) = refs[:-4], refs[-4:]
    fields, tiles = faces_ref.shape[1], sums.shape[1]
    for side in range(2):
        mix(tables_ref, halo_refs[side][...], mixed.at[side])

        def values_of(tile, here):
            return mixed[side, tile, here, :].astype(F32)

        def face_of(way, field, tile):
            return faces_ref[side, field, tile]

        run(weigh(values_of, face_of, (0,), fields, sums, range(tiles)))
        result = ends.at[lax.bitwise_xor(turn_ref[0], side)]
        for tile in range(tiles):
            result[tile] = SCALE * (share_refs[side][tile] - sums[0, tile])
    emit((ends.at[0], middle_in, ends.at[1]), packing, line, pieces)


def join_kernel(count, packing, order, me_ref, *refs):
    out_ref, held, ready, sent = refs[count:]
    full, odd, beside = packing.full, packing.odd, packing.beside
    me = me_ref[0]
    for step, piece_ref in zip(order, refs):
        held[lax.bitwise_xor(me, step)] = piece_ref[...].astype(F32)
    pieces = [images_of(held.at[source], packing) for source in range(count)]
    for plane in range(packing.planes):
        parts = []
        for images in pieces:
            parts += images[plane * full : (plane + 1) * full]
            if odd:
                spot = plane % beside
                parts.append(images[packing.planes * full + plane // beside][:, spot * odd : (spot + 1) * odd])
        ready[plane] = jnp.concatenate(parts, axis=1)[: packing.own].astype(BF16)
        pltpu.make_async_copy(ready.at[plane], out_ref.at[plane], sent.at[plane]).start()
    for plane in range(packing.planes):
        pltpu.make_async_copy(ready.at[plane], out_ref.at[plane], sent.at[plane]).wait()


def shards(panels, mean_field, fluctuations, products, triples, owner_slot):
    count, slabs = lax.axis_size("chaos"), lax.axis_size("space")
    me = lax.axis_index("chaos")
    own, planes, cells = panels.shape
    assert planes == 3
    chunk, halo = cells // count, REACH * NXY
    width = up(chunk + 2 * halo, LANES)
    near = up(chunk, LANES)
    padded = up(own, 8)
    rows = count * padded
    fields = 1 + fluctuations.shape[0]
    turn = lax.bitwise_and(lax.axis_index("space"), 1)
    me_alone, turn_alone = me.astype(jnp.int32).reshape(1), turn.astype(jnp.int32).reshape(1)
    tiles = width // LANES

    def exchange(block, step):
        return lax.ppermute(block, "chaos", [(i, i ^ step) for i in range(count)])

    def exchanged(blocks):
        arrived = {step: exchange(blocks[step], step) for step in range(count - 1, 0, -1)}
        return [blocks[0]] + [arrived[step] for step in range(1, count)]

    def neighbours(first_plane, last_plane):
        pairs = [(i, i ^ 1) for i in range(slabs)]
        others = [(i, i - 1 if i % 2 == 0 else i + 1) for i in range(1, slabs - 1)]
        after = lax.ppermute(last_plane, "space", pairs)
        return lax.ppermute(first_plane, "space", others), after

    def shape(*dims, dtype=BF16):
        return jax.ShapeDtypeStruct(dims, dtype)

    joint = min(JOINT, count)
    cut = call(
        functools.partial(cut_kernel, count, chunk),
        "cut",
        1,
        [shape(planes if step < joint else 2, padded, width) for step in range(count)]
        + [shape(padded, width)] * (count - joint),
        (me_alone, pltpu.with_memory_space_constraint(jnp.transpose(panels, (1, 0, 2)), pltpu.HBM)),
        [VMEM((padded, cells), F32), VMEM((planes, own, cells), BF16), pltpu.SemaphoreType.DMA((planes,))],
        scalars=1,
        unread=1,
        space=pltpu.HBM,
    )
    parts = exchanged(cut[:count])

    (tables,) = call(
        functools.partial(tables_kernel, fields, own),
        "tables",
        5,
        [shape(fields * rows, rows)],
        (me_alone, triples.T, products[None], owner_slot[None], cut[0]),
        [VMEM((8, up(products.shape[0], 2 * LANES)), F32), VMEM((3, rows, up(products.shape[0], 2 * LANES)), BF16)],
        scalars=1,
        unread=1,
    )

    conduct = jnp.concatenate([mean_field[:, None], fluctuations.transpose(1, 0, 2)], axis=1)
    conduct = jnp.where(turn > 0, conduct[::-1], conduct)
    conduct = jnp.pad(conduct, ((0, 0), (0, up(fields, 8) - fields), (halo, halo)))
    conduct = lax.dynamic_slice_in_dim(conduct, me * chunk, chunk + 2 * halo, 2)
    gap = jnp.zeros(conduct.shape[:-1] + (width - chunk - 2 * halo,), F32)
    conduct = jnp.concatenate([conduct[..., halo:], gap, conduct[..., :halo]], axis=-1)

    lane = jnp.arange(width)
    cell = jnp.where(lane < width - halo, lane, lane - width) + halo
    row = cell // NXY - REACH + me * (chunk // NXY)
    inside = (row >= 0) & (row < NXY) & ((lane < chunk + halo) | (lane >= width - halo))
    masks = jnp.stack([cell % NXY < NXY - 1, cell % NXY > 0, inside]).astype(F32)
    masks = jnp.broadcast_to(masks.reshape(3, tiles, 1, LANES), (3, tiles, 8, LANES))
    weights, *middles = call(
        weights_kernel,
        "weights",
        0.5,
        [shape(planes, 6, fields, tiles, 8, LANES, dtype=F32)] + [shape(padded, width)] * (count - joint),
        (conduct, masks, *cut[count:], tables, parts[-1] if count <= joint else parts[joint]),
        unread=2,
    )
    middles = parts[:joint] + [exchange(middles[step - joint], step) for step in range(joint, count)]

    common = (tables, weights, masks)
    plane_whole = shape(rows, width)
    share = shape(tiles, rows, LANES, dtype=F32)
    packing = Packing(planes, chunk, own)
    pieces = [shape(packing.rows, LANES)] * count
    line = VMEM((packing.rows, LANES), F32)
    near_tiles = near // LANES

    def scratch(tiles, kinds=7):
        return [VMEM((2, tiles, fields * rows, LANES), BF16), VMEM((kinds, tiles, rows, LANES), F32)]

    low, high = call(
        functools.partial(gather_kernel, count),
        "gather",
        0.5,
        [shape(rows + EXTRA, width)] * 2,
        (turn_alone, conduct, *parts, tables, weights),
        scalars=1,
        unread=2,
    )
    halos = neighbours(low, high)
    low, high, middle, mixed = call(
        outer_kernel,
        "outer",
        6,
        [share] * 3 + [shape(2, tiles, fields * rows, LANES)],
        (low, high, *common),
        [VMEM((2, 7, tiles, rows, LANES), F32)],
    )
    low, high, middle, middle_whole = call(
        functools.partial(inner_kernel, count),
        "inner",
        3,
        [share] * 3 + [plane_whole],
        (*middles, low, high, middle, *common),
        scratch(tiles),
    )
    low, high, low_near, high_near, faces, *sent = call(
        functools.partial(first_fix_kernel, packing),
        "fix",
        3,
        [plane_whole] * 2
        + [shape(rows, near)] * 2
        + [shape(2, fields, tiles, 8, LANES, dtype=F32)]
        + pieces,
        (turn_alone, *halos, conduct, mixed, low, high, middle, tables, masks),
        scratch(tiles, 1) + [VMEM((2, tiles, rows, LANES), F32), line],
        scalars=1,
    )
    sent = exchanged(sent)
    halos = neighbours(low_near, high_near)
    low, high, middle = call(
        functools.partial(own_kernel, near_tiles),
        "second",
        8,
        [share] * 3,
        (low, middle_whole, high, *common, faces),
        scratch(tiles)[:1] + [VMEM((2, 7, tiles, rows, LANES), F32)] + [VMEM((tiles, rows, LANES), F32)] * 3,
    )
    second = call(
        functools.partial(last_fix_kernel, packing),
        "last",
        3,
        pieces,
        (turn_alone, *halos, low, high, middle, tables, faces),
        scratch(near_tiles, 1) + [VMEM((2, near_tiles, rows, LANES), F32), line],
        scalars=1,
    )
    second = exchanged(second)

    def join(parts, order):
        (result,) = call(
            functools.partial(join_kernel, count, packing, order),
            "join",
            1,
            [shape(planes, own, cells)],
            (me_alone, *(parts[step] for step in order)),
            [
                VMEM((count,) + parts[0].shape, F32),
                VMEM((planes, own, cells), BF16),
                pltpu.SemaphoreType.DMA((planes,)),
            ],
            scalars=1,
            out_space=pl.ANY,
        )
        return jnp.transpose(result, (1, 0, 2))

    return join(sent, tuple(range(count))), join(second, tuple(range(count - 1, -1, -1)))


def solution(mesh):
    in_specs = (P("chaos", "space", None), P("space", None), P(None, "space", None), P(), P(), P())
    out_specs = (P("chaos", "space", None), P("chaos", "space", None))
    return jax.shard_map(shards, mesh=mesh, in_specs=in_specs, out_specs=out_specs, check_vma=False)
```
